32 devices in a mesh: leaf: 8 (over y, x, core), row: 4 (over z).
Axes of the slice: x: 2, y: 2, z: 4, core: 2. Of those that a mesh axis runs over, the one named last changes fastest.
Arguments:
- leaf_cost: float32 [8, 2048, 2048], P('leaf', 'row'), as said below
- a_blocks: float32 [8, 16, 8, 128, 128], P('leaf'), may hold values from -0.046875 to 0.046875
- a_cols: int32 [8, 16, 8], P('leaf'), may hold values from 0 to 15, as said below
- b_blocks: float32 [8, 16, 2, 128, 128], P('leaf'), may hold values from -0.1875 to 0.1875
- b_cols: int32 [8, 16, 2], P('leaf'), may hold values from 0 to 3, as said below
- branch_prob: float32 [8], P('leaf'), may hold values from 0.3 to 0.7
- state_cost: float32 [2048], P('row'), may hold values from 0.5 to 2
- control_cost: float32 [512], replicated, may hold values from 0.5 to 2
- parent_state: float32 [4, 2048, 128], P(None, 'row'), may hold values from -6 to 6
Outputs:
- parent_cost: float32 [8, 2048, 2048], P('leaf', 'row')
- gains: float32 [8, 512, 2048], P('leaf', None, 'row')
- child_state: float32 [8, 2048, 128], P('leaf', 'row')
The draws below stay inside these ranges and needn't reach their ends.
Inputs may be any that keep to these rules, and one draw needn't show every extreme that they name: a_cols[c, k, 0] equals k, and the 8 entries of one block row are distinct. `b_cols`: the 2 entries of one block row are distinct. Each leaf_cost[c] is symmetric with a diagonal of 2 to 4.
All inputs are finite; a program needn't handle non-finite values.
Results may differ from the reference program's by a relative error of at most 0.0003.
Values sent between devices are 32-bit elements; how exact they have to be, the bound alone decides.
No kernel may reach another device: no remote copies, remote signals or barrier semaphores. Data moves between devices by JAX's collectives and lax.ppermute only.
A program may use at most 256 MiB of HBM per device.

```python
import math
import jax
import jax.numpy as jnp
from jax import lax

NX = 2048
NU = 512
BLK = 128
NNZA = 8
NNZB = 2
SAMPLES = 128
LEAVES = 8
PARENTS = 4


def draw_leaf_cost(key, part):
    key = jax.random.fold_in(key, 11)
    key_diag, key_noise = jax.random.split(key)
    diag = jnp.exp(jax.random.uniform(key_diag, (LEAVES, NX), jnp.float32, jnp.log(2.0), jnp.log(4.0)))
    noise = jax.random.normal(key_noise, (LEAVES, NX, NX), jnp.float32)
    sym = (noise + jnp.swapaxes(noise, 1, 2)) * (0.015 / 1.4142135)
    ident = jnp.eye(NX, dtype=jnp.float32)
    return sym * (1.0 - ident)[None] + diag[:, :, None] * ident[None]


def draw_a_cols(key, part):
    key = jax.random.fold_in(key, 12)
    nbx = NX // BLK
    keys = jax.random.split(key, LEAVES * nbx)

    def one_row(k):
        perm = jax.random.permutation(k, nbx - 1) + 1
        return jnp.concatenate([jnp.zeros((1,), jnp.int32), perm[:NNZA - 1].astype(jnp.int32)])
    offsets = jax.vmap(one_row)(keys).reshape(LEAVES, nbx, NNZA)
    rows = jnp.arange(nbx, dtype=jnp.int32)[None, :, None]
    return ((rows + offsets) % nbx).astype(jnp.int32)


def draw_b_cols(key, part):
    key = jax.random.fold_in(key, 13)
    nbx = NX // BLK
    keys = jax.random.split(key, LEAVES * nbx)

    def one_row(k):
        perm = jax.random.permutation(k, NU // BLK)
        return perm[:NNZB].astype(jnp.int32)
    return jax.vmap(one_row)(keys).reshape(LEAVES, nbx, NNZB).astype(jnp.int32)


def level_of(rng, extent, cuts, low, top_value):
    loudness = 1.0
    for dim, blocks in cuts:
        draws = jax.random.uniform(jax.random.fold_in(jax.random.fold_in(rng, 6), dim), (blocks,), jnp.float32, low / len(cuts), top_value / len(cuts))
        loudness = loudness * jnp.repeat(jnp.exp(draws), extent[dim] // blocks).reshape((-1,) + (1,) * (len(extent) - 1 - dim))
    return loudness


def centred(key, shape, width, reach, shards=(), kind=jnp.bfloat16):
    values = width * jax.random.normal(key, shape, jnp.float32)
    if shards:
        values = values * level_of(key, shape, shards, -0.22, 0.18)
    return jnp.clip(values, -reach, reach).astype(kind)


def setup_inputs(seed: int = 0) -> dict:
    key_of = jax.random.split(jax.random.key(seed), 10)
    return {
        "leaf_cost": draw_leaf_cost(jax.random.fold_in(key_of[9], 71), 0),
        "a_blocks": centred(key_of[1], (LEAVES, NX // BLK, NNZA, BLK, BLK), (16 * BLK * NNZA) ** -0.5, 0.046875, ((0, 8),), jnp.float32),
        "a_cols": draw_a_cols(jax.random.fold_in(key_of[9], 71), 0),
        "b_blocks": centred(key_of[3], (LEAVES, NX // BLK, NNZB, BLK, BLK), (NX // 2) ** -0.5, 0.1875, ((0, 8),), jnp.float32),
        "b_cols": draw_b_cols(jax.random.fold_in(key_of[9], 71), 0),
        "branch_prob": jnp.clip(0.3 + 0.39999998 * jax.random.uniform(key_of[5], (LEAVES,), jnp.float32) ** level_of(key_of[5], (LEAVES,), ((0, 8),), -0.2, 0.2), 0.3, 0.7),
        "state_cost": jnp.clip(jnp.exp(math.log(2.0) - 1.3862944 * jax.random.uniform(key_of[6], (NX,), jnp.float32) ** level_of(key_of[6], (NX,), ((0, 4),), -0.2, 0.2)), 0.5, 2.0),
        "control_cost": jnp.clip(jnp.exp(jax.random.uniform(key_of[7], (NU,), jnp.float32, math.log(0.5), math.log(2.0))), 0.5, 2.0),
        "parent_state": centred(key_of[8], (PARENTS, NX, SAMPLES), 1.0, 6.0, ((1, 4),), jnp.float32),
    }


HIGH = lax.Precision.HIGHEST

def densify(blocks, cols, count):
    onehot = (cols[..., None] == jnp.arange(count)[None, None, :]).astype(jnp.float32)
    dense = jnp.einsum('ksj,ksab->kajb', onehot, blocks, precision=HIGH)
    return dense.reshape(blocks.shape[0] * blocks.shape[2], count * blocks.shape[3])

def lower_solve(factor, rhs):
    return lax.linalg.triangular_solve(factor, rhs, left_side=True, lower=True)

def upper_solve(factor, rhs):
    return lax.linalg.triangular_solve(factor, rhs, left_side=True, lower=True, transpose_a=True)

def reference(leaf_cost, a_blocks, a_cols, b_blocks, b_cols, branch_prob, state_cost, control_cost, parent_state):
    nbx = NX // BLK
    nbu = NU // BLK
    ident = jnp.eye(NX, dtype=jnp.float32)

    def parent_step(items):
        costs, ablk, acol, bblk, bcol, probs, start = items
        state_sum = jnp.diag(state_cost)
        cross = jnp.zeros((NU, NX), jnp.float32)
        gram = jnp.diag(control_cost)
        dyn = []
        for child in range(2):
            amat = densify(ablk[child], acol[child], nbx) + 0.75 * ident
            bmat = densify(bblk[child], bcol[child], nbu)
            image = jnp.dot(costs[child], amat, precision=HIGH)
            wimage = jnp.dot(costs[child], bmat, precision=HIGH)
            state_sum = state_sum + probs[child] * jnp.dot(amat.T, image, precision=HIGH)
            cross = cross + probs[child] * jnp.dot(bmat.T, image, precision=HIGH)
            gram = gram + probs[child] * jnp.dot(bmat.T, wimage, precision=HIGH)
            dyn.append((amat, bmat))
        factor = jnp.linalg.cholesky(gram)
        solved = lower_solve(factor, cross)
        pcost = state_sum - jnp.dot(solved.T, solved, precision=HIGH)
        gain = -upper_solve(factor, solved)
        control = jnp.dot(gain, start, precision=HIGH)
        nexts = [jnp.dot(m[0], start, precision=HIGH) + jnp.dot(m[1], control, precision=HIGH) for m in dyn]
        return (pcost, gain, jnp.stack(nexts))
    items = (leaf_cost.reshape(PARENTS, 2, NX, NX), a_blocks.reshape((PARENTS, 2) + a_blocks.shape[1:]), a_cols.reshape((PARENTS, 2) + a_cols.shape[1:]), b_blocks.reshape((PARENTS, 2) + b_blocks.shape[1:]), b_cols.reshape((PARENTS, 2) + b_cols.shape[1:]), branch_prob.reshape(PARENTS, 2), parent_state)
    pcosts, gains, nexts = lax.map(parent_step, items)
    parent_cost = jnp.repeat(pcosts, 2, axis=0)
    gain_out = jnp.repeat(gains, 2, axis=0)
    child_state = nexts.reshape(LEAVES, NX, SAMPLES)
    return (parent_cost, gain_out, child_state)
```

```python
import functools

import jax
import jax.numpy as jnp
from jax import lax
from jax.experimental import pallas as pl
from jax.experimental.pallas import tpu as pltpu
from jax.sharding import PartitionSpec as P

HIGHEST = lax.Precision.HIGHEST
F32 = jnp.float32
BF16 = jnp.bfloat16
VMEM_LIMIT = 48 * 2**20
NN = (((1,), (0,)), ((), ()))
NT = (((1,), (1,)), ((), ()))
TN = (((0,), (0,)), ((), ()))


def split(x):
    hi = x.astype(BF16)
    return hi, (x - hi.astype(F32)).astype(BF16)


def parted(x):
    hi = lax.reduce_precision(x, 8, 7)
    return hi.astype(BF16), (x - hi).astype(BF16)


def dot3(a, b, dims=NN):
    one = functools.partial(lax.dot_general, dimension_numbers=dims, preferred_element_type=F32)
    return one(a[0], b[0]) + (one(a[0], b[1]) + one(a[1], b[0]))


def dense_kernel(blk, step, nnza, nnzb, width, acol, bcol, a_ref, b_ref, p_ref, fh, fl, ph, pl_, w_ref, buf):
    i = pl.program_id(0)
    buf[...] = jnp.zeros_like(buf)
    diag = lax.broadcasted_iota(jnp.int32, (blk, blk), 0) == lax.broadcasted_iota(jnp.int32, (blk, blk), 1)
    eye = jnp.where(diag, 0.75, 0.0).astype(F32)
    for t in range(step // blk):
        row = i * (step // blk) + t
        for s in range(nnza):
            col = pl.multiple_of(acol[row * nnza + s] * blk, blk)
            block = a_ref[t, s]
            if s == 0:
                block = block + eye
            buf[t * blk : (t + 1) * blk, pl.ds(col, blk)] = block
        for s in range(nnzb):
            col = pl.multiple_of(width + bcol[row * nnzb + s] * blk, blk)
            buf[t * blk : (t + 1) * blk, pl.ds(col, blk)] = b_ref[t, s]
    hi, lo = split(buf[...])
    fh[...] = hi
    fl[...] = lo
    phi, plo = split(p_ref[...])
    ph[...] = phi
    pl_[...] = plo
    part = dot3((phi, plo), (hi[:, width:], lo[:, width:]))

    @pl.when(i == 0)
    def _():
        w_ref[...] = part

    @pl.when(i > 0)
    def _():
        w_ref[...] += part


def dense(cost_rows, a_blocks, a_cols, b_blocks, b_cols, orders):
    rows, width = cost_rows.shape
    nbx, nnza, blk, _ = a_blocks.shape
    nnzb = b_blocks.shape[1]
    step = 2 * blk
    total = width + orders
    return pl.pallas_call(
        functools.partial(dense_kernel, blk, step, nnza, nnzb, width),
        grid_spec=pltpu.PrefetchScalarGridSpec(
            num_scalar_prefetch=2,
            grid=(width // step,),
            in_specs=[
                pl.BlockSpec((2, nnza, blk, blk), lambda i, *_: (i, 0, 0, 0)),
                pl.BlockSpec((2, nnzb, blk, blk), lambda i, *_: (i, 0, 0, 0)),
                pl.BlockSpec((rows, step), lambda i, *_: (0, i)),
            ],
            out_specs=[
                pl.BlockSpec((step, total), lambda i, *_: (i, 0)),
                pl.BlockSpec((step, total), lambda i, *_: (i, 0)),
                pl.BlockSpec((rows, step), lambda i, *_: (0, i)),
                pl.BlockSpec((rows, step), lambda i, *_: (0, i)),
                pl.BlockSpec((rows, orders), lambda i, *_: (0, 0)),
            ],
            scratch_shapes=[pltpu.VMEM((step, total), F32)],
        ),
        out_shape=[
            jax.ShapeDtypeStruct((width, total), BF16),
            jax.ShapeDtypeStruct((width, total), BF16),
            jax.ShapeDtypeStruct((rows, width), BF16),
            jax.ShapeDtypeStruct((rows, width), BF16),
            jax.ShapeDtypeStruct((rows, orders), F32),
        ],
        compiler_params=pltpu.CompilerParams(vmem_limit_bytes=VMEM_LIMIT),
        cost_estimate=pl.CostEstimate(
            flops=6 * rows * width * orders, bytes_accessed=8 * width * total + 8 * rows * width, transcendentals=0
        ),
        name="dense",
    )(a_cols.reshape(-1), b_cols.reshape(-1), a_blocks, b_blocks, cost_rows)


def image_kernel(where, weight, fh, fl, ph, pl_, out, acc):
    k = pl.program_id(0)
    part = dot3((ph[...], pl_[...]), (fh[...], fl[...]))

    @pl.when(k == 0)
    def _():
        acc[...] = part

    @pl.when(k > 0)
    def _():
        acc[...] += part

    @pl.when(k == pl.num_programs(0) - 1)
    def _():
        out[...] = acc[...].T * weight[0]


def image(where, weight, fh, fl, ph, pl_):
    rows, width = ph.shape
    chunk = 512
    return pl.pallas_call(
        image_kernel,
        grid_spec=pltpu.PrefetchScalarGridSpec(
            num_scalar_prefetch=2,
            grid=(width // chunk,),
            in_specs=[
                pl.BlockSpec((chunk, rows), lambda k, where, _: (k, where[0])),
                pl.BlockSpec((chunk, rows), lambda k, where, _: (k, where[0])),
                pl.BlockSpec((rows, chunk), lambda k, *_: (0, k)),
                pl.BlockSpec((rows, chunk), lambda k, *_: (0, k)),
            ],
            out_specs=pl.BlockSpec((rows, rows), lambda k, *_: (0, 0)),
            scratch_shapes=[pltpu.VMEM((rows, rows), F32)],
        ),
        out_shape=jax.ShapeDtypeStruct((rows, rows), F32),
        compiler_params=pltpu.CompilerParams(vmem_limit_bytes=VMEM_LIMIT),
        cost_estimate=pl.CostEstimate(
            flops=6 * rows * rows * width, bytes_accessed=8 * rows * width, transcendentals=0
        ),
        name="image",
    )(where, weight, fh, fl, ph, pl_)


def gather_kernel(first, where, y_ref, fh, fl, *refs):
    out = refs[-1]
    part = dot3(split(y_ref[...]), (fh[...], fl[...]))
    out[...] = part if first else refs[0][...] + part


def accumulate(where, y, fh, fl, acc):
    rows = y.shape[0]
    total = fh.shape[1]
    tile = 512
    first = acc is None
    spec = pl.BlockSpec((rows, tile), lambda n, where: (0, n))
    factor = pl.BlockSpec((rows, tile), lambda n, where: (where[0], n))
    return pl.pallas_call(
        functools.partial(gather_kernel, first),
        grid_spec=pltpu.PrefetchScalarGridSpec(
            num_scalar_prefetch=1,
            grid=(total // tile,),
            in_specs=[pl.BlockSpec((rows, rows), lambda n, where: (0, 0)), factor, factor] + [spec] * (not first),
            out_specs=spec,
        ),
        out_shape=jax.ShapeDtypeStruct((rows, total), F32),
        input_output_aliases={} if first else {4: 0},
        compiler_params=pltpu.CompilerParams(vmem_limit_bytes=VMEM_LIMIT),
        cost_estimate=pl.CostEstimate(
            flops=6 * rows * rows * total, bytes_accessed=12 * rows * total, transcendentals=0
        ),
        name="accumulate",
    )(where, y, fh, fl, *(() if first else (acc,)))


def inverse_block(m):
    n = m.shape[0]
    sub = lax.broadcasted_iota(jnp.int32, (n, n), 0)
    lane = lax.broadcasted_iota(jnp.int32, (n, n), 1)
    for j in range(n):
        pivot = 1.0 / m[j : j + 1, j : j + 1]
        col = m[:, j : j + 1]
        row = jnp.where(lane[:1] == j, 1.0, m[j : j + 1, :]) * pivot
        m = jnp.where(sub == j, row, jnp.where(lane == j, 0.0, m) - col * row)
    return m


def inverse_kernel(blk, h_ref, out):
    n = h_ref.shape[0]
    dot = functools.partial(jnp.dot, precision=HIGHEST, preferred_element_type=F32)
    out[...] = h_ref[...]

    @pl.loop(0, n // blk)
    def _(b):
        here = pl.ds(pl.multiple_of(b * blk, blk), blk)
        inv = inverse_block(out[here, here])
        row = dot(inv, out[here, :])
        col = out[:, here]
        out[...] -= dot(col, row)
        out[:, here] = -dot(col, inv)
        out[here, :] = row
        out[here, here] = inv


def inverse(h, blk):
    n = h.shape[0]
    return pl.pallas_call(
        functools.partial(inverse_kernel, blk),
        out_shape=jax.ShapeDtypeStruct((n, n), F32),
        compiler_params=pltpu.CompilerParams(vmem_limit_bytes=VMEM_LIMIT),
        cost_estimate=pl.CostEstimate(flops=2**32, bytes_accessed=8 * n * n, transcendentals=n),
        name="inverse",
    )(h)


def final_kernel(where, s_ref, t_ref, k_ref, g_ref, d_ref, out):
    n = pl.program_id(0)
    rows = out.shape[0]
    part = s_ref[...] + t_ref[...] + dot3(split(k_ref[...]), split(g_ref[0]), NT)
    diag = lax.broadcasted_iota(jnp.int32, (rows, rows), 0) == lax.broadcasted_iota(jnp.int32, (rows, rows), 1)
    cost = jnp.where(diag & (n == where[0]), d_ref[...], 0.0)
    out[...] = part + cost


def final(where, own, other, gain_t, cross_t, state_cost):
    rows = own.shape[0]
    parts, _, orders = cross_t.shape
    spec = pl.BlockSpec((rows, rows), lambda n, where: (0, n))
    return pl.pallas_call(
        final_kernel,
        grid_spec=pltpu.PrefetchScalarGridSpec(
            num_scalar_prefetch=1,
            grid=(parts,),
            in_specs=[
                spec,
                spec,
                pl.BlockSpec((rows, orders), lambda n, where: (0, 0)),
                pl.BlockSpec((1, rows, orders), lambda n, where: (n, 0, 0)),
                pl.BlockSpec((1, rows), lambda n, where: (0, 0)),
            ],
            out_specs=spec,
        ),
        out_shape=jax.ShapeDtypeStruct((rows, parts * rows), F32),
        compiler_params=pltpu.CompilerParams(vmem_limit_bytes=VMEM_LIMIT),
        cost_estimate=pl.CostEstimate(
            flops=6 * rows * rows * parts * orders, bytes_accessed=16 * rows * rows * parts, transcendentals=0
        ),
        name="final",
    )(where, own, other, gain_t, cross_t, state_cost[None])


def swapped(x):
    n = lax.axis_size("leaf")
    return lax.ppermute(x, "leaf", [(i, i ^ 1) for i in range(n)])


def shards(
    leaf_cost,
    a_blocks,
    a_cols,
    b_blocks,
    b_cols,
    branch_prob,
    state_cost,
    control_cost,
    parent_state,
):
    rows, width = leaf_cost.shape[1:]
    blk = a_blocks.shape[3]
    orders = control_cost.shape[0]
    parts = lax.axis_size("row")
    z = lax.axis_index("row")
    leaf = lax.axis_index("leaf")
    core = leaf % 2
    weight = branch_prob[0]

    def halves(x, axis):
        size = x.shape[axis] // 2
        return lax.dynamic_slice_in_dim(x, core * size, size, axis)

    def joined(mine, axis):
        other = swapped(mine)
        first = jnp.where(core == 0, mine, other)
        second = jnp.where(core == 0, other, mine)
        return jnp.concatenate((first, second), axis)

    own_state = lax.dynamic_index_in_dim(parent_state, leaf // 2, 0, keepdims=False)
    full_state = joined(lax.all_gather(halves(own_state, 0), "row"), 1).reshape(width, -1)

    fh, fl, ph, pl_, w = dense(leaf_cost[0], a_blocks[0], a_cols[0], b_blocks[0], b_cols[0], orders)
    first = z * rows
    mine = lax.dynamic_slice_in_dim(fh, first, rows, 0), lax.dynamic_slice_in_dim(fl, first, rows, 0)
    a_mine = mine[0][:, :width], mine[1][:, :width]
    b_mine = mine[0][:, width:], mine[1][:, width:]

    arrived = []
    for d in list(range(1, parts)) + [0]:
        to = (z + d) % parts
        block = image(to[None], branch_prob, fh, fl, ph, pl_)
        if d:
            block = lax.ppermute(block, "row", [(i, (i + d) % parts) for i in range(parts)])
        arrived.append(((z - d) % parts, block))

    w_pair = parted(w)
    drift = dot3(a_mine, parted(full_state))
    gram = jnp.concatenate((dot3(b_mine, w_pair, TN), dot3(w_pair, parted(drift), TN)), axis=1) * weight
    gram = gram + swapped(gram)
    gram = joined(lax.psum(halves(gram, 0), "row"), 0)
    hinv = inverse(gram[:, :orders] + jnp.diag(control_cost), blk)
    order = -jnp.dot(hinv, gram[:, orders:], precision=HIGHEST)
    reached = drift + dot3(b_mine, parted(order))

    acc = None
    for source, block in arrived[-1:] + arrived[:-1]:
        acc = accumulate(source[None], block, fh, fl, acc)
    cross = acc[:, width:]
    cross = cross + swapped(cross)
    other = swapped(acc[:, :width])
    every = joined(lax.all_gather(halves(cross, 0), "row"), 1)
    gain_t = -jnp.dot(cross, hinv, precision=HIGHEST)
    pcost = final(z[None], acc, other, gain_t, every, state_cost)
    return pcost[None], gain_t.T[None], reached[None]


def solution(mesh):
    placed = (
        P("leaf", "row", None),
        P("leaf", None, None, None, None),
        P("leaf", None, None),
        P("leaf", None, None, None, None),
        P("leaf", None, None),
        P("leaf"),
        P("row"),
        P(),
        P(None, "row", None),
    )
    return jax.shard_map(
        shards,
        mesh=mesh,
        in_specs=placed,
        out_specs=(P("leaf", "row", None), P("leaf", None, "row"), P("leaf", "row", None)),
        check_vma=False,
    )
```

```python
import functools

import jax
import jax.numpy as jnp
from jax import lax
from jax.experimental import pallas as pl
from jax.experimental.pallas import tpu as pltpu
from jax.sharding import PartitionSpec as P

HIGHEST = lax.Precision.HIGHEST
F32 = jnp.float32
BF16 = jnp.bfloat16
VMEM_LIMIT = 48 * 2**20
NN = (((1,), (0,)), ((), ()))
NT = (((1,), (1,)), ((), ()))


def split(x):
    hi = x.astype(BF16)
    return hi, (x - hi.astype(F32)).astype(BF16)


def parted(x):
    hi = lax.reduce_precision(x, 8, 7)
    return hi.astype(BF16), (x - hi).astype(BF16)


def dot3(a, b, dims=NN):
    one = functools.partial(lax.dot_general, dimension_numbers=dims, preferred_element_type=F32)
    return one(a[0], b[0]) + (one(a[0], b[1]) + one(a[1], b[0]))


def call(kernel, grid, prefetch, ins, outs, shapes, flops, traffic, name, scratch=(), aliases=None):
    return pl.pallas_call(
        kernel,
        grid_spec=pltpu.PrefetchScalarGridSpec(
            num_scalar_prefetch=prefetch, grid=grid, in_specs=ins, out_specs=outs, scratch_shapes=scratch
        ),
        out_shape=[jax.ShapeDtypeStruct(shape, kind) for shape, kind in shapes],
        input_output_aliases=aliases or {},
        compiler_params=pltpu.CompilerParams(vmem_limit_bytes=VMEM_LIMIT),
        cost_estimate=pl.CostEstimate(flops=flops, bytes_accessed=traffic, transcendentals=0),
        name=name,
    )


def whole(*shape):
    return pl.BlockSpec(shape, lambda *_: (0,) * len(shape))


def lower(n):
    return [(i, j) for i in range(n) for j in range(i + 1)]


def dense_kernel(blk, step, nnza, nnzb, width, where, acol, bcol, a_ref, b_ref, p_ref, fh, fl, uh, ul, w_ref, buf):
    i = pl.program_id(0)
    rows = p_ref.shape[0]
    buf[...] = jnp.zeros_like(buf)
    diag = lax.broadcasted_iota(jnp.int32, (blk, blk), 0) == lax.broadcasted_iota(jnp.int32, (blk, blk), 1)
    eye = jnp.where(diag, 0.75, 0.0).astype(F32)
    for t in range(step // blk):
        row = i * (step // blk) + t
        for s in range(nnza):
            col = pl.multiple_of(acol[row * nnza + s] * blk, blk)
            block = a_ref[t, s]
            if s == 0:
                block = block + eye
            buf[t * blk : (t + 1) * blk, pl.ds(col, blk)] = block
        for s in range(nnzb):
            col = pl.multiple_of(width + bcol[row * nnzb + s] * blk, blk)
            buf[t * blk : (t + 1) * blk, pl.ds(col, blk)] = b_ref[t, s]
    hi, lo = split(buf[...])
    fh[...] = hi
    fl[...] = lo
    orders = buf.shape[1] - width
    uh[:orders], ul[:orders] = split(buf[:, width:].T)
    uh[orders:], ul[orders:] = split(buf[:, pl.ds(pl.multiple_of(where[0] * rows, rows), rows)].T)
    part = dot3(split(p_ref[...]), (hi[:, width:], lo[:, width:]))

    @pl.when(i == 0)
    def _():
        w_ref[...] = part

    @pl.when(i > 0)
    def _():
        w_ref[...] += part


def dense(where, cost_rows, a_blocks, a_cols, b_blocks, b_cols, orders):
    rows, width = cost_rows.shape
    _, nnza, blk, _ = a_blocks.shape
    nnzb = b_blocks.shape[1]
    step = 2 * blk
    total = width + orders
    factor = pl.BlockSpec((step, total), lambda i, *_: (i, 0))
    turned = pl.BlockSpec((rows + orders, step), lambda i, *_: (0, i))
    return call(
        functools.partial(dense_kernel, blk, step, nnza, nnzb, width),
        (width // step,),
        3,
        [
            pl.BlockSpec((2, nnza, blk, blk), lambda i, *_: (i, 0, 0, 0)),
            pl.BlockSpec((2, nnzb, blk, blk), lambda i, *_: (i, 0, 0, 0)),
            pl.BlockSpec((rows, step), lambda i, *_: (0, i)),
        ],
        [factor, factor, turned, turned, whole(rows, orders)],
        [((width, total), BF16)] * 2 + [((rows + orders, width), BF16)] * 2 + [((rows, orders), F32)],
        6 * rows * width * orders,
        8 * width * total,
        "dense",
        [pltpu.VMEM((step, total), F32)],
    )(where, a_cols.reshape(-1), b_cols.reshape(-1), a_blocks, b_blocks, cost_rows)


def gram_kernel(blk, weight, bh, bl, ah, al, w_ref, x_ref, tiles, drift):
    w = w_ref[...]
    h = dot3((bh[...], bl[...]), split(w)) * weight[0]
    y = dot3((ah[...], al[...]), split(x_ref[...]))
    drift[...] = y
    q = dot3(split(w.T), split(y)) * weight[0]
    pairs = lower(h.shape[0] // blk)
    for t, (i, j) in enumerate(pairs):
        tiles[t] = h[i * blk : (i + 1) * blk, j * blk : (j + 1) * blk]
    for i in range(h.shape[0] // blk):
        tiles[len(pairs) + i] = q[i * blk : (i + 1) * blk]


def gram(weight, where, fh, fl, uh, ul, w, x, blk):
    rows, orders = w.shape
    width, samples = x.shape
    count = orders // blk
    count = count * (count + 1) // 2 + count
    turned = pl.BlockSpec((orders, rows), lambda i, weight, where: (0, where[0]))
    factor = pl.BlockSpec((rows, width), lambda i, weight, where: (where[0], 0))

    def kernel(weight, where, *refs):
        gram_kernel(blk, weight, *refs)

    return call(
        kernel,
        (1,),
        2,
        [turned, turned, factor, factor, whole(rows, orders), whole(width, samples)],
        [whole(count, blk, samples), whole(rows, samples)],
        [((count, blk, samples), F32), ((rows, samples), F32)],
        6 * rows * orders * orders,
        6 * rows * width,
        "gram",
    )(weight, where, uh, ul, fh, fl, w, x)


def inverse_block(m):
    n = m.shape[0]
    sub = lax.broadcasted_iota(jnp.int32, (n, n), 0)
    lane = lax.broadcasted_iota(jnp.int32, (n, n), 1)
    for j in range(n):
        pivot = 1.0 / m[j : j + 1, j : j + 1]
        col = m[:, j : j + 1]
        row = jnp.where(lane[:1] == j, 1.0, m[j : j + 1, :]) * pivot
        m = jnp.where(sub == j, row, jnp.where(lane == j, 0.0, m) - col * row)
    return m


def inverse_kernel(blk, tiles, d_ref, out, u_ref):
    n = out.shape[0]
    dot = functools.partial(jnp.dot, precision=HIGHEST, preferred_element_type=F32)
    pairs = lower(n // blk)
    for t, (i, j) in enumerate(pairs):
        out[i * blk : (i + 1) * blk, j * blk : (j + 1) * blk] = tiles[t]
        if i != j:
            out[j * blk : (j + 1) * blk, i * blk : (i + 1) * blk] = tiles[t].T
    diag = lax.broadcasted_iota(jnp.int32, (n, n), 0) == lax.broadcasted_iota(jnp.int32, (n, n), 1)
    out[...] += jnp.where(diag, d_ref[...], 0.0)

    @pl.loop(0, n // blk)
    def _(b):
        here = pl.ds(pl.multiple_of(b * blk, blk), blk)
        inv = inverse_block(out[here, here])
        row = dot(inv, out[here, :])
        col = out[:, here]
        out[...] -= dot(col, row)
        out[:, here] = -dot(col, inv)
        out[here, :] = row
        out[here, here] = inv

    q = jnp.concatenate([tiles[len(pairs) + i] for i in range(n // blk)], axis=0)
    u_ref[...] = -dot(out[...], q)


def inverse(tiles, control_cost, *after):
    count, blk, samples = tiles.shape
    n = control_cost.shape[0]

    def kernel(tiles, d_ref, *refs):
        inverse_kernel(blk, tiles, d_ref, *refs[-2:])

    return call(
        kernel,
        (1,),
        0,
        [whole(count, blk, samples), whole(1, n)] + [pl.BlockSpec(memory_space=pl.ANY)] * len(after),
        [whole(n, n), whole(n, samples)],
        [((n, n), F32), ((n, samples), F32)],
        2**34,
        8 * n * n,
        "inverse",
    )(tiles, control_cost[None], *after)


def pack_kernel(blk, where, d_ref, *refs):
    n = len(refs) // 2
    for t, (i, j) in enumerate(lower(d_ref.shape[0] // blk)):
        refs[n][t] = d_ref[i * blk : (i + 1) * blk, j * blk : (j + 1) * blk]
    for t in range(n):
        refs[n + 1 + t][...] = refs[t][...]


def pack(where, cost_rows, blk):
    rows = cost_rows.shape[0]
    count = len(lower(rows // blk))
    specs = [pl.BlockSpec((rows, rows), functools.partial(lambda t, i, where: (0, where[t]), t)) for t in range(4)]
    return call(
        functools.partial(pack_kernel, blk),
        (1,),
        1,
        specs,
        [whole(count, blk, blk)] + [whole(rows, rows)] * 3,
        [((count, blk, blk), F32)] + [((rows, rows), F32)] * 3,
        1,
        8 * rows * rows * 4,
        "pack",
    )(where, *[cost_rows] * 4)


def unpacked(tiles, n):
    blocks = [[None] * n for _ in range(n)]
    for t, (i, j) in enumerate(lower(n)):
        blocks[i][j] = tiles[t]
        if i != j:
            blocks[j][i] = tiles[t].T
    return jnp.concatenate([jnp.concatenate(row, axis=1) for row in blocks], axis=0)


def begin_kernel(where, p_ref, uh, ul, vh, vl, mine, rest):
    j = pl.program_id(0)
    p = split(p_ref[...])
    part = dot3((uh[...], ul[...]), p, NT)

    @pl.when(j == 0)
    def _():
        mine[...] = part

    @pl.when(j > 0)
    def _():
        mine[...] += part

    rest[...] = dot3((vh[...], vl[...]), p)


def begin(where, cost_rows, uh, ul, *after):
    rows, width = cost_rows.shape
    tall = uh.shape[0]
    each = pl.BlockSpec((tall, rows), lambda j, where: (0, j))
    own = pl.BlockSpec((tall, rows), lambda j, where: (0, where[0]))

    def kernel(where, *refs):
        begin_kernel(where, *refs[:5], *refs[-2:])

    return call(
        kernel,
        (width // rows,),
        1,
        [pl.BlockSpec((rows, rows), lambda j, where: (0, j)), each, each, own, own]
        + [pl.BlockSpec(memory_space=pl.ANY)] * len(after),
        [whole(tall, rows), each],
        [((tall, rows), F32), ((tall, width), F32)],
        12 * tall * rows * width,
        16 * tall * width,
        "begin",
    )(where, cost_rows, uh, ul, uh, ul, *after)


def grow_kernel(options, where, *refs):
    size = len(refs[:-7]) // options
    uh, ul, vh, vl, n_in, n_out, done = refs[-7:]
    g = pl.program_id(0)
    for c in range(options):
        tiles, *blocks = refs[c * size : (c + 1) * size]
        chosen = where[0] == c

        @pl.when((g == 0) & chosen)
        def _():
            part = dot3((uh[...], ul[...]), split(unpacked(tiles, done.shape[1] // tiles.shape[1])))
            done[...] = n_in[...] + part
            n_out[...] = n_in[...]

        for t, block in enumerate(blocks):

            @pl.when((g == t + 1) & chosen)
            def _():
                x = split(block[...])
                done[...] += dot3((uh[...], ul[...]), x, NT)
                n_out[...] = n_in[...] + dot3((vh[...], vl[...]), x)


def grow(where, options, uh, ul, n, *after):
    size = len(options[0])
    count, blk, _ = options[0][0].shape
    tall, width = n.shape
    rows = width // 4
    block = pl.BlockSpec((tall, rows), lambda g, where: (0, where[1 + g]))
    focus = pl.BlockSpec((tall, rows), lambda g, where: (0, where[1]))
    ins = size * len(options) + 5

    def kernel(where, *refs):
        grow_kernel(len(options), where, *refs[:ins], *refs[-2:])

    return call(
        kernel,
        (size,),
        1,
        ([whole(count, blk, blk)] + [whole(rows, rows)] * (size - 1)) * len(options)
        + [block, block, focus, focus, block]
        + [pl.BlockSpec(memory_space=pl.ANY)] * len(after),
        [block, whole(tall, rows)],
        [((tall, width), F32), ((tall, rows), F32)],
        6 * tall * rows * rows * (2 * size - 1),
        12 * tall * rows * size,
        "grow",
        aliases={ins: 0},
    )(where, *[x for option in options for x in option], uh, ul, uh, ul, n, *after)


def spread_kernel(first, where, weight, n_ref, fh, fl, *refs):
    s_out, g_out, hi, lo = refs[-4:]

    @pl.when(pl.program_id(0) == 0)
    def _():
        hi[...], lo[...] = split(n_ref[...] * weight[0])

    part = dot3((hi[...], lo[...]), (fh[...], fl[...]))
    orders = g_out.shape[0]
    if first:
        s_out[...] = part[orders:]
        g_out[...] = part[:orders]
    else:
        s_out[...] = refs[0][...] + part[orders:]
        g_out[...] = refs[1][...] + part[:orders]


def spread(where, weight, n, fh, fl, width, sums=()):
    tall, rows = n.shape
    orders = tall - rows
    tile = 512
    s_spec = pl.BlockSpec((rows, tile), lambda n, *_: (0, n))
    g_spec = pl.BlockSpec((orders, tile), lambda n, *_: (0, n))
    factor = pl.BlockSpec((rows, tile), lambda n, where, _: (where[0], n))
    return call(
        functools.partial(spread_kernel, not sums),
        (width // tile,),
        2,
        [whole(tall, rows), factor, factor] + ([s_spec, g_spec] if sums else []),
        [s_spec, g_spec],
        [((rows, width), F32), ((orders, width), F32)],
        6 * tall * rows * width,
        12 * tall * width,
        "spread",
        [pltpu.VMEM((tall, rows), BF16)] * 2,
        {5: 0, 6: 1} if sums else None,
    )(where, weight, n, fh, fl, *sums)


def final_kernel(where, h_ref, g1, g2, s1, s2, q1, q2, d_ref, gain, out, hi, lo):
    n = pl.program_id(0)
    rows = out.shape[0]

    @pl.when(n == 0)
    def _():
        value = -dot3(split(h_ref[...]), split(g1[...] + g2[...]))
        gain[...] = value
        hi[...], lo[...] = split(value.T)

    part = s1[...] + s2[...] + dot3((hi[...], lo[...]), split(q1[...] + q2[...]))
    diag = lax.broadcasted_iota(jnp.int32, (rows, rows), 0) == lax.broadcasted_iota(jnp.int32, (rows, rows), 1)
    out[...] = part + jnp.where(diag & (n == where[0]), d_ref[...], 0.0)


def final(where, hinv, own, other, state_cost):
    rows, width = own[0].shape
    orders = own[1].shape[0]
    s_spec = pl.BlockSpec((rows, rows), lambda n, where: (0, n))
    g_spec = pl.BlockSpec((orders, rows), lambda n, where: (0, n))
    mine = pl.BlockSpec((orders, rows), lambda n, where: (0, where[0]))
    return call(
        final_kernel,
        (width // rows,),
        1,
        [whole(orders, orders), mine, mine, s_spec, s_spec, g_spec, g_spec, whole(1, rows)],
        [whole(orders, rows), s_spec],
        [((orders, rows), F32), ((rows, width), F32)],
        6 * rows * width * orders,
        20 * rows * width,
        "final",
        [pltpu.VMEM((rows, orders), BF16)] * 2,
    )(where, hinv, own[1], other[1], own[0], other[0], own[1], other[1], state_cost[None])


def image_kernel(where, weight, fh, fl, p_ref, out, acc):
    k = pl.program_id(0)
    part = dot3(split(p_ref[...]), (fh[...], fl[...]))

    @pl.when(k == 0)
    def _():
        acc[...] = part

    @pl.when(k > 0)
    def _():
        acc[...] += part

    @pl.when(k == pl.num_programs(0) - 1)
    def _():
        out[...] = acc[...].T * weight[0]


def image(where, weight, fh, fl, cost_rows):
    rows, width = cost_rows.shape
    chunk = 512
    factor = pl.BlockSpec((chunk, rows), lambda k, where, _: (k, where[0]))
    return call(
        image_kernel,
        (width // chunk,),
        2,
        [factor, factor, pl.BlockSpec((rows, chunk), lambda k, *_: (0, k))],
        [whole(rows, rows)],
        [((rows, rows), F32)],
        6 * rows * rows * width,
        8 * rows * width,
        "image",
        [pltpu.VMEM((rows, rows), F32)],
    )(where, weight, fh, fl, cost_rows)[0]


def accumulate_kernel(first, where, y_ref, fh, fl, *refs):
    out = refs[-1]
    part = dot3(split(y_ref[...]), (fh[...], fl[...]))
    out[...] = part if first else refs[0][...] + part


def accumulate(where, y, fh, fl, acc):
    rows = y.shape[0]
    total = fh.shape[1]
    tile = 512
    first = acc is None
    spec = pl.BlockSpec((rows, tile), lambda n, where: (0, n))
    factor = pl.BlockSpec((rows, tile), lambda n, where: (where[0], n))
    return call(
        functools.partial(accumulate_kernel, first),
        (total // tile,),
        1,
        [whole(rows, rows), factor, factor] + [spec] * (not first),
        [spec],
        [((rows, total), F32)],
        6 * rows * rows * total,
        12 * rows * total,
        "accumulate",
        aliases=None if first else {4: 0},
    )(where, y, fh, fl, *(() if first else (acc,)))[0]


def by_images(z, parts, weight, cost_rows, fh, fl):
    rows, width = cost_rows.shape
    acc = None
    for d in range(parts):
        block = image(((z + d) % parts)[None], weight, fh, fl, cost_rows)
        if d:
            block = lax.ppermute(block, "row", [(i, (i + d) % parts) for i in range(parts)])
        acc = accumulate(((z - d) % parts)[None], block, fh, fl, acc)
    cross = lax.all_gather(acc[:, width:], "row")
    return acc[:, :width], jnp.swapaxes(cross.reshape(width, -1), 0, 1)


def by_blocks(z, weight, cost_rows, fh, fl, uh, ul, blk, sent, after):
    width = cost_rows.shape[1]
    edge = (z == 0) | (z == 3)
    left = z < 2

    def at(i):
        return jnp.where(left, i, 3 - i)

    def moved(x, pairs):
        return lax.ppermute(x, "row", pairs)

    diag, near, inner, far = sent
    partner = [moved(x, [(0, 1), (1, 0), (2, 3), (3, 2)]) for x in (diag, inner, far)]
    mid = [moved(x, [(1, 2), (2, 1)]) for x in (diag, near, partner[0])]
    ends = [moved(x, [(1, 0), (2, 3)]) for x in mid]

    mine, n = begin(z[None], cost_rows, uh, ul, *after)
    sums = spread(z[None], weight, mine, fh, fl, width)
    where = jnp.stack([z * 0, z ^ 1, at(2), at(3)])
    n, done = grow(where, [partner], uh, ul, n, *mid)
    sums = spread(where[1:2], weight, done, fh, fl, width, sums)
    where = jnp.stack([edge.astype(jnp.int32), at(2), at(3)])
    n, done = grow(where, [mid[:2], ends[:2]], uh, ul, n)
    sums = spread(where[1:2], weight, done, fh, fl, width, sums)
    where = jnp.stack([edge.astype(jnp.int32), at(3)])
    n, done = grow(where, [mid[2:], ends[2:]], uh, ul, n)
    return spread(where[1:2], weight, done, fh, fl, width, sums)


def swapped(x):
    n = lax.axis_size("leaf")
    return lax.ppermute(x, "leaf", [(i, i ^ 1) for i in range(n)])


def shards(
    leaf_cost,
    a_blocks,
    a_cols,
    b_blocks,
    b_cols,
    branch_prob,
    state_cost,
    control_cost,
    parent_state,
):
    cost_rows = leaf_cost[0]
    rows, width = cost_rows.shape
    blk = a_blocks.shape[3]
    orders = control_cost.shape[0]
    parts = lax.axis_size("row")
    z = lax.axis_index("row")
    leaf = lax.axis_index("leaf")
    core = leaf % 2
    line = parts == 4 and rows == orders

    def halves(x, axis):
        size = x.shape[axis] // 2
        return lax.dynamic_slice_in_dim(x, core * size, size, axis)

    def joined(mine, axis):
        other = swapped(mine)
        first = jnp.where(core == 0, mine, other)
        second = jnp.where(core == 0, other, mine)
        return jnp.concatenate((first, second), axis)

    if line:
        left = z < 2
        near = jnp.where(left, 0, 3)
        sent = pack(jnp.stack([z, near, jnp.where(left, 2, 1), 3 - near]), cost_rows, blk)

    own_state = halves(lax.dynamic_index_in_dim(parent_state, leaf // 2, 0, keepdims=False), 0)
    states = jnp.zeros((parts,) + own_state.shape, F32)
    for d in range(parts):
        block = own_state
        if d:
            block = lax.ppermute(block, "row", [(i, (i + d) % parts) for i in range(parts)])
        states = lax.dynamic_update_index_in_dim(states, block, (z - d) % parts, 0)
    full_state = joined(states, 1).reshape(width, -1)

    fh, fl, uh, ul, w = dense(z[None], cost_rows, a_blocks[0], a_cols[0], b_blocks[0], b_cols[0], orders)
    tiles, drift = gram(branch_prob, z[None], fh, fl, uh, ul, w, full_state, blk)
    tiles = tiles + swapped(tiles)
    tiles_half = halves(tiles, 0)
    tiles = joined(lax.psum(tiles_half, "row"), 0)
    if line:
        own = by_blocks(z, branch_prob, cost_rows, fh, fl, uh, ul, blk, sent, [tiles_half])
    else:
        own = by_images(z, parts, branch_prob, cost_rows, fh, fl)
    hinv, order = inverse(tiles, control_cost)
    b_mine = [lax.dynamic_slice(f, (z * rows, width), (rows, orders)) for f in (fh, fl)]
    reached = drift + dot3(b_mine, parted(order))
    other = tuple(swapped(x) for x in own)
    gain, pcost = final(z[None], hinv, own, other, state_cost)
    return pcost[None], gain[None], reached[None]


def solution(mesh):
    placed = (
        P("leaf", "row", None),
        P("leaf", None, None, None, None),
        P("leaf", None, None),
        P("leaf", None, None, None, None),
        P("leaf", None, None),
        P("leaf"),
        P("row"),
        P(),
        P(None, "row", None),
    )
    return jax.shard_map(
        shards,
        mesh=mesh,
        in_specs=placed,
        out_specs=(P("leaf", "row", None), P("leaf", None, "row"), P("leaf", "row", None)),
        check_vma=False,
    )
```

```python
import functools

import jax
import jax.numpy as jnp
from jax import lax
from jax.experimental import pallas as pl
from jax.experimental.pallas import tpu as pltpu
from jax.sharding import PartitionSpec as P

HIGHEST = lax.Precision.HIGHEST
F32 = jnp.float32
BF16 = jnp.bfloat16
VMEM_LIMIT = 56 * 2**20
NN = (((1,), (0,)), ((), ()))
NT = (((1,), (1,)), ((), ()))


def split(x):
    hi = x.astype(BF16)
    return hi, (x - hi.astype(F32)).astype(BF16)


def parted(x):
    hi = lax.reduce_precision(x, 8, 7)
    return hi.astype(BF16), (x - hi).astype(BF16)


def dot3(a, b, dims=NN):
    (left,), (right,) = dims[0]
    a = jnp.concatenate((a[0], a[0], a[1]), axis=left)
    b = jnp.concatenate((b[0], b[1], b[0]), axis=right)
    return lax.dot_general(a, b, dims, preferred_element_type=F32)


def call(kernel, grid, prefetch, ins, outs, shapes, name, scratch=(), aliases=None, after=(), through=()):
    n_in, n_out = len(ins), len(outs)
    extra = len(after) + len(through)
    anywhere = pl.BlockSpec(memory_space=pl.ANY)

    def body(*refs):
        start = prefetch + n_in
        stop = start + extra + n_out
        kernel(*refs[:start], *refs[start + extra : stop], *refs[stop + len(through) :])

    aliases = dict(aliases or {})
    for t in range(len(through)):
        aliases[prefetch + n_in + len(after) + t] = n_out + t
    built = pl.pallas_call(
        body,
        grid_spec=pltpu.PrefetchScalarGridSpec(
            num_scalar_prefetch=prefetch,
            grid=grid,
            in_specs=list(ins) + [anywhere] * extra,
            out_specs=list(outs) + [anywhere] * len(through),
            scratch_shapes=scratch,
        ),
        out_shape=[jax.ShapeDtypeStruct(shape, kind) for shape, kind in shapes]
        + [jax.ShapeDtypeStruct(x.shape, x.dtype) for x in through],
        input_output_aliases=aliases,
        compiler_params=pltpu.CompilerParams(vmem_limit_bytes=VMEM_LIMIT),
        cost_estimate=pl.CostEstimate(flops=1, bytes_accessed=1, transcendentals=0),
        name=name,
    )
    return lambda *args: built(*args, *after, *through)


def whole(*shape):
    return pl.BlockSpec(shape, lambda *_: (0,) * len(shape))


def lower(n):
    return [(i, j) for i in range(n) for j in range(i + 1)]


def dense_kernel(blk, step, nnza, nnzb, width, where, acol, bcol, a_ref, b_ref, p_ref, fh, fl, uh, ul, w_ref, buf):
    i = pl.program_id(0)
    rows = p_ref.shape[0]
    buf[...] = jnp.zeros_like(buf)
    diag = lax.broadcasted_iota(jnp.int32, (blk, blk), 0) == lax.broadcasted_iota(jnp.int32, (blk, blk), 1)
    eye = jnp.where(diag, 0.75, 0.0).astype(F32)
    for t in range(step // blk):
        row = i * (step // blk) + t
        for s in range(nnza):
            col = pl.multiple_of(acol[row * nnza + s] * blk, blk)
            block = a_ref[t, s]
            if s == 0:
                block = block + eye
            buf[t * blk : (t + 1) * blk, pl.ds(col, blk)] = block
        for s in range(nnzb):
            col = pl.multiple_of(width + bcol[row * nnzb + s] * blk, blk)
            buf[t * blk : (t + 1) * blk, pl.ds(col, blk)] = b_ref[t, s]
    hi, lo = split(buf[...])
    fh[...] = hi
    fl[...] = lo
    orders = buf.shape[1] - width
    uh[:orders], ul[:orders] = split(buf[:, width:].T)
    uh[orders:], ul[orders:] = split(buf[:, pl.ds(pl.multiple_of(where[0] * rows, rows), rows)].T)
    part = dot3(split(p_ref[...]), (hi[:, width:], lo[:, width:]))

    @pl.when(i == 0)
    def _():
        w_ref[...] = part

    @pl.when(i > 0)
    def _():
        w_ref[...] += part


def dense(where, cost_rows, a_blocks, a_cols, b_blocks, b_cols, orders):
    rows, width = cost_rows.shape
    _, nnza, blk, _ = a_blocks.shape
    nnzb = b_blocks.shape[1]
    step = 2 * blk
    total = width + orders
    factor = pl.BlockSpec((step, total), lambda i, *_: (i, 0))
    turned = pl.BlockSpec((rows + orders, step), lambda i, *_: (0, i))
    return call(
        functools.partial(dense_kernel, blk, step, nnza, nnzb, width),
        (width // step,),
        3,
        [
            pl.BlockSpec((2, nnza, blk, blk), lambda i, *_: (i, 0, 0, 0)),
            pl.BlockSpec((2, nnzb, blk, blk), lambda i, *_: (i, 0, 0, 0)),
            pl.BlockSpec((rows, step), lambda i, *_: (0, i)),
        ],
        [factor, factor, turned, turned, whole(rows, orders)],
        [((width, total), BF16)] * 2 + [((rows + orders, width), BF16)] * 2 + [((rows, orders), F32)],
        "dense",
        [pltpu.VMEM((step, total), F32)],
    )(where, a_cols.reshape(-1), b_cols.reshape(-1), a_blocks, b_blocks, cost_rows)


def gram_kernel(blk, pieces, weight, where, bh, bl, ah, al, w_ref, own, *refs):
    mine, other = refs[: pieces - 1], refs[pieces - 1 : 2 * pieces - 2]
    keep, give, drift, x = refs[2 * pieces - 2 :]
    rows = own.shape[0]
    half = rows // 2
    z, core = where[0], where[1]
    x[pl.ds(pl.multiple_of(z * rows, rows), rows)] = own[...]
    for d in range(1, pieces):
        base = lax.rem(z - d + pieces, pieces) * rows
        x[pl.ds(pl.multiple_of(base + core * half, half), half)] = mine[d - 1][...]
        x[pl.ds(pl.multiple_of(base + (1 - core) * half, half), half)] = other[d - 1][...]
    w = w_ref[...]
    h = dot3((bh[...], bl[...]), split(w)) * weight[0]
    y = dot3((ah[...], al[...]), split(x[...]))
    drift[...] = y
    q = dot3(split(w.T), split(y)) * weight[0]
    tiles = [h[i * blk : (i + 1) * blk, j * blk : (j + 1) * blk] for i, j in lower(h.shape[0] // blk)]
    tiles += [q[i * blk : (i + 1) * blk] for i in range(h.shape[0] // blk)]
    count = len(tiles) // 2
    for side in range(2):

        @pl.when(core == side)
        def _():
            for t in range(count):
                keep[t] = tiles[side * count + t]
                give[t] = tiles[(1 - side) * count + t]


def gram(weight, where, fh, fl, uh, ul, w, own, mine, other, blk):
    rows, orders = w.shape
    samples = own.shape[1]
    pieces = len(mine) + 1
    width = rows * pieces
    count = orders // blk
    count = (count * (count + 1) // 2 + count) // 2
    turned = pl.BlockSpec((orders, rows), lambda i, weight, where: (0, where[0]))
    factor = pl.BlockSpec((rows, width), lambda i, weight, where: (where[0], 0))
    return call(
        functools.partial(gram_kernel, blk, pieces),
        (1,),
        2,
        [turned, turned, factor, factor, whole(rows, orders), whole(rows, samples)]
        + [whole(rows // 2, samples)] * (2 * pieces - 2),
        [whole(count, blk, samples)] * 2 + [whole(rows, samples)],
        [((count, blk, samples), F32)] * 2 + [((rows, samples), F32)],
        "gram",
        [pltpu.VMEM((width, samples), F32)],
    )(weight, where, uh, ul, fh, fl, w, own, *mine, *other)


def inverse_block(m):
    n = m.shape[0]
    sub = lax.broadcasted_iota(jnp.int32, (8, n), 0)
    lane = lax.broadcasted_iota(jnp.int32, (8, n), 1)
    strips = [m[i : i + 8] for i in range(0, n, 8)]
    for j in range(0, n, 2):
        strip, at = strips[j // 8], j % 8
        r0, r1 = strip[at : at + 1], strip[at + 1 : at + 2]
        a, b = r0[:, j : j + 1], r0[:, j + 1 : j + 2]
        c, d = r1[:, j : j + 1], r1[:, j + 1 : j + 2]
        inv_a = 1.0 / a
        f = c * inv_a
        inv_s = 1.0 / (d - f * b)
        first, second = lane == j, lane == j + 1
        r0 = jnp.where(first[:1], 1.0, jnp.where(second[:1], 0.0, r0))
        r1 = jnp.where(first[:1], 0.0, jnp.where(second[:1], 1.0, r1))
        r1 = (r1 - f * r0) * inv_s
        r0 = (r0 - b * r1) * inv_a
        both = first | second
        new = []
        for t, strip in enumerate(strips):
            part = jnp.where(both, 0.0, strip) - strip[:, j : j + 1] * r0 - strip[:, j + 1 : j + 2] * r1
            if t == j // 8:
                part = jnp.where(sub == at, r0, jnp.where(sub == at + 1, r1, part))
            new.append(part)
        strips = new
    return jnp.concatenate(strips, axis=0)


def inverse_kernel(where, mine, other, d_ref, out, u_ref, tiles):
    core = where[0]
    half, blk, _ = mine.shape
    n = out.shape[0]
    tiles[pl.ds(core * half, half)] = mine[...]
    tiles[pl.ds((1 - core) * half, half)] = other[...]
    dot = functools.partial(jnp.dot, precision=HIGHEST, preferred_element_type=F32)
    pairs = lower(n // blk)
    for t, (i, j) in enumerate(pairs):
        out[i * blk : (i + 1) * blk, j * blk : (j + 1) * blk] = tiles[t]
        if i != j:
            out[j * blk : (j + 1) * blk, i * blk : (i + 1) * blk] = tiles[t].T
    diag = lax.broadcasted_iota(jnp.int32, (n, n), 0) == lax.broadcasted_iota(jnp.int32, (n, n), 1)
    out[...] += jnp.where(diag, d_ref[...], 0.0)

    @pl.loop(0, n // blk)
    def _(b):
        here = pl.ds(pl.multiple_of(b * blk, blk), blk)
        inv = inverse_block(out[here, here])
        row = dot(inv, out[here, :])
        col = out[:, here]
        out[...] -= dot(col, row)
        out[:, here] = -dot(col, inv)
        out[here, :] = row
        out[here, here] = inv

    q = jnp.concatenate([tiles[len(pairs) + i] for i in range(n // blk)], axis=0)
    u_ref[...] = -dot(out[...], q)


def inverse(where, mine, other, control_cost, after):
    half, blk, samples = mine.shape
    n = control_cost.shape[0]
    return call(
        inverse_kernel,
        (1,),
        1,
        [whole(half, blk, samples)] * 2 + [whole(1, n)],
        [whole(n, n), whole(n, samples)],
        [((n, n), F32), ((n, samples), F32)],
        "inverse",
        [pltpu.VMEM((2 * half, blk, samples), F32)],
        after=after,
    )(where, mine, other, control_cost[None])


def pack_kernel(blk, where, d_ref, *refs):
    n = len(refs) // 2
    for t, (i, j) in enumerate(lower(d_ref.shape[0] // blk)):
        refs[n][t] = d_ref[i * blk : (i + 1) * blk, j * blk : (j + 1) * blk]
    for t in range(n):
        refs[n + 1 + t][...] = refs[t][...]


def pack(where, cost_rows, blk):
    rows = cost_rows.shape[0]
    count = len(lower(rows // blk))
    specs = [pl.BlockSpec((rows, rows), functools.partial(lambda t, i, where: (0, where[t]), t)) for t in range(4)]
    return call(
        functools.partial(pack_kernel, blk),
        (1,),
        1,
        specs,
        [whole(count, blk, blk)] + [whole(rows, rows)] * 3,
        [((count, blk, blk), F32)] + [((rows, rows), F32)] * 3,
        "pack",
    )(where, *[cost_rows] * 4)


def unpacked(tiles, n):
    blocks = [[None] * n for _ in range(n)]
    for t, (i, j) in enumerate(lower(n)):
        blocks[i][j] = tiles[t]
        if i != j:
            blocks[j][i] = tiles[t].T
    return jnp.concatenate([jnp.concatenate(row, axis=1) for row in blocks], axis=0)


def begin_kernel(where, p_ref, uh, ul, vh, vl, mine, rest):
    j = pl.program_id(0)
    p = split(p_ref[...])
    part = dot3((uh[...], ul[...]), p, NT)

    @pl.when(j == 0)
    def _():
        mine[...] = part

    @pl.when(j > 0)
    def _():
        mine[...] += part

    rest[...] = dot3((vh[...], vl[...]), p)


def begin(where, cost_rows, uh, ul, after, through):
    rows, width = cost_rows.shape
    tall = uh.shape[0]
    each = pl.BlockSpec((tall, rows), lambda j, where: (0, j))
    own = pl.BlockSpec((tall, rows), lambda j, where: (0, where[0]))
    return call(
        begin_kernel,
        (width // rows,),
        1,
        [pl.BlockSpec((rows, rows), lambda j, where: (0, j)), each, each, own, own],
        [whole(tall, rows), each],
        [((tall, rows), F32), ((tall, width), F32)],
        "begin",
        after=after,
        through=through,
    )(where, cost_rows, uh, ul, uh, ul)


def spread_kernel(where, weight, n_ref, fh, fl, s_out, g_out, hi, lo):
    @pl.when(pl.program_id(0) == 0)
    def _():
        hi[...], lo[...] = split(n_ref[...] * weight[0])

    part = dot3((hi[...], lo[...]), (fh[...], fl[...]))
    orders = g_out.shape[0]
    s_out[...] = part[orders:]
    g_out[...] = part[:orders]


def spread(where, weight, n, fh, fl, width, after, through):
    tall, rows = n.shape
    orders = tall - rows
    tile = 512
    s_spec = pl.BlockSpec((rows, tile), lambda n, *_: (0, n))
    g_spec = pl.BlockSpec((orders, tile), lambda n, *_: (0, n))
    factor = pl.BlockSpec((rows, tile), lambda n, where, _: (where[0], n))
    return call(
        spread_kernel,
        (width // tile,),
        2,
        [whole(tall, rows), factor, factor],
        [s_spec, g_spec],
        [((rows, width), F32), ((orders, width), F32)],
        "spread",
        [pltpu.VMEM((tall, rows), BF16)] * 2,
        after=after,
        through=through,
    )(where, weight, n, fh, fl)


def stage_kernel(options, size, where, weight, *refs):
    arrived = refs[: size * options]
    vh, vl, n_in, fh, fl, s_in, g_in, *refs = refs[size * options :]
    if size > 1:
        uh, ul, s_out, g_out, n_out, done, hi, lo = refs
    else:
        s_out, g_out, done, hi, lo = refs
    g = pl.program_id(0)
    for c in range(options):
        tiles, *blocks = arrived[c * size : (c + 1) * size]
        chosen = where[0] == c

        @pl.when((g == 0) & chosen)
        def _():
            whole_block = unpacked(tiles, done.shape[1] // tiles.shape[1])
            done[...] = n_in[...] + dot3((vh[...], vl[...]), split(whole_block))

        for t, block in enumerate(blocks):

            @pl.when((g == t + 1) & chosen)
            def _():
                x = split(block[...])
                done[...] += dot3((uh[...], ul[...]), x, NT)
                n_out[...] = n_in[...] + dot3((vh[...], vl[...]), x)

    @pl.when(g == size)
    def _():
        hi[...], lo[...] = split(done[...] * weight[0])

    @pl.when(g >= size)
    def _():
        part = dot3((hi[...], lo[...]), (fh[...], fl[...]))
        orders = g_out.shape[0]
        s_out[...] = s_in[...] + part[orders:]
        g_out[...] = g_in[...] + part[:orders]


def stage(where, weight, options, uh, ul, n, fh, fl, sums, after=(), through=()):
    size = len(options[0])
    count, blk, _ = options[0][0].shape
    tall, width = n.shape
    rows, orders = sums[0].shape[0], sums[1].shape[0]
    tile = 512

    def place(g, where):
        return where[1 + jnp.minimum(g, size - 1)]

    def later(g, where):
        return where[1 + jnp.clip(g, 1, size - 1)]

    def turn(g):
        return jnp.maximum(g - size, 0)

    block = pl.BlockSpec((tall, rows), lambda g, where, _: (0, place(g, where)))
    beyond = pl.BlockSpec((tall, rows), lambda g, where, _: (0, later(g, where)))
    focus = pl.BlockSpec((tall, rows), lambda g, where, _: (0, where[1]))
    factor = pl.BlockSpec((rows, tile), lambda g, where, _: (where[1], turn(g)))
    s_spec = pl.BlockSpec((rows, tile), lambda g, *_: (0, turn(g)))
    g_spec = pl.BlockSpec((orders, tile), lambda g, *_: (0, turn(g)))
    first = 2 + size * len(options)
    more = size > 1
    return call(
        functools.partial(stage_kernel, len(options), size),
        (size + width // tile,),
        2,
        ([whole(count, blk, blk)] + [whole(rows, rows)] * (size - 1)) * len(options)
        + [focus, focus, block, factor, factor, s_spec, g_spec]
        + [beyond] * (2 * more),
        [s_spec, g_spec] + [beyond] * more,
        [((rows, width), F32), ((orders, width), F32)] + [((tall, width), F32)] * more,
        "stage",
        [pltpu.VMEM((tall, rows), F32)] + [pltpu.VMEM((tall, rows), BF16)] * 2,
        {first + 5: 0, first + 6: 1, **({first + 2: 2} if more else {})},
        after,
        through,
    )(where, weight, *[x for o in options for x in o], uh, ul, n, fh, fl, *sums, *([uh, ul] if more else []))


def final_kernel(where, h_ref, g1, g2, s1, s2, q1, q2, d_ref, gain, out, hi, lo):
    n = pl.program_id(0)
    rows = out.shape[0]

    @pl.when(n == 0)
    def _():
        value = -dot3(split(h_ref[...]), split(g1[...] + g2[...]))
        gain[...] = value
        hi[...], lo[...] = split(value.T)

    part = s1[...] + s2[...] + dot3((hi[...], lo[...]), split(q1[...] + q2[...]))
    diag = lax.broadcasted_iota(jnp.int32, (rows, rows), 0) == lax.broadcasted_iota(jnp.int32, (rows, rows), 1)
    out[...] = part + jnp.where(diag & (n == where[0]), d_ref[...], 0.0)


def final(where, hinv, own, other, state_cost):
    rows, width = own[0].shape
    orders = own[1].shape[0]
    s_spec = pl.BlockSpec((rows, rows), lambda n, where: (0, n))
    g_spec = pl.BlockSpec((orders, rows), lambda n, where: (0, n))
    mine = pl.BlockSpec((orders, rows), lambda n, where: (0, where[0]))
    return call(
        final_kernel,
        (width // rows,),
        1,
        [whole(orders, orders), mine, mine, s_spec, s_spec, g_spec, g_spec, whole(1, rows)],
        [whole(orders, rows), s_spec],
        [((orders, rows), F32), ((rows, width), F32)],
        "final",
        [pltpu.VMEM((rows, orders), BF16)] * 2,
    )(where, hinv, own[1], other[1], own[0], other[0], own[1], other[1], state_cost[None])


def image_kernel(where, weight, fh, fl, p_ref, out, acc):
    k = pl.program_id(0)
    part = dot3(split(p_ref[...]), (fh[...], fl[...]))

    @pl.when(k == 0)
    def _():
        acc[...] = part

    @pl.when(k > 0)
    def _():
        acc[...] += part

    @pl.when(k == pl.num_programs(0) - 1)
    def _():
        out[...] = acc[...].T * weight[0]


def image(where, weight, fh, fl, cost_rows):
    rows, width = cost_rows.shape
    chunk = 512
    factor = pl.BlockSpec((chunk, rows), lambda k, where, _: (k, where[0]))
    return call(
        image_kernel,
        (width // chunk,),
        2,
        [factor, factor, pl.BlockSpec((rows, chunk), lambda k, *_: (0, k))],
        [whole(rows, rows)],
        [((rows, rows), F32)],
        "image",
        [pltpu.VMEM((rows, rows), F32)],
    )(where, weight, fh, fl, cost_rows)[0]


def accumulate_kernel(first, where, y_ref, fh, fl, *refs):
    out = refs[-1]
    part = dot3(split(y_ref[...]), (fh[...], fl[...]))
    out[...] = part if first else refs[0][...] + part


def accumulate(where, y, fh, fl, acc):
    rows = y.shape[0]
    total = fh.shape[1]
    tile = 512
    first = acc is None
    spec = pl.BlockSpec((rows, tile), lambda n, where: (0, n))
    factor = pl.BlockSpec((rows, tile), lambda n, where: (where[0], n))
    return call(
        functools.partial(accumulate_kernel, first),
        (total // tile,),
        1,
        [whole(rows, rows), factor, factor] + [spec] * (not first),
        [spec],
        [((rows, total), F32)],
        "accumulate",
        aliases=None if first else {4: 0},
    )(where, y, fh, fl, *(() if first else (acc,)))[0]


def by_images(z, parts, weight, cost_rows, fh, fl):
    rows, width = cost_rows.shape
    acc = None
    for d in range(parts):
        block = image(((z + d) % parts)[None], weight, fh, fl, cost_rows)
        if d:
            block = lax.ppermute(block, "row", [(i, (i + d) % parts) for i in range(parts)])
        acc = accumulate(((z - d) % parts)[None], block, fh, fl, acc)
    cross = lax.all_gather(acc[:, width:], "row")
    return acc[:, :width], jnp.swapaxes(cross.reshape(width, -1), 0, 1)


def by_blocks(z, weight, cost_rows, fh, fl, uh, ul, sent, tiles):
    width = cost_rows.shape[1]
    edge = ((z == 0) | (z == 3)).astype(jnp.int32)
    left = z < 2

    def at(i):
        return jnp.where(left, i, 3 - i)

    def moved(x, pairs):
        return lax.ppermute(x, "row", pairs)

    def to_partner(x):
        return moved(x, [(0, 1), (1, 0), (2, 3), (3, 2)])

    def across(x):
        return moved(x, [(1, 2), (2, 1)])

    def to_end(x):
        return moved(x, [(1, 0), (2, 3)])

    diag, near, inner, far = sent
    partner = [to_partner(x) for x in (diag, inner, far)]
    mid = [across(x) for x in (diag, near)]

    mine, n = begin(z[None], cost_rows, uh, ul, [], [])
    tiles = tiles[0] + swapped(tiles[1])
    tiles = tiles + to_partner(tiles)
    *sums, first, mid[0], mid[1] = spread(
        z[None], weight, mine, fh, fl, width, [tiles], [partner[0], *mid]
    )
    partner[0] = first
    mid.append(across(first))
    ends = [to_end(x) for x in mid[:2]]
    tiles = tiles + moved(tiles, [(0, 3), (1, 2), (2, 1), (3, 0)])
    where = jnp.stack([z * 0, z ^ 1, at(2), at(3)])
    *sums, n, last = stage(where, weight, [partner], uh, ul, n, fh, fl, sums, [tiles], [mid[2]])
    mid[2] = last
    ends.append(to_end(last))

    def rest(hinv):
        where = jnp.stack([edge, at(2), at(3)])
        *more, whole_n = stage(where, weight, [mid[:2], ends[:2]], uh, ul, n, fh, fl, sums, [hinv])
        where = jnp.stack([edge, at(3)])
        return stage(where, weight, [mid[2:], ends[2:]], uh, ul, whole_n, fh, fl, more)

    return tiles, sums[0], rest


def swapped(x):
    n = lax.axis_size("leaf")
    return lax.ppermute(x, "leaf", [(i, i ^ 1) for i in range(n)])


def shards(
    leaf_cost,
    a_blocks,
    a_cols,
    b_blocks,
    b_cols,
    branch_prob,
    state_cost,
    control_cost,
    parent_state,
):
    cost_rows = leaf_cost[0]
    rows, width = cost_rows.shape
    blk = a_blocks.shape[3]
    orders = control_cost.shape[0]
    parts = lax.axis_size("row")
    z = lax.axis_index("row")
    leaf = lax.axis_index("leaf")
    core = leaf % 2
    line = parts == 4 and rows == orders

    place = jnp.stack([z, core])
    if line:
        left = z < 2
        near = jnp.where(left, 0, 3)
        sent = pack(jnp.stack([z, near, jnp.where(left, 2, 1), 3 - near]), cost_rows, blk)

    own_state = lax.dynamic_index_in_dim(parent_state, leaf // 2, 0, keepdims=False)
    half_state = lax.dynamic_slice_in_dim(own_state, core * (rows // 2), rows // 2, 0)
    mine = [lax.ppermute(half_state, "row", [(i, (i + d) % parts) for i in range(parts)]) for d in range(1, parts)]
    other = [swapped(x) for x in mine]

    fh, fl, uh, ul, w = dense(z[None], cost_rows, a_blocks[0], a_cols[0], b_blocks[0], b_cols[0], orders)
    *tiles, drift = gram(branch_prob, place, fh, fl, uh, ul, w, own_state, mine, other, blk)
    if line:
        tiles, ready, rest = by_blocks(z, branch_prob, cost_rows, fh, fl, uh, ul, sent, tiles)
    else:
        tiles = lax.psum(tiles[0] + swapped(tiles[1]), "row")
        own = by_images(z, parts, branch_prob, cost_rows, fh, fl)
        ready, rest = own[0], lambda hinv: own
    hinv, order = inverse(core[None], tiles, swapped(tiles), control_cost, [ready])
    own = rest(hinv)
    other = tuple(swapped(x) for x in own)
    b_mine = [lax.dynamic_slice(f, (z * rows, width), (rows, orders)) for f in (fh, fl)]
    reached = drift + dot3(b_mine, parted(order))
    gain, pcost = final(z[None], hinv, own, other, state_cost)
    return pcost[None], gain[None], reached[None]


def solution(mesh):
    placed = (
        P("leaf", "row", None),
        P("leaf", None, None, None, None),
        P("leaf", None, None),
        P("leaf", None, None, None, None),
        P("leaf", None, None),
        P("leaf"),
        P("row"),
        P(),
        P(None, "row", None),
    )
    return jax.shard_map(
        shards,
        mesh=mesh,
        in_specs=placed,
        out_specs=(P("leaf", "row", None), P("leaf", None, "row"), P("leaf", "row", None)),
        check_vma=False,
    )
```

```python
import functools

import jax
import jax.numpy as jnp
from jax import lax
from jax.experimental import pallas as pl
from jax.experimental.pallas import tpu as pltpu
from jax.sharding import PartitionSpec as P

HIGHEST = lax.Precision.HIGHEST
F32 = jnp.float32
BF16 = jnp.bfloat16
VMEM_LIMIT = 56 * 2**20
NN = (((1,), (0,)), ((), ()))
NT = (((1,), (1,)), ((), ()))


def split(x):
    hi = x.astype(BF16)
    return hi, (x - hi.astype(F32)).astype(BF16)


def parted(x):
    hi = lax.reduce_precision(x, 8, 7)
    return hi.astype(BF16), (x - hi).astype(BF16)


def dot3(a, b, dims=NN):
    one = functools.partial(lax.dot_general, dimension_numbers=dims, preferred_element_type=F32)
    return one(a[0], b[0]) + (one(a[0], b[1]) + one(a[1], b[0]))


def call(kernel, grid, prefetch, ins, outs, shapes, name, scratch=(), aliases=None, after=(), through=()):
    n_in, n_out = len(ins), len(outs)
    extra = len(after) + len(through)
    anywhere = pl.BlockSpec(memory_space=pl.ANY)

    def body(*refs):
        start = prefetch + n_in
        stop = start + extra + n_out
        kernel(*refs[:start], *refs[start + extra : stop], *refs[stop + len(through) :])

    aliases = dict(aliases or {})
    for t in range(len(through)):
        aliases[prefetch + n_in + len(after) + t] = n_out + t
    built = pl.pallas_call(
        body,
        grid_spec=pltpu.PrefetchScalarGridSpec(
            num_scalar_prefetch=prefetch,
            grid=grid,
            in_specs=list(ins) + [anywhere] * extra,
            out_specs=list(outs) + [anywhere] * len(through),
            scratch_shapes=scratch,
        ),
        out_shape=[jax.ShapeDtypeStruct(shape, kind) for shape, kind in shapes]
        + [jax.ShapeDtypeStruct(x.shape, x.dtype) for x in through],
        input_output_aliases=aliases,
        compiler_params=pltpu.CompilerParams(vmem_limit_bytes=VMEM_LIMIT),
        cost_estimate=pl.CostEstimate(flops=1, bytes_accessed=1, transcendentals=0),
        name=name,
    )
    return lambda *args: built(*args, *after, *through)


def whole(*shape):
    return pl.BlockSpec(shape, lambda *_: (0,) * len(shape))


def lower(n):
    return [(i, j) for i in range(n) for j in range(i + 1)]


def dense_kernel(blk, step, nnza, nnzb, width, where, acol, bcol, a_ref, b_ref, p_ref, fh, fl, uh, ul, w_ref, buf):
    i = pl.program_id(0)
    rows = p_ref.shape[0]
    buf[...] = jnp.zeros_like(buf)
    diag = lax.broadcasted_iota(jnp.int32, (blk, blk), 0) == lax.broadcasted_iota(jnp.int32, (blk, blk), 1)
    eye = jnp.where(diag, 0.75, 0.0).astype(F32)
    for t in range(step // blk):
        row = i * (step // blk) + t
        for s in range(nnza):
            col = pl.multiple_of(acol[row * nnza + s] * blk, blk)
            block = a_ref[t, s]
            if s == 0:
                block = block + eye
            buf[t * blk : (t + 1) * blk, pl.ds(col, blk)] = block
        for s in range(nnzb):
            col = pl.multiple_of(width + bcol[row * nnzb + s] * blk, blk)
            buf[t * blk : (t + 1) * blk, pl.ds(col, blk)] = b_ref[t, s]
    hi, lo = split(buf[...])
    fh[...] = hi
    fl[...] = lo
    orders = buf.shape[1] - width
    uh[:orders], ul[:orders] = split(buf[:, width:].T)
    uh[orders:], ul[orders:] = split(buf[:, pl.ds(pl.multiple_of(where[0] * rows, rows), rows)].T)
    part = dot3(split(p_ref[...]), (hi[:, width:], lo[:, width:]))

    @pl.when(i == 0)
    def _():
        w_ref[...] = part

    @pl.when(i > 0)
    def _():
        w_ref[...] += part


def dense(where, cost_rows, a_blocks, a_cols, b_blocks, b_cols, orders, after):
    rows, width = cost_rows.shape
    _, nnza, blk, _ = a_blocks.shape
    nnzb = b_blocks.shape[1]
    step = 2 * blk
    total = width + orders
    factor = pl.BlockSpec((step, total), lambda i, *_: (i, 0))
    turned = pl.BlockSpec((rows + orders, step), lambda i, *_: (0, i))
    return call(
        functools.partial(dense_kernel, blk, step, nnza, nnzb, width),
        (width // step,),
        3,
        [
            pl.BlockSpec((2, nnza, blk, blk), lambda i, *_: (i, 0, 0, 0)),
            pl.BlockSpec((2, nnzb, blk, blk), lambda i, *_: (i, 0, 0, 0)),
            pl.BlockSpec((rows, step), lambda i, *_: (0, i)),
        ],
        [factor, factor, turned, turned, whole(rows, orders)],
        [((width, total), BF16)] * 2 + [((rows + orders, width), BF16)] * 2 + [((rows, orders), F32)],
        "dense",
        [pltpu.VMEM((step, total), F32)],
        after=after,
    )(where, a_cols.reshape(-1), b_cols.reshape(-1), a_blocks, b_blocks, cost_rows)


def gram_kernel(blk, pieces, weight, where, bh, bl, ah, al, w_ref, own, *refs):
    keep, give, drift, x = refs[pieces - 1 :]
    rows = own.shape[0]
    z, core = where[0], where[1]
    x[pl.ds(pl.multiple_of(z * rows, rows), rows)] = own[...]
    for d in range(1, pieces):
        base = lax.rem(z - d + pieces, pieces) * rows
        x[pl.ds(pl.multiple_of(base, rows), rows)] = refs[d - 1][...]
    w = w_ref[...]
    h = dot3((bh[...], bl[...]), split(w)) * weight[0]
    y = dot3((ah[...], al[...]), split(x[...]))
    drift[...] = y
    q = dot3(split(w.T), split(y)) * weight[0]
    tiles = [h[i * blk : (i + 1) * blk, j * blk : (j + 1) * blk] for i, j in lower(h.shape[0] // blk)]
    tiles += [q[i * blk : (i + 1) * blk] for i in range(h.shape[0] // blk)]
    count = len(tiles) // 2
    for side in range(2):

        @pl.when(core == side)
        def _():
            for t in range(count):
                keep[t] = tiles[side * count + t]
                give[t] = tiles[(1 - side) * count + t]


def gram(weight, where, fh, fl, uh, ul, w, own, other, blk):
    rows, orders = w.shape
    samples = own.shape[1]
    pieces = len(other) + 1
    width = rows * pieces
    count = orders // blk
    count = (count * (count + 1) // 2 + count) // 2
    turned = pl.BlockSpec((orders, rows), lambda i, weight, where: (0, where[0]))
    factor = pl.BlockSpec((rows, width), lambda i, weight, where: (where[0], 0))
    return call(
        functools.partial(gram_kernel, blk, pieces),
        (1,),
        2,
        [turned, turned, factor, factor, whole(rows, orders)] + [whole(rows, samples)] * pieces,
        [whole(count, blk, samples)] * 2 + [whole(rows, samples)],
        [((count, blk, samples), F32)] * 2 + [((rows, samples), F32)],
        "gram",
        [pltpu.VMEM((width, samples), F32)],
    )(weight, where, uh, ul, fh, fl, w, own, *other)


def inverse_block(m):
    n = m.shape[0]
    sub = lax.broadcasted_iota(jnp.int32, (8, n), 0)
    lane = lax.broadcasted_iota(jnp.int32, (8, n), 1)
    strips = [m[i : i + 8] for i in range(0, n, 8)]

    def along(v, j):
        return jnp.broadcast_to(v[:, j : j + 1], (8, n))

    def down(v, t):
        return jnp.broadcast_to(v[t : t + 1], (8, n))

    for q in range(n // 8):
        panel = strips[q]
        cols = [along(panel, 8 * q + b) for b in range(8)]
        for t in range(8):
            here = sub == t
            inv = 1.0 / down(cols[t], t)

            def reduced(v):
                r = down(v, t) * inv
                return jnp.where(here, r, v - cols[t] * r)

            panel = reduced(jnp.where(lane == 8 * q + t, jnp.where(here, 1.0, 0.0), panel))
            cols[t + 1 :] = [reduced(v) for v in cols[t + 1 :]]
        inside = (lane >= 8 * q) & (lane < 8 * q + 8)
        rows = [down(panel, b) for b in range(8)]
        for i in range(q + 1, q + n // 8):
            old = strips[i % (n // 8)]
            terms = [along(old, 8 * q + b) * rows[b] for b in range(8)]
            while len(terms) > 1:
                terms = [x + y for x, y in zip(terms[::2], terms[1::2])]
            strips[i % (n // 8)] = jnp.where(inside, 0.0, old) - terms[0]
        strips[q] = panel
    return jnp.concatenate(strips, axis=0)


def inverse_kernel(where, mine, other, d_ref, out, u_ref, tiles):
    core = where[0]
    half, blk, _ = mine.shape
    n = out.shape[0]
    tiles[pl.ds(core * half, half)] = mine[...]
    tiles[pl.ds((1 - core) * half, half)] = other[...]
    dot = functools.partial(jnp.dot, precision=HIGHEST, preferred_element_type=F32)
    pairs = lower(n // blk)
    for t, (i, j) in enumerate(pairs):
        out[i * blk : (i + 1) * blk, j * blk : (j + 1) * blk] = tiles[t]
        if i != j:
            out[j * blk : (j + 1) * blk, i * blk : (i + 1) * blk] = tiles[t].T
    diag = lax.broadcasted_iota(jnp.int32, (n, n), 0) == lax.broadcasted_iota(jnp.int32, (n, n), 1)
    out[...] += jnp.where(diag, d_ref[...], 0.0)

    @pl.loop(0, n // blk)
    def _(b):
        here = pl.ds(pl.multiple_of(b * blk, blk), blk)
        inv = inverse_block(out[here, here])
        row = dot(inv, out[here, :])
        col = out[:, here]
        out[...] -= dot(col, row)
        out[:, here] = -dot(col, inv)
        out[here, :] = row
        out[here, here] = inv

    q = jnp.concatenate([tiles[len(pairs) + i] for i in range(n // blk)], axis=0)
    u_ref[...] = -dot(out[...], q)


def inverse(where, mine, other, control_cost, after):
    half, blk, samples = mine.shape
    n = control_cost.shape[0]
    return call(
        inverse_kernel,
        (1,),
        1,
        [whole(half, blk, samples)] * 2 + [whole(1, n)],
        [whole(n, n), whole(n, samples)],
        [((n, n), F32), ((n, samples), F32)],
        "inverse",
        [pltpu.VMEM((2 * half, blk, samples), F32)],
        after=after,
    )(where, mine, other, control_cost[None])


def tiled(block, blk):
    n = block.shape[0] // blk
    return [block[i * blk : (i + 1) * blk, j * blk : (j + 1) * blk] for i in range(n) for j in range(n)]


def pack_kernel(blk, where, own, near, inner, far, diag_out, pair_out, mid_out):
    for t, (i, j) in enumerate(lower(own.shape[0] // blk)):
        tile = own[i * blk : (i + 1) * blk, j * blk : (j + 1) * blk]
        diag_out[t] = tile
        mid_out[t] = tile
    count = diag_out.shape[0]
    for t, tile in enumerate(tiled(near, blk)):
        mid_out[count + t] = tile
    for t, tile in enumerate(tiled(inner, blk) + tiled(far, blk)):
        pair_out[t] = tile


def pack(where, cost_rows, blk):
    rows = cost_rows.shape[0]
    count, full = len(lower(rows // blk)), (rows // blk) ** 2
    specs = [pl.BlockSpec((rows, rows), functools.partial(lambda t, i, where: (0, where[t]), t)) for t in range(4)]
    sizes = [count, 2 * full, count + full]
    return call(
        functools.partial(pack_kernel, blk),
        (1,),
        1,
        specs,
        [whole(size, blk, blk) for size in sizes],
        [((size, blk, blk), F32) for size in sizes],
        "pack",
    )(where, *[cost_rows] * 4)


def unpack(tiles, step, n, xh, xl):
    blk = tiles.shape[1]
    for t, (i, j) in enumerate(lower(n) if step == 0 else [(i, j) for i in range(n) for j in range(n)]):
        tile = tiles[t if step == 0 else len(lower(n)) + (step - 1) * n * n + t]
        places = [(i, j, tile)] + ([(j, i, tile.T)] if step == 0 and i != j else [])
        for r, c, value in places:
            at = slice(r * blk, (r + 1) * blk), slice(c * blk, (c + 1) * blk)
            xh[at], xl[at] = split(value)


def begin_kernel(where, p_ref, uh, ul, vh, vl, mine, rest):
    j = pl.program_id(0)
    p = split(p_ref[...])
    part = dot3((uh[...], ul[...]), p, NT)

    @pl.when(j == 0)
    def _():
        mine[...] = part

    @pl.when(j > 0)
    def _():
        mine[...] += part

    rest[...] = dot3((vh[...], vl[...]), p)


def begin(where, cost_rows, uh, ul, after, through):
    rows, width = cost_rows.shape
    tall = uh.shape[0]
    each = pl.BlockSpec((tall, rows), lambda j, where: (0, j))
    own = pl.BlockSpec((tall, rows), lambda j, where: (0, where[0]))
    return call(
        begin_kernel,
        (width // rows,),
        1,
        [pl.BlockSpec((rows, rows), lambda j, where: (0, j)), each, each, own, own],
        [whole(tall, rows), each],
        [((tall, rows), F32), ((tall, width), F32)],
        "begin",
        after=after,
        through=through,
    )(where, cost_rows, uh, ul, uh, ul)


def spread_kernel(where, weight, n_ref, fh, fl, s_out, g_out, hi, lo):
    @pl.when(pl.program_id(0) == 0)
    def _():
        hi[...], lo[...] = split(n_ref[...] * weight[0])

    part = dot3((hi[...], lo[...]), (fh[...], fl[...]))
    orders = g_out.shape[0]
    s_out[...] = part[orders:]
    g_out[...] = part[:orders]


def spread(where, weight, n, fh, fl, width, after, through):
    tall, rows = n.shape
    orders = tall - rows
    tile = 512
    s_spec = pl.BlockSpec((rows, tile), lambda n, *_: (0, n))
    g_spec = pl.BlockSpec((orders, tile), lambda n, *_: (0, n))
    factor = pl.BlockSpec((rows, tile), lambda n, where, _: (where[0], n))
    return call(
        spread_kernel,
        (width // tile,),
        2,
        [whole(tall, rows), factor, factor],
        [s_spec, g_spec],
        [((rows, width), F32), ((orders, width), F32)],
        "spread",
        [pltpu.VMEM((tall, rows), BF16)] * 2,
        after=after,
        through=through,
    )(where, weight, n, fh, fl)


def stage_kernel(sources, options, size, where, weight, *refs):
    arrived = refs[: sources * options]
    vh, vl, n_in, fh, fl, s_in, g_in, *refs = refs[sources * options :]
    if size > 1:
        uh, ul, s_out, g_out, n_out, done, hi, lo, xh, xl = refs
    else:
        s_out, g_out, done, hi, lo, xh, xl = refs
    g = pl.program_id(0)
    n = xh.shape[0] // arrived[0].shape[1]
    for c in range(options):
        for t in range(size):

            @pl.when((g == t) & (where[0] == c))
            def _():
                if sources == 2 and t > 0:
                    rest = arrived[2 * c + 1]
                    for k in range(n * n):
                        at = slice(k // n * rest.shape[1], (k // n + 1) * rest.shape[1])
                        to = slice(k % n * rest.shape[2], (k % n + 1) * rest.shape[2])
                        xh[at, to], xl[at, to] = split(rest[(t - 1) * n * n + k])
                else:
                    unpack(arrived[sources * c], t, n, xh, xl)

    @pl.when(g == 0)
    def _():
        done[...] = n_in[...] + dot3((vh[...], vl[...]), (xh[...], xl[...]))

    if size > 1:

        @pl.when((g > 0) & (g < size))
        def _():
            x = xh[...], xl[...]
            done[...] += dot3((uh[...], ul[...]), x, NT)
            n_out[...] = n_in[...] + dot3((vh[...], vl[...]), x)

    @pl.when(g == size)
    def _():
        hi[...], lo[...] = split(done[...] * weight[0])

    @pl.when(g >= size)
    def _():
        part = dot3((hi[...], lo[...]), (fh[...], fl[...]))
        orders = g_out.shape[0]
        s_out[...] = s_in[...] + part[orders:]
        g_out[...] = g_in[...] + part[:orders]


def stage(where, weight, options, size, uh, ul, n, fh, fl, sums, after=(), through=()):
    tall, width = n.shape
    rows, orders = sums[0].shape[0], sums[1].shape[0]
    sources = len(options[0])
    tile = 512

    def place(g, where):
        return where[1 + jnp.minimum(g, size - 1)]

    def later(g, where):
        return where[1 + jnp.clip(g, 1, size - 1)]

    def turn(g):
        return jnp.maximum(g - size, 0)

    block = pl.BlockSpec((tall, rows), lambda g, where, _: (0, place(g, where)))
    beyond = pl.BlockSpec((tall, rows), lambda g, where, _: (0, later(g, where)))
    focus = pl.BlockSpec((tall, rows), lambda g, where, _: (0, where[1]))
    factor = pl.BlockSpec((rows, tile), lambda g, where, _: (where[1], turn(g)))
    s_spec = pl.BlockSpec((rows, tile), lambda g, *_: (0, turn(g)))
    g_spec = pl.BlockSpec((orders, tile), lambda g, *_: (0, turn(g)))
    arrived = [x for o in options for x in o]
    first = 2 + len(arrived)
    more = size > 1
    return call(
        functools.partial(stage_kernel, sources, len(options), size),
        (size + width // tile,),
        2,
        [whole(*x.shape) for x in arrived]
        + [focus, focus, block, factor, factor, s_spec, g_spec]
        + [beyond] * (2 * more),
        [s_spec, g_spec] + [beyond] * more,
        [((rows, width), F32), ((orders, width), F32)] + [((tall, width), F32)] * more,
        "stage",
        [pltpu.VMEM((tall, rows), F32)] + [pltpu.VMEM((tall, rows), BF16)] * 2 + [pltpu.VMEM((rows, rows), BF16)] * 2,
        {first + 5: 0, first + 6: 1, **({first + 2: 2} if more else {})},
        after,
        through,
    )(where, weight, *arrived, uh, ul, n, fh, fl, *sums, *([uh, ul] if more else []))


def final_kernel(where, h_ref, g1, g2, s1, s2, q1, q2, d_ref, gain, out, hi, lo):
    n = pl.program_id(0)
    rows = out.shape[0]

    @pl.when(n == 0)
    def _():
        value = -dot3(split(h_ref[...]), split(g1[...] + g2[...]))
        gain[...] = value
        hi[...], lo[...] = split(value.T)

    part = s1[...] + s2[...] + dot3((hi[...], lo[...]), split(q1[...] + q2[...]))
    diag = lax.broadcasted_iota(jnp.int32, (rows, rows), 0) == lax.broadcasted_iota(jnp.int32, (rows, rows), 1)
    out[...] = part + jnp.where(diag & (n == where[0]), d_ref[...], 0.0)


def final(where, hinv, own, other, state_cost):
    rows, width = own[0].shape
    orders = own[1].shape[0]
    s_spec = pl.BlockSpec((rows, rows), lambda n, where: (0, n))
    g_spec = pl.BlockSpec((orders, rows), lambda n, where: (0, n))
    mine = pl.BlockSpec((orders, rows), lambda n, where: (0, where[0]))
    return call(
        final_kernel,
        (width // rows,),
        1,
        [whole(orders, orders), mine, mine, s_spec, s_spec, g_spec, g_spec, whole(1, rows)],
        [whole(orders, rows), s_spec],
        [((orders, rows), F32), ((rows, width), F32)],
        "final",
        [pltpu.VMEM((rows, orders), BF16)] * 2,
    )(where, hinv, own[1], other[1], own[0], other[0], own[1], other[1], state_cost[None])


def image_kernel(where, weight, fh, fl, p_ref, out, acc):
    k = pl.program_id(0)
    part = dot3(split(p_ref[...]), (fh[...], fl[...]))

    @pl.when(k == 0)
    def _():
        acc[...] = part

    @pl.when(k > 0)
    def _():
        acc[...] += part

    @pl.when(k == pl.num_programs(0) - 1)
    def _():
        out[...] = acc[...].T * weight[0]


def image(where, weight, fh, fl, cost_rows):
    rows, width = cost_rows.shape
    chunk = 512
    factor = pl.BlockSpec((chunk, rows), lambda k, where, _: (k, where[0]))
    return call(
        image_kernel,
        (width // chunk,),
        2,
        [factor, factor, pl.BlockSpec((rows, chunk), lambda k, *_: (0, k))],
        [whole(rows, rows)],
        [((rows, rows), F32)],
        "image",
        [pltpu.VMEM((rows, rows), F32)],
    )(where, weight, fh, fl, cost_rows)[0]


def accumulate_kernel(first, where, y_ref, fh, fl, *refs):
    out = refs[-1]
    part = dot3(split(y_ref[...]), (fh[...], fl[...]))
    out[...] = part if first else refs[0][...] + part


def accumulate(where, y, fh, fl, acc):
    rows = y.shape[0]
    total = fh.shape[1]
    tile = 512
    first = acc is None
    spec = pl.BlockSpec((rows, tile), lambda n, where: (0, n))
    factor = pl.BlockSpec((rows, tile), lambda n, where: (where[0], n))
    return call(
        functools.partial(accumulate_kernel, first),
        (total // tile,),
        1,
        [whole(rows, rows), factor, factor] + [spec] * (not first),
        [spec],
        [((rows, total), F32)],
        "accumulate",
        aliases=None if first else {4: 0},
    )(where, y, fh, fl, *(() if first else (acc,)))[0]


def by_images(z, parts, weight, cost_rows, fh, fl):
    rows, width = cost_rows.shape
    acc = None
    for d in range(parts):
        block = image(((z + d) % parts)[None], weight, fh, fl, cost_rows)
        if d:
            block = lax.ppermute(block, "row", [(i, (i + d) % parts) for i in range(parts)])
        acc = accumulate(((z - d) % parts)[None], block, fh, fl, acc)
    cross = lax.all_gather(acc[:, width:], "row")
    return acc[:, :width], jnp.swapaxes(cross.reshape(width, -1), 0, 1)


def by_blocks(z, weight, cost_rows, fh, fl, uh, ul, sent, tiles):
    width = cost_rows.shape[1]
    edge = ((z == 0) | (z == 3)).astype(jnp.int32)
    left = z < 2

    def at(i):
        return jnp.where(left, i, 3 - i)

    def moved(x, pairs):
        return lax.ppermute(x, "row", pairs)

    def to_partner(x):
        return moved(x, [(0, 1), (1, 0), (2, 3), (3, 2)])

    def across(x):
        return moved(x, [(1, 2), (2, 1)])

    def to_end(x):
        return moved(x, [(1, 0), (2, 3)])

    diag, pair, inward = sent
    diag, pair, mid = to_partner(diag), to_partner(pair), across(inward)
    tiles = tiles[0] + swapped(tiles[1])
    mine, n = begin(z[None], cost_rows, uh, ul, [tiles], [])
    tiles = tiles + to_partner(tiles)
    *sums, diag, mid = spread(z[None], weight, mine, fh, fl, width, [tiles], [diag, mid])
    mid_last, end = across(diag), to_end(mid)
    tiles = tiles + moved(tiles, [(0, 3), (1, 2), (2, 1), (3, 0)])
    where = jnp.stack([z * 0, z ^ 1, at(2), at(3)])
    *sums, n, mid_last = stage(
        where, weight, [[diag, pair]], 3, uh, ul, n, fh, fl, sums, [tiles], [mid_last]
    )
    end_last = to_end(mid_last)

    def rest(hinv):
        where = jnp.stack([edge, at(2), at(3)])
        *more, whole_n = stage(where, weight, [[mid], [end]], 2, uh, ul, n, fh, fl, sums, [hinv])
        where = jnp.stack([edge, at(3)])
        return stage(where, weight, [[mid_last], [end_last]], 1, uh, ul, whole_n, fh, fl, more)

    return tiles, sums[0], rest


def swapped(x):
    n = lax.axis_size("leaf")
    return lax.ppermute(x, "leaf", [(i, i ^ 1) for i in range(n)])


def shards(
    leaf_cost,
    a_blocks,
    a_cols,
    b_blocks,
    b_cols,
    branch_prob,
    state_cost,
    control_cost,
    parent_state,
):
    cost_rows = leaf_cost[0]
    rows, width = cost_rows.shape
    blk = a_blocks.shape[3]
    orders = control_cost.shape[0]
    parts = lax.axis_size("row")
    z = lax.axis_index("row")
    leaf = lax.axis_index("leaf")
    core = leaf % 2
    line = parts == 4 and rows == orders

    place = jnp.stack([z, core])
    sent = []
    if line:
        left = z < 2
        near = jnp.where(left, 0, 3)
        sent = pack(jnp.stack([z, near, jnp.where(left, 2, 1), 3 - near]), cost_rows, blk)

    own_state = lax.dynamic_index_in_dim(parent_state, leaf // 2, 0, keepdims=False)
    other = [lax.ppermute(own_state, "row", [(i, (i + d) % parts) for i in range(parts)]) for d in range(1, parts)]

    fh, fl, uh, ul, w = dense(z[None], cost_rows, a_blocks[0], a_cols[0], b_blocks[0], b_cols[0], orders, sent)
    *tiles, drift = gram(branch_prob, place, fh, fl, uh, ul, w, own_state, other, blk)
    if line:
        tiles, ready, rest = by_blocks(z, branch_prob, cost_rows, fh, fl, uh, ul, sent, tiles)
    else:
        tiles = lax.psum(tiles[0] + swapped(tiles[1]), "row")
        own = by_images(z, parts, branch_prob, cost_rows, fh, fl)
        ready, rest = own[0], lambda hinv: own
    hinv, order = inverse(core[None], tiles, swapped(tiles), control_cost, [ready])
    own = rest(hinv)
    other = tuple(swapped(x) for x in own)
    b_mine = [lax.dynamic_slice(f, (z * rows, width), (rows, orders)) for f in (fh, fl)]
    reached = drift + dot3(b_mine, parted(order))
    gain, pcost = final(z[None], hinv, own, other, state_cost)
    return pcost[None], gain[None], reached[None]


def solution(mesh):
    placed = (
        P("leaf", "row", None),
        P("leaf", None, None, None, None),
        P("leaf", None, None),
        P("leaf", None, None, None, None),
        P("leaf", None, None),
        P("leaf"),
        P("row"),
        P(),
        P(None, "row", None),
    )
    return jax.shard_map(
        shards,
        mesh=mesh,
        in_specs=placed,
        out_specs=(P("leaf", "row", None), P("leaf", None, "row"), P("leaf", "row", None)),
        check_vma=False,
    )
```

```python
import functools

import jax
import jax.numpy as jnp
from jax import lax
from jax.experimental import pallas as pl
from jax.experimental.pallas import tpu as pltpu
from jax.sharding import PartitionSpec as P

HIGHEST = lax.Precision.HIGHEST
F32 = jnp.float32
BF16 = jnp.bfloat16
VMEM_LIMIT = 56 * 2**20
NN = (((1,), (0,)), ((), ()))
NT = (((1,), (1,)), ((), ()))


def split(x):
    hi = x.astype(BF16)
    return hi, (x - hi.astype(F32)).astype(BF16)


def parted(x):
    hi = lax.reduce_precision(x, 8, 7)
    return hi.astype(BF16), (x - hi).astype(BF16)


def dot3(a, b, dims=NN):
    one = functools.partial(lax.dot_general, dimension_numbers=dims, preferred_element_type=F32)
    return one(a[0], b[0]) + (one(a[0], b[1]) + one(a[1], b[0]))


def call(kernel, grid, prefetch, ins, outs, shapes, name, scratch=(), aliases=None, after=(), through=()):
    n_in, n_out = len(ins), len(outs)
    extra = len(after) + len(through)
    anywhere = pl.BlockSpec(memory_space=pl.ANY)

    def body(*refs):
        start = prefetch + n_in
        stop = start + extra + n_out
        kernel(*refs[:start], *refs[start + extra : stop], *refs[stop + len(through) :])

    aliases = dict(aliases or {})
    for t in range(len(through)):
        aliases[prefetch + n_in + len(after) + t] = n_out + t
    built = pl.pallas_call(
        body,
        grid_spec=pltpu.PrefetchScalarGridSpec(
            num_scalar_prefetch=prefetch,
            grid=grid,
            in_specs=list(ins) + [anywhere] * extra,
            out_specs=list(outs) + [anywhere] * len(through),
            scratch_shapes=scratch,
        ),
        out_shape=[jax.ShapeDtypeStruct(shape, kind) for shape, kind in shapes]
        + [jax.ShapeDtypeStruct(x.shape, x.dtype) for x in through],
        input_output_aliases=aliases,
        compiler_params=pltpu.CompilerParams(vmem_limit_bytes=VMEM_LIMIT),
        cost_estimate=pl.CostEstimate(flops=1, bytes_accessed=1, transcendentals=0),
        name=name,
    )
    return lambda *args: built(*args, *after, *through)


def whole(*shape):
    return pl.BlockSpec(shape, lambda *_: (0,) * len(shape))


def lower(n):
    return [(i, j) for i in range(n) for j in range(i + 1)]


def dense_kernel(blk, step, width, where, acol, bcol, a_ref, b_ref, p_ref, fh, fl, uh, ul, w_ref, buf, turned):
    i = pl.program_id(0)
    rows = p_ref.shape[0]
    orders = buf.shape[1] - width
    buf[...] = jnp.zeros_like(buf)
    turned[...] = jnp.zeros_like(turned)
    diag = lax.broadcasted_iota(jnp.int32, (blk, blk), 0) == lax.broadcasted_iota(jnp.int32, (blk, blk), 1)
    eye = jnp.where(diag, 0.75, 0.0).astype(F32)
    for t in range(step // blk):
        row = i * (step // blk) + t
        at = slice(t * blk, (t + 1) * blk)
        for s in range(a_ref.shape[1]):
            col = acol[0, row, s]
            block = a_ref[t, s] + eye if s == 0 else a_ref[t, s]
            buf[at, pl.ds(pl.multiple_of(col * blk, blk), blk)] = block
            local = col - where[0] * (rows // blk)

            @pl.when((local >= 0) & (local < rows // blk))
            def _():
                turned[pl.ds(pl.multiple_of(orders + local * blk, blk), blk), at] = block.T

        for s in range(b_ref.shape[1]):
            col = bcol[0, row, s]
            buf[at, pl.ds(pl.multiple_of(width + col * blk, blk), blk)] = b_ref[t, s]
            turned[pl.ds(pl.multiple_of(col * blk, blk), blk), at] = b_ref[t, s].T
    hi, lo = split(buf[...])
    fh[...] = hi
    fl[...] = lo
    uh[...], ul[...] = split(turned[...])
    part = dot3(split(p_ref[...]), (hi[:, width:], lo[:, width:]))

    @pl.when(i == 0)
    def _():
        w_ref[...] = part

    @pl.when(i > 0)
    def _():
        w_ref[...] += part


def dense(where, cost_rows, a_blocks, a_cols, b_blocks, b_cols, orders, after):
    rows, width = cost_rows.shape
    _, nnza, blk, _ = a_blocks.shape
    nnzb = b_blocks.shape[1]
    step = 2 * blk
    total = width + orders
    factor = pl.BlockSpec((step, total), lambda i, *_: (i, 0))
    turned = pl.BlockSpec((rows + orders, step), lambda i, *_: (0, i))
    return call(
        functools.partial(dense_kernel, blk, step, width),
        (width // step,),
        3,
        [
            pl.BlockSpec((2, nnza, blk, blk), lambda i, *_: (i, 0, 0, 0)),
            pl.BlockSpec((2, nnzb, blk, blk), lambda i, *_: (i, 0, 0, 0)),
            pl.BlockSpec((rows, step), lambda i, *_: (0, i)),
        ],
        [factor, factor, turned, turned, whole(rows, orders)],
        [((width, total), BF16)] * 2 + [((rows + orders, width), BF16)] * 2 + [((rows, orders), F32)],
        "dense",
        [pltpu.VMEM((step, total), F32), pltpu.VMEM((rows + orders, step), F32)],
        after=after,
    )(where, a_cols, b_cols, a_blocks, b_blocks, cost_rows)


def gram_kernel(blk, weight, where, bh, bl, w_ref, keep, give):
    core = where[1]
    h = dot3((bh[...], bl[...]), split(w_ref[...])) * weight[0]
    tiles = [h[i * blk : (i + 1) * blk, j * blk : (j + 1) * blk] for i, j in lower(h.shape[0] // blk)]
    count = len(tiles) // 2
    for side in range(2):

        @pl.when(core == side)
        def _():
            for t in range(count):
                keep[t] = tiles[side * count + t]
                give[t] = tiles[(1 - side) * count + t]


def gram(weight, where, uh, ul, w, blk, through):
    rows, orders = w.shape
    count = len(lower(orders // blk)) // 2
    turned = pl.BlockSpec((orders, rows), lambda i, weight, where: (0, where[0]))
    return call(
        functools.partial(gram_kernel, blk),
        (1,),
        2,
        [turned, turned, whole(rows, orders)],
        [whole(count, blk, blk)] * 2,
        [((count, blk, blk), F32)] * 2,
        "gram",
        through=through,
    )(weight, where, uh, ul, w)


def inverse_block(m):
    n = m.shape[0]
    sub = lax.broadcasted_iota(jnp.int32, (8, n), 0)
    lane = lax.broadcasted_iota(jnp.int32, (8, n), 1)
    strips = [m[i : i + 8] for i in range(0, n, 8)]

    def along(v, j):
        return jnp.broadcast_to(v[:, j : j + 1], (8, n))

    def down(v, t):
        return jnp.broadcast_to(v[t : t + 1], (8, n))

    for q in range(n // 8):
        panel = strips[q]
        cols = [along(panel, 8 * q + b) for b in range(8)]
        for t in range(8):
            here = sub == t
            inv = 1.0 / down(cols[t], t)

            def reduced(v):
                r = down(v, t) * inv
                return jnp.where(here, r, v - cols[t] * r)

            panel = reduced(jnp.where(lane == 8 * q + t, jnp.where(here, 1.0, 0.0), panel))
            cols[t + 1 :] = [reduced(v) for v in cols[t + 1 :]]
        inside = (lane >= 8 * q) & (lane < 8 * q + 8)
        rows = [down(panel, b) for b in range(8)]
        for i in range(q + 1, q + n // 8):
            old = strips[i % (n // 8)]
            terms = [along(old, 8 * q + b) * rows[b] for b in range(8)]
            while len(terms) > 1:
                terms = [x + y for x, y in zip(terms[::2], terms[1::2])]
            strips[i % (n // 8)] = jnp.where(inside, 0.0, old) - terms[0]
        strips[q] = panel
    return jnp.concatenate(strips, axis=0)


def inverse_kernel(where, mine, other, d_ref, out):
    half, blk, _ = mine.shape
    n = out.shape[0]
    dot = functools.partial(jnp.dot, precision=HIGHEST, preferred_element_type=F32)
    for side in range(2):

        @pl.when(where[0] == side)
        def _():
            for t, (i, j) in enumerate(lower(n // blk)):
                tile = (mine if t // half == side else other)[t % half]
                out[i * blk : (i + 1) * blk, j * blk : (j + 1) * blk] = tile
                if i != j:
                    out[j * blk : (j + 1) * blk, i * blk : (i + 1) * blk] = tile.T

    diag = lax.broadcasted_iota(jnp.int32, (n, n), 0) == lax.broadcasted_iota(jnp.int32, (n, n), 1)
    out[...] += jnp.where(diag, d_ref[...], 0.0)

    @pl.loop(0, n // blk)
    def _(b):
        here = pl.ds(pl.multiple_of(b * blk, blk), blk)
        inv = inverse_block(out[here, here])
        row = dot(inv, out[here, :])
        col = out[:, here]
        out[...] -= dot(col, row)
        out[:, here] = -dot(col, inv)
        out[here, :] = row
        out[here, here] = inv


def inverse(where, mine, other, control_cost, after):
    half, blk, _ = mine.shape
    n = control_cost.shape[0]
    return call(
        inverse_kernel,
        (1,),
        1,
        [whole(half, blk, blk)] * 2 + [whole(1, n)],
        [whole(n, n)],
        [((n, n), F32)],
        "inverse",
        after=after,
    )(where, mine, other, control_cost[None])[0]


def tiled(block, blk):
    n = block.shape[0] // blk
    return [block[i * blk : (i + 1) * blk, j * blk : (j + 1) * blk] for i in range(n) for j in range(n)]


def pack_kernel(blk, where, own, near, inner, far, x_ref, pair_out, mid_out):
    diag = [own[i * blk : (i + 1) * blk, j * blk : (j + 1) * blk] for i, j in lower(own.shape[0] // blk)]
    x = [x_ref[0, :blk], x_ref[0, blk:]]
    for t, tile in enumerate(diag + x + tiled(inner, blk) + tiled(far, blk)):
        pair_out[t] = tile
    for t, tile in enumerate(diag + x + tiled(near, blk)):
        mid_out[t] = tile


def pack(where, cost_rows, parent_state, blk):
    rows = cost_rows.shape[0]
    samples = parent_state.shape[2]
    count, full = len(lower(rows // blk)) + 2, (rows // blk) ** 2
    specs = [pl.BlockSpec((rows, rows), functools.partial(lambda t, i, where: (0, where[t]), t)) for t in range(4)]
    specs.append(pl.BlockSpec((1, rows // 2, samples), lambda i, where: (where[4], where[5], 0)))
    sizes = [count + 2 * full, count + full]
    return call(
        functools.partial(pack_kernel, blk),
        (1,),
        1,
        specs,
        [whole(size, blk, blk) for size in sizes],
        [((size, blk, blk), F32) for size in sizes],
        "pack",
    )(where, *[cost_rows] * 4, parent_state)


def unpack(tiles, step, n, xh, xl):
    blk = tiles.shape[1]
    lead = len(lower(n))
    for t, (i, j) in enumerate(lower(n) if step == 0 else [(i, j) for i in range(n) for j in range(n)]):
        tile = tiles[t if step == 0 else lead + 2 + (step - 1) * n * n + t]
        places = [(i, j, tile)] + ([(j, i, tile.T)] if step == 0 and i != j else [])
        for r, c, value in places:
            at = slice(r * blk, (r + 1) * blk), slice(c * blk, (c + 1) * blk)
            xh[at], xl[at] = split(value)


def collect_kernel(where, pair, mid, end, mid_last, end_last, out):
    out[:2] = pair[...]

    @pl.when(where[0] == 1)
    def _():
        out[2:4] = end[...]
        out[4:6] = end_last[...]

    @pl.when(where[0] == 0)
    def _():
        out[2:4] = mid[...]
        out[4:6] = mid_last[...]


def collect(where, messages):
    blk = messages[0].shape[1]
    lead = messages[3].shape[0] // 2 - 1
    return call(
        collect_kernel,
        (1,),
        1,
        [pl.BlockSpec((2, blk, blk), lambda i, where: (lead, 0, 0))] * 5,
        [whole(6, blk, blk)],
        [((6, blk, blk), F32)],
        "collect",
    )(where, *messages)[0]


def drift_kernel(where, own, mine, other, fh, fl, x_ref, out):
    blk = mine.shape[1]
    rows = own.shape[1]
    core = where[0]
    x_ref[pl.ds(pl.multiple_of(where[1] * rows, rows), rows)] = own[0]
    for d in range(3):
        for t in range(2):
            base = where[2 + d] * rows + t * blk
            half = rows // 2
            x_ref[pl.ds(pl.multiple_of(base + core * half, blk), blk)] = mine[2 * d + t]
            x_ref[pl.ds(pl.multiple_of(base + (1 - core) * half, blk), blk)] = other[2 * d + t]
    out[...] = dot3((fh[...], fl[...]), split(x_ref[...]))


def drift(where, parent_state, mine, other, fh, fl):
    _, rows, samples = parent_state.shape
    count, blk, _ = mine.shape
    width = rows * 4
    factor = pl.BlockSpec((rows, width), lambda i, where: (where[1], 0))
    return call(
        drift_kernel,
        (1,),
        1,
        [pl.BlockSpec((1, rows, samples), lambda i, where: (where[5], 0, 0))]
        + [whole(count, blk, blk)] * 2
        + [factor, factor],
        [whole(width, samples), whole(rows, samples)],
        [((width, samples), F32), ((rows, samples), F32)],
        "drift",
    )(where, parent_state, mine, other, fh, fl)


def passed(arrays, after):
    return call(lambda *_: None, (1,), 0, [], [], [], "passed", after=[after], through=arrays)()


def begin_kernel(steps, where, weight, p_ref, uh, ul, vh, vl, fh, fl, rest, s_out, g_out, mine, hi, lo):
    g = pl.program_id(0)

    @pl.when(g < steps)
    def _():
        p = split(p_ref[...])
        part = dot3((uh[...], ul[...]), p, NT)

        @pl.when(g == 0)
        def _():
            mine[...] = part

        @pl.when(g > 0)
        def _():
            mine[...] += part

        @pl.when(g != where[0])
        def _():
            rest[...] = dot3((vh[...], vl[...]), p)

    @pl.when(g == steps)
    def _():
        hi[...], lo[...] = split(mine[...] * weight[0])

    @pl.when(g >= steps)
    def _():
        part = dot3((hi[...], lo[...]), (fh[...], fl[...]))
        orders = g_out.shape[0]
        s_out[...] = part[orders:]
        g_out[...] = part[:orders]


def begin(where, weight, cost_rows, uh, ul, fh, fl, after):
    rows, width = cost_rows.shape
    tall = uh.shape[0]
    orders = tall - rows
    steps = width // rows
    tile = 512

    def early(g):
        return jnp.minimum(g, steps - 1)

    def late(g):
        return jnp.maximum(g - steps, 0)

    each = pl.BlockSpec((tall, rows), lambda g, *_: (0, early(g)))
    own = pl.BlockSpec((tall, rows), lambda g, where, _: (0, where[0]))
    factor = pl.BlockSpec((rows, tile), lambda g, where, _: (where[0], late(g)))
    return call(
        functools.partial(begin_kernel, steps),
        (steps + width // tile,),
        2,
        [pl.BlockSpec((rows, rows), lambda g, *_: (0, early(g))), each, each, own, own, factor, factor],
        [
            each,
            pl.BlockSpec((rows, tile), lambda g, *_: (0, late(g))),
            pl.BlockSpec((orders, tile), lambda g, *_: (0, late(g))),
        ],
        [((tall, width), F32), ((rows, width), F32), ((orders, width), F32)],
        "begin",
        [pltpu.VMEM((tall, rows), F32)] + [pltpu.VMEM((tall, rows), BF16)] * 2,
        after=after,
    )(where, weight, cost_rows, uh, ul, uh, ul, fh, fl)


def stage_kernel(options, size, where, weight, *refs):
    arrived = refs[:options]
    vh, vl, n_in, fh, fl, s_in, g_in, *refs = refs[options:]
    if size > 1:
        uh, ul, s_out, g_out, n_out, done, hi, lo, xh, xl = refs
    else:
        s_out, g_out, done, hi, lo, xh, xl = refs
    g = pl.program_id(0)
    n = xh.shape[0] // arrived[0].shape[1]
    for c in range(options):
        for t in range(size):

            @pl.when((g == t) & (where[0] == c))
            def _():
                unpack(arrived[c], t, n, xh, xl)

    @pl.when(g == 0)
    def _():
        done[...] = n_in[...] + dot3((vh[...], vl[...]), (xh[...], xl[...]))

    if size > 1:

        @pl.when((g > 0) & (g < size))
        def _():
            x = xh[...], xl[...]
            done[...] += dot3((uh[...], ul[...]), x, NT)
            n_out[...] = n_in[...] + dot3((vh[...], vl[...]), x)

    @pl.when(g == size)
    def _():
        hi[...], lo[...] = split(done[...] * weight[0])

    @pl.when(g >= size)
    def _():
        part = dot3((hi[...], lo[...]), (fh[...], fl[...]))
        orders = g_out.shape[0]
        s_out[...] = s_in[...] + part[orders:]
        g_out[...] = g_in[...] + part[:orders]


def stage(where, weight, arrived, size, uh, ul, n, fh, fl, sums, after=(), through=()):
    tall, width = n.shape
    rows, orders = sums[0].shape[0], sums[1].shape[0]
    tile = 512

    def place(g, where):
        return where[1 + jnp.minimum(g, size - 1)]

    def later(g, where):
        return where[1 + jnp.clip(g, 1, size - 1)]

    def turn(g):
        return jnp.maximum(g - size, 0)

    block = pl.BlockSpec((tall, rows), lambda g, where, _: (0, place(g, where)))
    beyond = pl.BlockSpec((tall, rows), lambda g, where, _: (0, later(g, where)))
    focus = pl.BlockSpec((tall, rows), lambda g, where, _: (0, where[1]))
    factor = pl.BlockSpec((rows, tile), lambda g, where, _: (where[1], turn(g)))
    s_spec = pl.BlockSpec((rows, tile), lambda g, *_: (0, turn(g)))
    g_spec = pl.BlockSpec((orders, tile), lambda g, *_: (0, turn(g)))
    first = 2 + len(arrived)
    more = size > 1
    return call(
        functools.partial(stage_kernel, len(arrived), size),
        (size + width // tile,),
        2,
        [whole(*x.shape) for x in arrived]
        + [focus, focus, block, factor, factor, s_spec, g_spec]
        + [beyond] * (2 * more),
        [s_spec, g_spec] + [beyond] * more,
        [((rows, width), F32), ((orders, width), F32)] + [((tall, width), F32)] * more,
        "stage",
        [pltpu.VMEM((tall, rows), F32)] + [pltpu.VMEM((tall, rows), BF16)] * 2 + [pltpu.VMEM((rows, rows), BF16)] * 2,
        {first + 5: 0, first + 6: 1, **({first + 2: 2} if more else {})},
        after,
        through,
    )(where, weight, *arrived, uh, ul, n, fh, fl, *sums, *([uh, ul] if more else []))


def final_kernel(where, h_ref, g1, g2, s1, s2, q1, q2, d_ref, x_ref, y_ref, bh, bl, gain, out, reached, hi, lo, q):
    n = pl.program_id(0)
    rows = out.shape[0]

    @pl.when(n == 0)
    def _():
        value = -dot3(split(h_ref[...]), split(g1[...] + g2[...]))
        gain[...] = value
        hi[...], lo[...] = split(value.T)
        q[...] = jnp.zeros_like(q)

    cross = split(q1[...] + q2[...])
    part = s1[...] + s2[...] + dot3((hi[...], lo[...]), cross)
    diag = lax.broadcasted_iota(jnp.int32, (rows, rows), 0) == lax.broadcasted_iota(jnp.int32, (rows, rows), 1)
    out[...] = part + jnp.where(diag & (n == where[0]), d_ref[...], 0.0)
    q[...] += dot3(cross, split(x_ref[...]))

    @pl.when(n == pl.num_programs(0) - 1)
    def _():
        u = -dot3(split(h_ref[...]), split(q[...]))
        reached[...] = y_ref[...] + dot3((bh[...], bl[...]), split(u))


def final(where, hinv, own, other, state_cost, x, y, fh, fl):
    rows, width = own[0].shape
    orders = own[1].shape[0]
    samples = x.shape[1]
    s_spec = pl.BlockSpec((rows, rows), lambda n, where: (0, n))
    g_spec = pl.BlockSpec((orders, rows), lambda n, where: (0, n))
    mine = pl.BlockSpec((orders, rows), lambda n, where: (0, where[0]))
    factor = pl.BlockSpec((rows, orders), lambda n, where: (where[0], width // orders))
    return call(
        final_kernel,
        (width // rows,),
        1,
        [whole(orders, orders), mine, mine, s_spec, s_spec, g_spec, g_spec, whole(1, rows)]
        + [pl.BlockSpec((rows, samples), lambda n, where: (n, 0)), whole(rows, samples), factor, factor],
        [whole(orders, rows), s_spec, whole(rows, samples)],
        [((orders, rows), F32), ((rows, width), F32), ((rows, samples), F32)],
        "final",
        [pltpu.VMEM((rows, orders), BF16)] * 2 + [pltpu.VMEM((orders, samples), F32)],
    )(where, hinv, own[1], other[1], own[0], other[0], own[1], other[1], state_cost[None], x, y, fh, fl)


def image_kernel(where, weight, fh, fl, p_ref, out, acc):
    k = pl.program_id(0)
    part = dot3(split(p_ref[...]), (fh[...], fl[...]))

    @pl.when(k == 0)
    def _():
        acc[...] = part

    @pl.when(k > 0)
    def _():
        acc[...] += part

    @pl.when(k == pl.num_programs(0) - 1)
    def _():
        out[...] = acc[...].T * weight[0]


def image(where, weight, fh, fl, cost_rows):
    rows, width = cost_rows.shape
    chunk = 512
    factor = pl.BlockSpec((chunk, rows), lambda k, where, _: (k, where[0]))
    return call(
        image_kernel,
        (width // chunk,),
        2,
        [factor, factor, pl.BlockSpec((rows, chunk), lambda k, *_: (0, k))],
        [whole(rows, rows)],
        [((rows, rows), F32)],
        "image",
        [pltpu.VMEM((rows, rows), F32)],
    )(where, weight, fh, fl, cost_rows)[0]


def accumulate_kernel(first, where, y_ref, fh, fl, *refs):
    out = refs[-1]
    part = dot3(split(y_ref[...]), (fh[...], fl[...]))
    out[...] = part if first else refs[0][...] + part


def accumulate(where, y, fh, fl, acc):
    rows = y.shape[0]
    total = fh.shape[1]
    tile = 512
    first = acc is None
    spec = pl.BlockSpec((rows, tile), lambda n, where: (0, n))
    factor = pl.BlockSpec((rows, tile), lambda n, where: (where[0], n))
    return call(
        functools.partial(accumulate_kernel, first),
        (total // tile,),
        1,
        [whole(rows, rows), factor, factor] + [spec] * (not first),
        [spec],
        [((rows, total), F32)],
        "accumulate",
        aliases=None if first else {4: 0},
    )(where, y, fh, fl, *(() if first else (acc,)))[0]


def by_images(z, parts, weight, cost_rows, fh, fl):
    rows, width = cost_rows.shape
    acc = None
    for d in range(parts):
        block = image(((z + d) % parts)[None], weight, fh, fl, cost_rows)
        if d:
            block = lax.ppermute(block, "row", [(i, (i + d) % parts) for i in range(parts)])
        acc = accumulate(((z - d) % parts)[None], block, fh, fl, acc)
    cross = lax.all_gather(acc[:, width:], "row")
    return acc[:, :width], jnp.swapaxes(cross.reshape(width, -1), 0, 1)


def by_blocks(z, core, parent, weight, cost_rows, parent_state, dense_parts, control_cost, blk, messages):
    fh, fl, uh, ul, w = dense_parts
    edge = ((z == 0) | (z == 3)).astype(jnp.int32)
    left = z < 2
    second, third = jnp.where(left, 2, 1), jnp.where(left, 3, 0)

    def moved(x, *pairs):
        return lax.ppermute(x, "row", pairs)

    def across(x):
        return moved(x, (1, 2), (2, 1))

    def to_end(x):
        return moved(x, (1, 0), (2, 3))

    pair = moved(messages[0], (0, 1), (1, 0), (2, 3), (3, 2))
    mid = across(messages[1])
    keep, give = gram(weight, jnp.stack([z, core]), uh, ul, w, blk, [])
    tiles = keep + swapped(give)
    n, *sums = begin(z[None], weight, cost_rows, uh, ul, fh, fl, [tiles])
    tiles = tiles + moved(tiles, (0, 1), (3, 2))
    mid, tiles = passed([mid, tiles], n)
    end = to_end(mid)
    tiles = tiles + across(tiles)
    pair, tiles = passed([pair, tiles], n)
    mid_last = across(pair[: len(lower(w.shape[0] // blk)) + 2])
    finished = to_end(tiles)
    where = jnp.stack([z * 0, z ^ 1, second, third])
    *sums, n = stage(where, weight, [pair], 3, uh, ul, n, fh, fl, sums)
    mid_last, finished = passed([mid_last, finished], n)
    end_last = to_end(mid_last)
    tiles = jnp.where(edge == 1, finished, tiles)
    hinv = inverse(core[None], tiles, swapped(tiles), control_cost, [n])
    where = jnp.stack([edge, second, third])
    *sums, n = stage(where, weight, [mid, end], 2, uh, ul, n, fh, fl, sums, [hinv])
    where = jnp.stack([edge, third])
    sums = stage(where, weight, [mid_last, end_last], 1, uh, ul, n, fh, fl, sums)
    halves = collect(edge[None], [pair, mid, end, mid_last, end_last])
    where = jnp.stack([core, z, z ^ 1, second, third, parent])
    x, y = drift(where, parent_state, halves, swapped(halves), fh, fl)
    return hinv, sums, x, y


def swapped(x):
    n = lax.axis_size("leaf")
    return lax.ppermute(x, "leaf", [(i, i ^ 1) for i in range(n)])


def shards(
    leaf_cost,
    a_blocks,
    a_cols,
    b_blocks,
    b_cols,
    branch_prob,
    state_cost,
    control_cost,
    parent_state,
):
    cost_rows = leaf_cost[0]
    rows, width = cost_rows.shape
    blk = a_blocks.shape[3]
    orders = control_cost.shape[0]
    parts = lax.axis_size("row")
    z = lax.axis_index("row")
    leaf = lax.axis_index("leaf")
    core = leaf % 2
    line = parts == 4 and rows == orders

    sent = []
    if line:
        left = z < 2
        near = jnp.where(left, 0, 3)
        where = jnp.stack([z, near, jnp.where(left, 2, 1), 3 - near, leaf // 2, core])
        sent = pack(where, cost_rows, parent_state, blk)
    parts_of = dense(z[None], cost_rows, a_blocks[0], a_cols, b_blocks[0], b_cols, orders, sent)
    fh, fl, uh, ul, w = parts_of
    if line:
        hinv, own, x, y = by_blocks(
            z, core, leaf // 2, branch_prob, cost_rows, parent_state, parts_of, control_cost, blk, sent
        )
    else:
        keep, give = gram(branch_prob, jnp.stack([z, core]), uh, ul, w, blk, [])
        tiles = lax.psum(keep + swapped(give), "row")
        hinv = inverse(core[None], tiles, swapped(tiles), control_cost, [])
        own = by_images(z, parts, branch_prob, cost_rows, fh, fl)
        own_state = lax.dynamic_index_in_dim(parent_state, leaf // 2, 0, keepdims=False)
        x = lax.all_gather(own_state, "row", tiled=True)
        y = dot3([lax.dynamic_slice(f, (z * rows, 0), (rows, width)) for f in (fh, fl)], parted(x))
    other = tuple(swapped(x) for x in own)
    gain, pcost, reached = final(z[None], hinv, own, other, state_cost, x, y, fh, fl)
    return pcost[None], gain[None], reached[None]


def solution(mesh):
    placed = (
        P("leaf", "row", None),
        P("leaf", None, None, None, None),
        P("leaf", None, None),
        P("leaf", None, None, None, None),
        P("leaf", None, None),
        P("leaf"),
        P("row"),
        P(),
        P(None, "row", None),
    )
    return jax.shard_map(
        shards,
        mesh=mesh,
        in_specs=placed,
        out_specs=(P("leaf", "row", None), P("leaf", None, "row"), P("leaf", "row", None)),
        check_vma=False,
    )
```

```python
import functools

import jax
import jax.numpy as jnp
from jax import lax
from jax.experimental import pallas as pl
from jax.experimental.pallas import tpu as pltpu
from jax.sharding import PartitionSpec as P

HIGHEST = lax.Precision.HIGHEST
F32 = jnp.float32
BF16 = jnp.bfloat16
VMEM_LIMIT = 56 * 2**20
NN = (((1,), (0,)), ((), ()))
NT = (((1,), (1,)), ((), ()))


def split(x):
    hi = x.astype(BF16)
    return hi, (x - hi.astype(F32)).astype(BF16)


def parted(x):
    hi = lax.reduce_precision(x, 8, 7)
    return hi.astype(BF16), (x - hi).astype(BF16)


def dot3(a, b, dims=NN):
    one = functools.partial(lax.dot_general, dimension_numbers=dims, preferred_element_type=F32)
    return one(a[0], b[0]) + (one(a[0], b[1]) + one(a[1], b[0]))


def call(kernel, grid, prefetch, ins, outs, shapes, name, scratch=(), aliases=None, after=(), through=()):
    n_in, n_out = len(ins), len(outs)
    extra = len(after) + len(through)
    anywhere = pl.BlockSpec(memory_space=pl.ANY)

    def body(*refs):
        start = prefetch + n_in
        stop = start + extra + n_out
        kernel(*refs[:start], *refs[start + extra : stop], *refs[stop + len(through) :])

    aliases = dict(aliases or {})
    for t in range(len(through)):
        aliases[prefetch + n_in + len(after) + t] = n_out + t
    built = pl.pallas_call(
        body,
        grid_spec=pltpu.PrefetchScalarGridSpec(
            num_scalar_prefetch=prefetch,
            grid=grid,
            in_specs=list(ins) + [anywhere] * extra,
            out_specs=list(outs) + [anywhere] * len(through),
            scratch_shapes=scratch,
        ),
        out_shape=[jax.ShapeDtypeStruct(shape, kind) for shape, kind in shapes]
        + [jax.ShapeDtypeStruct(x.shape, x.dtype) for x in through],
        input_output_aliases=aliases,
        compiler_params=pltpu.CompilerParams(vmem_limit_bytes=VMEM_LIMIT),
        cost_estimate=pl.CostEstimate(flops=1, bytes_accessed=1, transcendentals=0),
        name=name,
    )
    return lambda *args: built(*args, *after, *through)


def whole(*shape):
    return pl.BlockSpec(shape, lambda *_: (0,) * len(shape))


def lower(n):
    return [(i, j) for i in range(n) for j in range(i + 1)]


def dense_kernel(blk, step, width, where, acol, bcol, a_ref, b_ref, fh, fl, uh, ul):
    i = pl.program_id(0)
    orders = fh.shape[1] - width
    group = (uh.shape[0] - orders) // blk
    for ref in (fh, fl, uh, ul):
        ref[...] = jnp.zeros_like(ref)
    diag = lax.broadcasted_iota(jnp.int32, (blk, blk), 0) == lax.broadcasted_iota(jnp.int32, (blk, blk), 1)
    eye = jnp.where(diag, 0.75, 0.0).astype(F32)
    for t in range(step // blk):
        row = i * (step // blk) + t
        at = slice(t * blk, (t + 1) * blk)
        for s in range(a_ref.shape[1]):
            col = acol[0, row, s]
            block = a_ref[t, s] + eye if s == 0 else a_ref[t, s]
            to = pl.ds(pl.multiple_of(col * blk, blk), blk)
            fh[at, to], fl[at, to] = split(block)
            local = col - where[0] * group

            @pl.when((local >= 0) & (local < group))
            def _():
                to = pl.ds(pl.multiple_of(orders + local * blk, blk), blk)
                uh[to, at], ul[to, at] = split(block.T)

        for s in range(b_ref.shape[1]):
            col = bcol[0, row, s]
            block = b_ref[t, s]
            to = pl.ds(pl.multiple_of(width + col * blk, blk), blk)
            fh[at, to], fl[at, to] = split(block)
            to = pl.ds(pl.multiple_of(col * blk, blk), blk)
            uh[to, at], ul[to, at] = split(block.T)


def dense(where, rows, a_blocks, a_cols, b_blocks, b_cols, orders, after):
    count, nnza, blk, _ = a_blocks.shape
    nnzb = b_blocks.shape[1]
    width = count * blk
    step = 2 * blk
    total = width + orders
    factor = pl.BlockSpec((step, total), lambda i, *_: (i, 0))
    turned = pl.BlockSpec((rows + orders, step), lambda i, *_: (0, i))
    return call(
        functools.partial(dense_kernel, blk, step, width),
        (width // step,),
        3,
        [
            pl.BlockSpec((2, nnza, blk, blk), lambda i, *_: (i, 0, 0, 0)),
            pl.BlockSpec((2, nnzb, blk, blk), lambda i, *_: (i, 0, 0, 0)),
        ],
        [factor, factor, turned, turned],
        [((width, total), BF16)] * 2 + [((rows + orders, width), BF16)] * 2,
        "dense",
        after=after,
    )(where, a_cols, b_cols, a_blocks, b_blocks)


def inverse_block(m):
    n = m.shape[0]
    sub = lax.broadcasted_iota(jnp.int32, (8, n), 0)
    lane = lax.broadcasted_iota(jnp.int32, (8, n), 1)
    strips = [m[i : i + 8] for i in range(0, n, 8)]

    def along(v, j):
        return jnp.broadcast_to(v[:, j : j + 1], (8, n))

    def down(v, t):
        return jnp.broadcast_to(v[t : t + 1], (8, n))

    for q in range(n // 8):
        panel = strips[q]
        cols = [along(panel, 8 * q + b) for b in range(8)]
        for t in range(8):
            here = sub == t
            inv = 1.0 / down(cols[t], t)

            def reduced(v):
                r = down(v, t) * inv
                return jnp.where(here, r, v - cols[t] * r)

            panel = reduced(jnp.where(lane == 8 * q + t, jnp.where(here, 1.0, 0.0), panel))
            cols[t + 1 :] = [reduced(v) for v in cols[t + 1 :]]
        inside = (lane >= 8 * q) & (lane < 8 * q + 8)
        rows = [down(panel, b) for b in range(8)]
        for i in range(q + 1, q + n // 8):
            old = strips[i % (n // 8)]
            terms = [along(old, 8 * q + b) * rows[b] for b in range(8)]
            while len(terms) > 1:
                terms = [x + y for x, y in zip(terms[::2], terms[1::2])]
            strips[i % (n // 8)] = jnp.where(inside, 0.0, old) - terms[0]
        strips[q] = panel
    return jnp.concatenate(strips, axis=0)


def inverse_kernel(blk, mine, other, d_ref, out):
    n = out.shape[0]
    dot = functools.partial(jnp.dot, precision=HIGHEST, preferred_element_type=F32)
    diag = lax.broadcasted_iota(jnp.int32, (n, n), 0) == lax.broadcasted_iota(jnp.int32, (n, n), 1)
    out[...] = mine[...] + other[...] + jnp.where(diag, d_ref[...], 0.0)

    @pl.loop(0, n // blk)
    def _(b):
        here = pl.ds(pl.multiple_of(b * blk, blk), blk)
        inv = inverse_block(out[here, here])
        row = dot(inv, out[here, :])
        col = out[:, here]
        out[...] -= dot(col, row)
        out[:, here] = -dot(col, inv)
        out[here, :] = row
        out[here, here] = inv


def inverse(mine, other, control_cost, blk):
    n = control_cost.shape[0]
    return call(
        functools.partial(inverse_kernel, blk),
        (1,),
        0,
        [whole(n, n)] * 2 + [whole(1, n)],
        [whole(n, n)],
        [((n, n), F32)],
        "inverse",
    )(mine, other, control_cost[None])[0]


def tiled(block, blk):
    n = block.shape[0] // blk
    return [block[i * blk : (i + 1) * blk, j * blk : (j + 1) * blk] for i in range(n) for j in range(n)]


def pack_kernel(blk, where, own, x_ref, *refs):
    *blocks, out = refs
    diag = [own[i * blk : (i + 1) * blk, j * blk : (j + 1) * blk] for i, j in lower(own.shape[0] // blk)]
    x = [x_ref[0, :blk], x_ref[0, blk:]]
    for t, tile in enumerate(diag + x + [tile for block in blocks for tile in tiled(block, blk)]):
        out[t] = tile


def pack(where, cost_rows, parent_state, blk, after):
    rows = cost_rows.shape[0]
    samples = parent_state.shape[2]
    picks = [0] + list(range(3, where.shape[0]))
    size = len(lower(rows // blk)) + 2 + (len(picks) - 1) * (rows // blk) ** 2
    specs = [pl.BlockSpec((rows, rows), functools.partial(lambda t, i, where: (0, where[t]), t)) for t in picks]
    specs.insert(1, pl.BlockSpec((1, rows // 2, samples), lambda i, where: (where[1], where[2], 0)))
    args = [cost_rows] * len(picks)
    args.insert(1, parent_state)
    return call(
        functools.partial(pack_kernel, blk),
        (1,),
        1,
        specs,
        [whole(size, blk, blk)],
        [((size, blk, blk), F32)],
        "pack",
        after=after,
    )(where, *args)[0]


def front(message, size):
    shape = (size,) + message.shape[1:]

    def kernel(x, out):
        out[...] = x[...]

    return call(kernel, (1,), 0, [whole(*shape)], [whole(*shape)], [(shape, F32)], "front")(message)[0]


def unpack(tiles, step, n, xh, xl):
    blk = tiles.shape[1]
    lead = len(lower(n))
    for t, (i, j) in enumerate(lower(n) if step == 0 else [(i, j) for i in range(n) for j in range(n)]):
        tile = tiles[t if step == 0 else lead + 2 + (step - 1) * n * n + t]
        places = [(i, j, tile)] + ([(j, i, tile.T)] if step == 0 and i != j else [])
        for r, c, value in places:
            at = slice(r * blk, (r + 1) * blk), slice(c * blk, (c + 1) * blk)
            xh[at], xl[at] = split(value)


def collect_kernel(where, pair, mid, end, mid_last, end_last, out):
    out[:2] = pair[...]

    @pl.when(where[0] == 1)
    def _():
        out[2:4] = end[...]
        out[4:6] = end_last[...]

    @pl.when(where[0] == 0)
    def _():
        out[2:4] = mid[...]
        out[4:6] = mid_last[...]


def collect(where, messages, after):
    blk = messages[0].shape[1]
    lead = messages[3].shape[0] // 2 - 1
    return call(
        collect_kernel,
        (1,),
        1,
        [pl.BlockSpec((2, blk, blk), lambda i, where: (lead, 0, 0))] * 5,
        [whole(6, blk, blk)],
        [((6, blk, blk), F32)],
        "collect",
        after=[after],
    )(where, *messages)[0]


def drift_kernel(where, own, mine, other, fh, fl, x_ref, out):
    blk = mine.shape[1]
    rows = own.shape[1]
    core = where[0]
    x_ref[pl.ds(pl.multiple_of(where[1] * rows, rows), rows)] = own[0]
    for d in range(3):
        for t in range(2):
            base = where[2 + d] * rows + t * blk
            half = rows // 2
            x_ref[pl.ds(pl.multiple_of(base + core * half, blk), blk)] = mine[2 * d + t]
            x_ref[pl.ds(pl.multiple_of(base + (1 - core) * half, blk), blk)] = other[2 * d + t]
    out[...] = dot3((fh[...], fl[...]), split(x_ref[...]))


def drift(where, parent_state, mine, other, fh, fl, after):
    _, rows, samples = parent_state.shape
    count, blk, _ = mine.shape
    width = rows * 4
    factor = pl.BlockSpec((rows, width), lambda i, where: (where[1], 0))
    return call(
        drift_kernel,
        (1,),
        1,
        [pl.BlockSpec((1, rows, samples), lambda i, where: (where[5], 0, 0))]
        + [whole(count, blk, blk)] * 2
        + [factor, factor],
        [whole(width, samples), whole(rows, samples)],
        [((width, samples), F32), ((rows, samples), F32)],
        "drift",
        after=[after],
    )(where, parent_state, mine, other, fh, fl)


def passed(arrays, *after):
    return call(lambda *_: None, (1,), 0, [], [], [], "passed", after=after, through=arrays)()


def begin_kernel(steps, where, weight, p_ref, uh, ul, vh, vl, fh, fl, bh, bl, rest, s_out, g_out, h_out, mine, hi, lo):
    g = pl.program_id(0)

    @pl.when(g < steps)
    def _():
        p = split(p_ref[...])
        part = dot3((uh[...], ul[...]), p, NT)

        @pl.when(g == 0)
        def _():
            mine[...] = part

        @pl.when(g > 0)
        def _():
            mine[...] += part

        @pl.when(g != where[0])
        def _():
            rest[...] = dot3((vh[...], vl[...]), p)

    @pl.when(g == steps)
    def _():
        hi[...], lo[...] = split(mine[...] * weight[0])
        orders = h_out.shape[0]
        h_out[...] = dot3((hi[:orders], lo[:orders]), (bh[...], bl[...]))

    @pl.when(g >= steps)
    def _():
        part = dot3((hi[...], lo[...]), (fh[...], fl[...]))
        orders = g_out.shape[0]
        s_out[...] = part[orders:]
        g_out[...] = part[:orders]


def begin(where, weight, cost_rows, uh, ul, fh, fl):
    rows, width = cost_rows.shape
    tall = uh.shape[0]
    orders = tall - rows
    steps = width // rows
    tile = 512

    def early(g):
        return jnp.minimum(g, steps - 1)

    def late(g):
        return jnp.maximum(g - steps, 0)

    each = pl.BlockSpec((tall, rows), lambda g, *_: (0, early(g)))
    own = pl.BlockSpec((tall, rows), lambda g, where, _: (0, where[0]))
    factor = pl.BlockSpec((rows, tile), lambda g, where, _: (where[0], late(g)))
    control = pl.BlockSpec((rows, orders), lambda g, where, _: (where[0], width // orders))
    return call(
        functools.partial(begin_kernel, steps),
        (steps + width // tile,),
        2,
        [pl.BlockSpec((rows, rows), lambda g, *_: (0, early(g))), each, each, own, own, factor, factor, control, control],
        [
            each,
            pl.BlockSpec((rows, tile), lambda g, *_: (0, late(g))),
            pl.BlockSpec((orders, tile), lambda g, *_: (0, late(g))),
            whole(orders, orders),
        ],
        [((tall, width), F32), ((rows, width), F32), ((orders, width), F32), ((orders, orders), F32)],
        "begin",
        [pltpu.VMEM((tall, rows), F32)] + [pltpu.VMEM((tall, rows), BF16)] * 2,
    )(where, weight, cost_rows, uh, ul, uh, ul, fh, fl, fh, fl)


def stage_kernel(options, size, where, weight, *refs):
    arrived = refs[:options]
    vh, vl, n_in, fh, fl, bh, bl, s_in, g_in, h_in, *refs = refs[options:]
    if size > 1:
        uh, ul, s_out, g_out, h_out, n_out, done, hi, lo, xh, xl = refs
    else:
        s_out, g_out, h_out, done, hi, lo, xh, xl = refs
    g = pl.program_id(0)
    n = xh.shape[0] // arrived[0].shape[1]
    for c in range(options):
        for t in range(size):

            @pl.when((g == t) & (where[0] == c))
            def _():
                unpack(arrived[c], t, n, xh, xl)

    @pl.when(g == 0)
    def _():
        done[...] = n_in[...] + dot3((vh[...], vl[...]), (xh[...], xl[...]))

    if size > 1:

        @pl.when((g > 0) & (g < size))
        def _():
            x = xh[...], xl[...]
            done[...] += dot3((uh[...], ul[...]), x, NT)
            n_out[...] = n_in[...] + dot3((vh[...], vl[...]), x)

    @pl.when(g == size)
    def _():
        hi[...], lo[...] = split(done[...] * weight[0])
        orders = h_out.shape[0]
        h_out[...] = h_in[...] + dot3((hi[:orders], lo[:orders]), (bh[...], bl[...]))

    @pl.when(g >= size)
    def _():
        part = dot3((hi[...], lo[...]), (fh[...], fl[...]))
        orders = g_out.shape[0]
        s_out[...] = s_in[...] + part[orders:]
        g_out[...] = g_in[...] + part[:orders]


def stage(where, weight, arrived, size, uh, ul, n, fh, fl, sums, after=(), through=()):
    tall, width = n.shape
    rows, orders = sums[0].shape[0], sums[1].shape[0]
    tile = 512

    def place(g, where):
        return where[1 + jnp.minimum(g, size - 1)]

    def later(g, where):
        return where[1 + jnp.clip(g, 1, size - 1)]

    def turn(g):
        return jnp.maximum(g - size, 0)

    block = pl.BlockSpec((tall, rows), lambda g, where, _: (0, place(g, where)))
    beyond = pl.BlockSpec((tall, rows), lambda g, where, _: (0, later(g, where)))
    focus = pl.BlockSpec((tall, rows), lambda g, where, _: (0, where[1]))
    factor = pl.BlockSpec((rows, tile), lambda g, where, _: (where[1], turn(g)))
    s_spec = pl.BlockSpec((rows, tile), lambda g, *_: (0, turn(g)))
    g_spec = pl.BlockSpec((orders, tile), lambda g, *_: (0, turn(g)))
    control = pl.BlockSpec((rows, orders), lambda g, where, _: (where[1], width // orders))
    first = 2 + len(arrived)
    more = size > 1
    return call(
        functools.partial(stage_kernel, len(arrived), size),
        (size + width // tile,),
        2,
        [whole(*x.shape) for x in arrived]
        + [focus, focus, block, factor, factor, control, control, s_spec, g_spec, whole(orders, orders)]
        + [beyond] * (2 * more),
        [s_spec, g_spec, whole(orders, orders)] + [beyond] * more,
        [((rows, width), F32), ((orders, width), F32), ((orders, orders), F32)] + [((tall, width), F32)] * more,
        "stage",
        [pltpu.VMEM((tall, rows), F32)] + [pltpu.VMEM((tall, rows), BF16)] * 2 + [pltpu.VMEM((rows, rows), BF16)] * 2,
        {first + 7: 0, first + 8: 1, first + 9: 2, **({first + 2: 3} if more else {})},
        after,
        through,
    )(where, weight, *arrived, uh, ul, n, fh, fl, fh, fl, *sums, *([uh, ul] if more else []))


def final_kernel(where, h_ref, g1, g2, s1, s2, q1, q2, d_ref, x_ref, y_ref, bh, bl, gain, out, reached, hi, lo, q):
    n = pl.program_id(0)
    rows = out.shape[0]

    @pl.when(n == 0)
    def _():
        value = -dot3(split(h_ref[...]), split(g1[...] + g2[...]))
        gain[...] = value
        hi[...], lo[...] = split(value.T)
        q[...] = jnp.zeros_like(q)

    cross = split(q1[...] + q2[...])
    part = s1[...] + s2[...] + dot3((hi[...], lo[...]), cross)
    diag = lax.broadcasted_iota(jnp.int32, (rows, rows), 0) == lax.broadcasted_iota(jnp.int32, (rows, rows), 1)
    out[...] = part + jnp.where(diag & (n == where[0]), d_ref[...], 0.0)
    q[...] += dot3(cross, split(x_ref[...]))

    @pl.when(n == pl.num_programs(0) - 1)
    def _():
        u = -dot3(split(h_ref[...]), split(q[...]))
        reached[...] = y_ref[...] + dot3((bh[...], bl[...]), split(u))


def final(where, hinv, own, other, state_cost, x, y, fh, fl):
    rows, width = own[0].shape
    orders = own[1].shape[0]
    samples = x.shape[1]
    s_spec = pl.BlockSpec((rows, rows), lambda n, where: (0, n))
    g_spec = pl.BlockSpec((orders, rows), lambda n, where: (0, n))
    mine = pl.BlockSpec((orders, rows), lambda n, where: (0, where[0]))
    factor = pl.BlockSpec((rows, orders), lambda n, where: (where[0], width // orders))
    return call(
        final_kernel,
        (width // rows,),
        1,
        [whole(orders, orders), mine, mine, s_spec, s_spec, g_spec, g_spec, whole(1, rows)]
        + [pl.BlockSpec((rows, samples), lambda n, where: (n, 0)), whole(rows, samples), factor, factor],
        [whole(orders, rows), s_spec, whole(rows, samples)],
        [((orders, rows), F32), ((rows, width), F32), ((rows, samples), F32)],
        "final",
        [pltpu.VMEM((rows, orders), BF16)] * 2 + [pltpu.VMEM((orders, samples), F32)],
    )(where, hinv, own[1], other[1], own[0], other[0], own[1], other[1], state_cost[None], x, y, fh, fl)


def image_kernel(where, weight, fh, fl, p_ref, out, acc):
    k = pl.program_id(0)
    part = dot3(split(p_ref[...]), (fh[...], fl[...]))

    @pl.when(k == 0)
    def _():
        acc[...] = part

    @pl.when(k > 0)
    def _():
        acc[...] += part

    @pl.when(k == pl.num_programs(0) - 1)
    def _():
        out[...] = acc[...].T * weight[0]


def image(where, weight, fh, fl, cost_rows):
    rows, width = cost_rows.shape
    chunk = 512
    factor = pl.BlockSpec((chunk, rows), lambda k, where, _: (k, where[0]))
    return call(
        image_kernel,
        (width // chunk,),
        2,
        [factor, factor, pl.BlockSpec((rows, chunk), lambda k, *_: (0, k))],
        [whole(rows, rows)],
        [((rows, rows), F32)],
        "image",
        [pltpu.VMEM((rows, rows), F32)],
    )(where, weight, fh, fl, cost_rows)[0]


def accumulate_kernel(first, where, y_ref, fh, fl, *refs):
    out = refs[-1]
    part = dot3(split(y_ref[...]), (fh[...], fl[...]))
    out[...] = part if first else refs[0][...] + part


def accumulate(where, y, fh, fl, acc):
    rows = y.shape[0]
    total = fh.shape[1]
    tile = 512
    first = acc is None
    spec = pl.BlockSpec((rows, tile), lambda n, where: (0, n))
    factor = pl.BlockSpec((rows, tile), lambda n, where: (where[0], n))
    return call(
        functools.partial(accumulate_kernel, first),
        (total // tile,),
        1,
        [whole(rows, rows), factor, factor] + [spec] * (not first),
        [spec],
        [((rows, total), F32)],
        "accumulate",
        aliases=None if first else {4: 0},
    )(where, y, fh, fl, *(() if first else (acc,)))[0]


def by_images(z, parts, weight, cost_rows, fh, fl):
    rows, width = cost_rows.shape
    acc = None
    for d in range(parts):
        block = image(((z + d) % parts)[None], weight, fh, fl, cost_rows)
        if d:
            block = lax.ppermute(block, "row", [(i, (i + d) % parts) for i in range(parts)])
        acc = accumulate(((z - d) % parts)[None], block, fh, fl, acc)
    cross = lax.all_gather(acc[:, width:], "row")
    return acc[:, :width], jnp.swapaxes(cross.reshape(width, -1), 0, 1)


def by_blocks(z, core, parent, weight, cost_rows, parent_state, dense_parts, control_cost, messages):
    fh, fl, uh, ul = dense_parts
    edge = ((z == 0) | (z == 3)).astype(jnp.int32)
    left = z < 2
    second, third = jnp.where(left, 2, 1), jnp.where(left, 3, 0)
    pair, mid = messages
    lead = 2 * mid.shape[0] - pair.shape[0]

    def moved(x, *pairs):
        return lax.ppermute(x, "row", pairs)

    def across(x):
        return moved(x, (1, 2), (2, 1))

    def to_end(x):
        return moved(x, (1, 0), (2, 3))

    pair = moved(pair, (0, 1), (1, 0), (2, 3), (3, 2))
    mid = across(mid)
    n, *sums = begin(z[None], weight, cost_rows, uh, ul, fh, fl)
    (mid,) = passed([mid], n)
    end = to_end(mid)
    mid_last = across(front(pair, lead))
    where = jnp.stack([z * 0, z ^ 1, second, third])
    *sums, n = stage(where, weight, [pair], 3, uh, ul, n, fh, fl, sums)
    (mid_last,) = passed([mid_last], n)
    end_last = to_end(mid_last)
    where = jnp.stack([edge, second, third])
    *sums, n = stage(where, weight, [mid, end], 2, uh, ul, n, fh, fl, sums)
    halves = collect(edge[None], [pair, mid, end, mid_last, end_last], n)
    where = jnp.stack([edge, third])
    s, g, h = stage(where, weight, [mid_last, end_last], 1, uh, ul, n, fh, fl, sums, [halves])
    where = jnp.stack([core, z, z ^ 1, second, third, parent])
    x, y = drift(where, parent_state, halves, swapped(halves), fh, fl, h)
    other = swapped(h)
    return h, other, passed([s, g], other, y), x, y


def swapped(x):
    n = lax.axis_size("leaf")
    return lax.ppermute(x, "leaf", [(i, i ^ 1) for i in range(n)])


def shards(
    leaf_cost,
    a_blocks,
    a_cols,
    b_blocks,
    b_cols,
    branch_prob,
    state_cost,
    control_cost,
    parent_state,
):
    cost_rows = leaf_cost[0]
    rows, width = cost_rows.shape
    blk = a_blocks.shape[3]
    orders = control_cost.shape[0]
    parts = lax.axis_size("row")
    z = lax.axis_index("row")
    leaf = lax.axis_index("leaf")
    core = leaf % 2
    line = parts == 4 and rows == orders

    sent = []
    if line:
        left = z < 2
        near = jnp.where(left, 0, 3)
        lead = [z, leaf // 2, core]
        sent.append(pack(jnp.stack(lead + [jnp.where(left, 2, 1), 3 - near]), cost_rows, parent_state, blk, []))
        sent.append(pack(jnp.stack(lead + [near]), cost_rows, parent_state, blk, sent))
    fh, fl, uh, ul = parts_of = dense(z[None], rows, a_blocks[0], a_cols, b_blocks[0], b_cols, orders, sent)
    if line:
        h, other_h, own, x, y = by_blocks(
            z, core, leaf // 2, branch_prob, cost_rows, parent_state, parts_of, control_cost, sent
        )
    else:
        w = dot3(parted(cost_rows), (fh[:, width:], fl[:, width:]))
        b_rows = [lax.dynamic_slice(f, (0, z * rows), (orders, rows)) for f in (uh, ul)]
        h = lax.psum(dot3(b_rows, parted(w)) * branch_prob[0], "row")
        other_h = swapped(h)
        own = by_images(z, parts, branch_prob, cost_rows, fh, fl)
        own_state = lax.dynamic_index_in_dim(parent_state, leaf // 2, 0, keepdims=False)
        x = lax.all_gather(own_state, "row", tiled=True)
        y = dot3([lax.dynamic_slice(f, (z * rows, 0), (rows, width)) for f in (fh, fl)], parted(x))
    hinv = inverse(h, other_h, control_cost, blk)
    other = tuple(swapped(x) for x in own)
    gain, pcost, reached = final(z[None], hinv, own, other, state_cost, x, y, fh, fl)
    return pcost[None], gain[None], reached[None]


def solution(mesh):
    placed = (
        P("leaf", "row", None),
        P("leaf", None, None, None, None),
        P("leaf", None, None),
        P("leaf", None, None, None, None),
        P("leaf", None, None),
        P("leaf"),
        P("row"),
        P(),
        P(None, "row", None),
    )
    return jax.shard_map(
        shards,
        mesh=mesh,
        in_specs=placed,
        out_specs=(P("leaf", "row", None), P("leaf", None, "row"), P("leaf", "row", None)),
        check_vma=False,
    )
```

```python
import functools

import jax
import jax.numpy as jnp
from jax import lax
from jax.experimental import pallas as pl
from jax.experimental.pallas import tpu as pltpu
from jax.sharding import PartitionSpec as P

HIGHEST = lax.Precision.HIGHEST
F32 = jnp.float32
BF16 = jnp.bfloat16
VMEM_LIMIT = 62 * 2**20
NN = (((1,), (0,)), ((), ()))
NT = (((1,), (1,)), ((), ()))


def split(x):
    hi = x.astype(BF16)
    return hi, (x - hi.astype(F32)).astype(BF16)


def parted(x):
    hi = lax.reduce_precision(x, 8, 7)
    return hi.astype(BF16), (x - hi).astype(BF16)


def dot3(a, b, dims=NN):
    one = functools.partial(lax.dot_general, dimension_numbers=dims, preferred_element_type=F32)
    rows = a[0].shape[0]
    both = jnp.concatenate(a, axis=0) if isinstance(a, (tuple, list)) else a.reshape(2 * rows, a.shape[2])
    part = one(both, b[0])
    return part[:rows] + (part[rows:] + one(a[0], b[1]))


def call(kernel, grid, prefetch, ins, outs, shapes, name, scratch=(), aliases=None, after=(), through=()):
    n_in, n_out = len(ins), len(outs)
    extra = len(after) + len(through)
    anywhere = pl.BlockSpec(memory_space=pl.ANY)

    def body(*refs):
        start = prefetch + n_in
        stop = start + extra + n_out
        kernel(*refs[:start], *refs[start + extra : stop], *refs[stop + len(through) :])

    aliases = dict(aliases or {})
    for t in range(len(through)):
        aliases[prefetch + n_in + len(after) + t] = n_out + t
    built = pl.pallas_call(
        body,
        grid_spec=pltpu.PrefetchScalarGridSpec(
            num_scalar_prefetch=prefetch,
            grid=grid,
            in_specs=list(ins) + [anywhere] * extra,
            out_specs=list(outs) + [anywhere] * len(through),
            scratch_shapes=scratch,
        ),
        out_shape=[jax.ShapeDtypeStruct(shape, kind) for shape, kind in shapes]
        + [jax.ShapeDtypeStruct(x.shape, x.dtype) for x in through],
        input_output_aliases=aliases,
        compiler_params=pltpu.CompilerParams(vmem_limit_bytes=VMEM_LIMIT),
        cost_estimate=pl.CostEstimate(flops=1, bytes_accessed=1, transcendentals=0),
        name=name,
    )
    return lambda *args: built(*args, *after, *through)


def whole(*shape):
    return pl.BlockSpec(shape, lambda *_: (0,) * len(shape))


def lower(n):
    return [(i, j) for i in range(n) for j in range(i + 1)]


def dense_kernel(blk, step, width, where, acol, bcol, a_ref, b_ref, fh, fl, u):
    i = pl.program_id(0)
    orders = fh.shape[1] - width
    group = (u.shape[1] - orders) // blk
    for ref in (fh, fl, u):
        ref[...] = jnp.zeros_like(ref)
    diag = lax.broadcasted_iota(jnp.int32, (blk, blk), 0) == lax.broadcasted_iota(jnp.int32, (blk, blk), 1)
    eye = jnp.where(diag, 0.75, 0.0).astype(F32)
    for t in range(step // blk):
        row = i * (step // blk) + t
        at = slice(t * blk, (t + 1) * blk)
        for s in range(a_ref.shape[1]):
            col = acol[0, row, s]
            block = a_ref[t, s] + eye if s == 0 else a_ref[t, s]
            to = pl.ds(pl.multiple_of(col * blk, blk), blk)
            fh[at, to], fl[at, to] = split(block)
            local = col - where[0] * group

            @pl.when((local >= 0) & (local < group))
            def _():
                to = pl.ds(pl.multiple_of(orders + local * blk, blk), blk)
                u[0, to, at], u[1, to, at] = split(block.T)

        for s in range(b_ref.shape[1]):
            col = bcol[0, row, s]
            block = b_ref[t, s]
            to = pl.ds(pl.multiple_of(width + col * blk, blk), blk)
            fh[at, to], fl[at, to] = split(block)
            to = pl.ds(pl.multiple_of(col * blk, blk), blk)
            u[0, to, at], u[1, to, at] = split(block.T)


def dense(where, rows, a_blocks, a_cols, b_blocks, b_cols, orders, after):
    count, nnza, blk, _ = a_blocks.shape
    nnzb = b_blocks.shape[1]
    width = count * blk
    step = 2 * blk
    total = width + orders
    factor = pl.BlockSpec((step, total), lambda i, *_: (i, 0))
    turned = pl.BlockSpec((2, rows + orders, step), lambda i, *_: (0, 0, i))
    return call(
        functools.partial(dense_kernel, blk, step, width),
        (width // step,),
        3,
        [
            pl.BlockSpec((2, nnza, blk, blk), lambda i, *_: (i, 0, 0, 0)),
            pl.BlockSpec((2, nnzb, blk, blk), lambda i, *_: (i, 0, 0, 0)),
        ],
        [factor, factor, turned],
        [((width, total), BF16)] * 2 + [((2, rows + orders, width), BF16)],
        "dense",
        after=after,
    )(where, a_cols, b_cols, a_blocks, b_blocks)


def inverse_block(m):
    n = m.shape[0]
    sub = lax.broadcasted_iota(jnp.int32, (8, n), 0)
    lane = lax.broadcasted_iota(jnp.int32, (8, n), 1)
    strips = [m[i : i + 8] for i in range(0, n, 8)]

    def along(v, j):
        return jnp.broadcast_to(v[:, j : j + 1], (8, n))

    def down(v, t):
        return jnp.broadcast_to(v[t : t + 1], (8, n))

    for q in range(n // 8):
        panel = strips[q]
        cols = [along(panel, 8 * q + b) for b in range(8)]
        for t in range(8):
            here = sub == t
            inv = 1.0 / down(cols[t], t)

            def reduced(v):
                r = down(v, t) * inv
                return jnp.where(here, r, v - cols[t] * r)

            panel = reduced(jnp.where(lane == 8 * q + t, jnp.where(here, 1.0, 0.0), panel))
            cols[t + 1 :] = [reduced(v) for v in cols[t + 1 :]]
        inside = (lane >= 8 * q) & (lane < 8 * q + 8)
        rows = [down(panel, b) for b in range(8)]
        for i in range(q + 1, q + n // 8):
            old = strips[i % (n // 8)]
            terms = [along(old, 8 * q + b) * rows[b] for b in range(8)]
            while len(terms) > 1:
                terms = [x + y for x, y in zip(terms[::2], terms[1::2])]
            strips[i % (n // 8)] = jnp.where(inside, 0.0, old) - terms[0]
        strips[q] = panel
    return jnp.concatenate(strips, axis=0)


def inverse_kernel(blk, mine, other, d_ref, out):
    n = out.shape[0]
    dot = functools.partial(jnp.dot, precision=HIGHEST, preferred_element_type=F32)
    diag = lax.broadcasted_iota(jnp.int32, (n, n), 0) == lax.broadcasted_iota(jnp.int32, (n, n), 1)
    out[...] = mine[...] + other[...] + jnp.where(diag, d_ref[...], 0.0)

    place = lax.broadcasted_iota(jnp.int32, (n, blk), 0) // blk

    @pl.loop(0, n // blk)
    def _(b):
        here = pl.ds(pl.multiple_of(b * blk, blk), blk)
        inv = inverse_block(out[here, here])
        row = dot(inv, out[here, :])
        out[...] -= dot(out[:, here], row)
        col = row.T
        out[:, here] = jnp.where(place < b, col, -col)
        out[here, :] = row
        out[here, here] = inv


def inverse(mine, other, control_cost, blk):
    n = control_cost.shape[0]
    return call(
        functools.partial(inverse_kernel, blk),
        (1,),
        0,
        [whole(n, n)] * 2 + [whole(1, n)],
        [whole(n, n)],
        [((n, n), F32)],
        "inverse",
    )(mine, other, control_cost[None])[0]


def tiled(block, blk):
    n = block.shape[0] // blk
    return [block[i * blk : (i + 1) * blk, j * blk : (j + 1) * blk] for i in range(n) for j in range(n)]


def pack_kernel(blk, where, own, x_ref, *refs):
    *blocks, out = refs
    diag = [own[i * blk : (i + 1) * blk, j * blk : (j + 1) * blk] for i, j in lower(own.shape[0] // blk)]
    x = [x_ref[0, :blk], x_ref[0, blk:]]
    for t, tile in enumerate(diag + x + [tile for block in blocks for tile in tiled(block, blk)]):
        out[t] = tile


def pack(where, cost_rows, parent_state, blk, after):
    rows = cost_rows.shape[0]
    samples = parent_state.shape[2]
    picks = [0] + list(range(3, where.shape[0]))
    size = len(lower(rows // blk)) + 2 + (len(picks) - 1) * (rows // blk) ** 2
    specs = [pl.BlockSpec((rows, rows), functools.partial(lambda t, i, where: (0, where[t]), t)) for t in picks]
    specs.insert(1, pl.BlockSpec((1, rows // 2, samples), lambda i, where: (where[1], where[2], 0)))
    args = [cost_rows] * len(picks)
    args.insert(1, parent_state)
    return call(
        functools.partial(pack_kernel, blk),
        (1,),
        1,
        specs,
        [whole(size, blk, blk)],
        [((size, blk, blk), F32)],
        "pack",
        after=after,
    )(where, *args)[0]


def front(message, size):
    shape = (size,) + message.shape[1:]

    def kernel(x, out):
        out[...] = x[...]

    return call(kernel, (1,), 0, [whole(*shape)], [whole(*shape)], [(shape, F32)], "front")(message)[0]


def unpack(tiles, step, n, xh, xl):
    blk = tiles.shape[1]
    lead = len(lower(n))
    for t, (i, j) in enumerate(lower(n) if step == 0 else [(i, j) for i in range(n) for j in range(n)]):
        tile = tiles[t if step == 0 else lead + 2 + (step - 1) * n * n + t]
        places = [(i, j, tile)] + ([(j, i, tile.T)] if step == 0 and i != j else [])
        for r, c, value in places:
            at = slice(r * blk, (r + 1) * blk), slice(c * blk, (c + 1) * blk)
            xh[at], xl[at] = split(value)


def collect_kernel(where, pair, mid, end, mid_last, end_last, out):
    out[:2] = pair[...]

    @pl.when(where[0] == 1)
    def _():
        out[2:4] = end[...]
        out[4:6] = end_last[...]

    @pl.when(where[0] == 0)
    def _():
        out[2:4] = mid[...]
        out[4:6] = mid_last[...]


def collect(where, messages, after):
    blk = messages[0].shape[1]
    lead = messages[3].shape[0] // 2 - 1
    return call(
        collect_kernel,
        (1,),
        1,
        [pl.BlockSpec((2, blk, blk), lambda i, where: (lead, 0, 0))] * 5,
        [whole(6, blk, blk)],
        [((6, blk, blk), F32)],
        "collect",
        after=[after],
    )(where, *messages)[0]


def drift_kernel(where, own, mine, other, fh, fl, x_ref, out):
    g = pl.program_id(0)
    core = where[0]
    blk = mine.shape[1]
    rows = own.shape[1]

    @pl.when(g == 0)
    def _():
        x_ref[...] = own[0]

    for d in range(3):

        @pl.when(g == d + 1)
        def _():
            for t in range(2):
                x_ref[pl.ds(pl.multiple_of(core * (rows // 2) + t * blk, blk), blk)] = mine[2 * d + t]
                x_ref[pl.ds(pl.multiple_of((1 - core) * (rows // 2) + t * blk, blk), blk)] = other[2 * d + t]

    part = dot3((fh[...], fl[...]), split(x_ref[...]))

    @pl.when(g == 0)
    def _():
        out[...] = part

    @pl.when(g > 0)
    def _():
        out[...] += part


def drift(where, parent_state, mine, other, fh, fl, after):
    _, rows, samples = parent_state.shape
    count, blk, _ = mine.shape
    factor = pl.BlockSpec((rows, rows), lambda g, where: (where[1], where[1 + g]))
    return call(
        drift_kernel,
        (4,),
        1,
        [pl.BlockSpec((1, rows, samples), lambda g, where: (where[5], 0, 0))]
        + [whole(count, blk, blk)] * 2
        + [factor, factor],
        [pl.BlockSpec((rows, samples), lambda g, where: (where[1 + g], 0)), whole(rows, samples)],
        [((4 * rows, samples), F32), ((rows, samples), F32)],
        "drift",
        after=[after],
    )(where, parent_state, mine, other, fh, fl)


def passed(arrays, *after):
    return call(lambda *_: None, (1,), 0, [], [], [], "passed", after=after, through=arrays)()


def begin_kernel(steps, where, weight, p_ref, u, v, fh, fl, bh, bl, rest, s_out, g_out, h_out, mine, pair):
    g = pl.program_id(0)

    @pl.when(g < steps)
    def _():
        p = split(p_ref[...])
        part = dot3(u[...], p, NT)

        @pl.when(g == 0)
        def _():
            mine[...] = part

        @pl.when(g > 0)
        def _():
            mine[...] += part

        @pl.when(g != where[0])
        def _():
            rest[...] = dot3(v[...], p)

    @pl.when(g == steps)
    def _():
        pair[0], pair[1] = split(mine[...] * weight[0])
        orders = h_out.shape[0]
        h_out[...] = dot3(pair[:, :orders], (bh[...], bl[...]))

    @pl.when(g >= steps)
    def _():
        part = dot3(pair[...], (fh[...], fl[...]))
        orders = g_out.shape[0]
        s_out[...] = part[orders:]
        g_out[...] = part[:orders]


def begin(where, weight, cost_rows, u, fh, fl):
    rows, width = cost_rows.shape
    tall = u.shape[1]
    orders = tall - rows
    steps = width // rows
    tile = 512

    def early(g):
        return jnp.minimum(g, steps - 1)

    def late(g):
        return jnp.maximum(g - steps, 0)

    each = pl.BlockSpec((2, tall, rows), lambda g, *_: (0, 0, early(g)))
    own = pl.BlockSpec((2, tall, rows), lambda g, where, _: (0, 0, where[0]))
    factor = pl.BlockSpec((rows, tile), lambda g, where, _: (where[0], late(g)))
    control = pl.BlockSpec((rows, orders), lambda g, where, _: (where[0], width // orders))
    return call(
        functools.partial(begin_kernel, steps),
        (steps + width // tile,),
        2,
        [pl.BlockSpec((rows, rows), lambda g, *_: (0, early(g))), each, own, factor, factor, control, control],
        [
            pl.BlockSpec((tall, rows), lambda g, *_: (0, early(g))),
            pl.BlockSpec((rows, tile), lambda g, *_: (0, late(g))),
            pl.BlockSpec((orders, tile), lambda g, *_: (0, late(g))),
            whole(orders, orders),
        ],
        [((tall, width), F32), ((rows, width), F32), ((orders, width), F32), ((orders, orders), F32)],
        "begin",
        [pltpu.VMEM((tall, rows), F32), pltpu.VMEM((2, tall, rows), BF16)],
    )(where, weight, cost_rows, u, u, fh, fl, fh, fl)


def stage_kernel(options, size, where, weight, *refs):
    arrived = refs[:options]
    v, n_in, fh, fl, bh, bl, s_in, g_in, h_in, *refs = refs[options:]
    if size > 1:
        u, s_out, g_out, h_out, n_out, done, pair, xh, xl = refs
    else:
        s_out, g_out, h_out, done, pair, xh, xl = refs
    g = pl.program_id(0)
    n = xh.shape[0] // arrived[0].shape[1]
    for c in range(options):
        for t in range(size):

            @pl.when((g == t) & (where[0] == c))
            def _():
                unpack(arrived[c], t, n, xh, xl)

    @pl.when(g == 0)
    def _():
        done[...] = n_in[...] + dot3(v[...], (xh[...], xl[...]))

    if size > 1:

        @pl.when((g > 0) & (g < size))
        def _():
            x = xh[...], xl[...]
            done[...] += dot3(u[...], x, NT)
            n_out[...] = n_in[...] + dot3(v[...], x)

    @pl.when(g == size)
    def _():
        pair[0], pair[1] = split(done[...] * weight[0])
        orders = h_out.shape[0]
        h_out[...] = h_in[...] + dot3(pair[:, :orders], (bh[...], bl[...]))

    @pl.when(g >= size)
    def _():
        part = dot3(pair[...], (fh[...], fl[...]))
        orders = g_out.shape[0]
        s_out[...] = s_in[...] + part[orders:]
        g_out[...] = g_in[...] + part[:orders]


def stage(where, weight, arrived, size, u, n, fh, fl, sums, after=(), through=()):
    tall, width = n.shape
    rows, orders = sums[0].shape[0], sums[1].shape[0]
    tile = 512

    def place(g, where):
        return where[1 + jnp.minimum(g, size - 1)]

    def later(g, where):
        return where[1 + jnp.clip(g, 1, size - 1)]

    def turn(g):
        return jnp.maximum(g - size, 0)

    block = pl.BlockSpec((tall, rows), lambda g, where, _: (0, place(g, where)))
    beyond = pl.BlockSpec((tall, rows), lambda g, where, _: (0, later(g, where)))
    u_beyond = pl.BlockSpec((2, tall, rows), lambda g, where, _: (0, 0, later(g, where)))
    u_focus = pl.BlockSpec((2, tall, rows), lambda g, where, _: (0, 0, where[1]))
    factor = pl.BlockSpec((rows, tile), lambda g, where, _: (where[1], turn(g)))
    s_spec = pl.BlockSpec((rows, tile), lambda g, *_: (0, turn(g)))
    g_spec = pl.BlockSpec((orders, tile), lambda g, *_: (0, turn(g)))
    control = pl.BlockSpec((rows, orders), lambda g, where, _: (where[1], width // orders))
    first = 2 + len(arrived)
    more = size > 1
    return call(
        functools.partial(stage_kernel, len(arrived), size),
        (size + width // tile,),
        2,
        [whole(*x.shape) for x in arrived]
        + [u_focus, block, factor, factor, control, control, s_spec, g_spec, whole(orders, orders)]
        + [u_beyond] * more,
        [s_spec, g_spec, whole(orders, orders)] + [beyond] * more,
        [((rows, width), F32), ((orders, width), F32), ((orders, orders), F32)] + [((tall, width), F32)] * more,
        "stage",
        [pltpu.VMEM((tall, rows), F32), pltpu.VMEM((2, tall, rows), BF16)] + [pltpu.VMEM((rows, rows), BF16)] * 2,
        {first + 6: 0, first + 7: 1, first + 8: 2, **({first + 1: 3} if more else {})},
        after,
        through,
    )(where, weight, *arrived, u, n, fh, fl, fh, fl, *sums, *([u] if more else []))


def final_kernel(where, h_ref, g1, g2, s1, s2, q1, q2, d_ref, x_ref, y_ref, bh, bl, gain, out, reached, pair, q):
    n = pl.program_id(0)
    rows = out.shape[0]

    @pl.when(n == 0)
    def _():
        value = -dot3(split(h_ref[...]), split(g1[...] + g2[...]))
        gain[...] = value
        pair[0], pair[1] = split(value.T)
        q[...] = jnp.zeros_like(q)

    cross = split(q1[...] + q2[...])
    part = s1[...] + s2[...] + dot3(pair[...], cross)
    diag = lax.broadcasted_iota(jnp.int32, (rows, rows), 0) == lax.broadcasted_iota(jnp.int32, (rows, rows), 1)
    out[...] = part + jnp.where(diag & (n == where[0]), d_ref[...], 0.0)
    q[...] += dot3(cross, split(x_ref[...]))

    @pl.when(n == pl.num_programs(0) - 1)
    def _():
        u = -dot3(split(h_ref[...]), split(q[...]))
        reached[...] = y_ref[...] + dot3((bh[...], bl[...]), split(u))


def final(where, hinv, own, other, state_cost, x, y, fh, fl):
    rows, width = own[0].shape
    orders = own[1].shape[0]
    samples = x.shape[1]
    s_spec = pl.BlockSpec((rows, rows), lambda n, where: (0, n))
    g_spec = pl.BlockSpec((orders, rows), lambda n, where: (0, n))
    mine = pl.BlockSpec((orders, rows), lambda n, where: (0, where[0]))
    factor = pl.BlockSpec((rows, orders), lambda n, where: (where[0], width // orders))
    return call(
        final_kernel,
        (width // rows,),
        1,
        [whole(orders, orders), mine, mine, s_spec, s_spec, g_spec, g_spec, whole(1, rows)]
        + [pl.BlockSpec((rows, samples), lambda n, where: (n, 0)), whole(rows, samples), factor, factor],
        [whole(orders, rows), s_spec, whole(rows, samples)],
        [((orders, rows), F32), ((rows, width), F32), ((rows, samples), F32)],
        "final",
        [pltpu.VMEM((2, rows, orders), BF16), pltpu.VMEM((orders, samples), F32)],
    )(where, hinv, own[1], other[1], own[0], other[0], own[1], other[1], state_cost[None], x, y, fh, fl)


def image_kernel(where, weight, fh, fl, p_ref, out, acc):
    k = pl.program_id(0)
    part = dot3(split(p_ref[...]), (fh[...], fl[...]))

    @pl.when(k == 0)
    def _():
        acc[...] = part

    @pl.when(k > 0)
    def _():
        acc[...] += part

    @pl.when(k == pl.num_programs(0) - 1)
    def _():
        out[...] = acc[...].T * weight[0]


def image(where, weight, fh, fl, cost_rows):
    rows, width = cost_rows.shape
    chunk = 512
    factor = pl.BlockSpec((chunk, rows), lambda k, where, _: (k, where[0]))
    return call(
        image_kernel,
        (width // chunk,),
        2,
        [factor, factor, pl.BlockSpec((rows, chunk), lambda k, *_: (0, k))],
        [whole(rows, rows)],
        [((rows, rows), F32)],
        "image",
        [pltpu.VMEM((rows, rows), F32)],
    )(where, weight, fh, fl, cost_rows)[0]


def accumulate_kernel(first, where, y_ref, fh, fl, *refs):
    out = refs[-1]
    part = dot3(split(y_ref[...]), (fh[...], fl[...]))
    out[...] = part if first else refs[0][...] + part


def accumulate(where, y, fh, fl, acc):
    rows = y.shape[0]
    total = fh.shape[1]
    tile = 512
    first = acc is None
    spec = pl.BlockSpec((rows, tile), lambda n, where: (0, n))
    factor = pl.BlockSpec((rows, tile), lambda n, where: (where[0], n))
    return call(
        functools.partial(accumulate_kernel, first),
        (total // tile,),
        1,
        [whole(rows, rows), factor, factor] + [spec] * (not first),
        [spec],
        [((rows, total), F32)],
        "accumulate",
        aliases=None if first else {4: 0},
    )(where, y, fh, fl, *(() if first else (acc,)))[0]


def by_images(z, parts, weight, cost_rows, fh, fl):
    rows, width = cost_rows.shape
    acc = None
    for d in range(parts):
        block = image(((z + d) % parts)[None], weight, fh, fl, cost_rows)
        if d:
            block = lax.ppermute(block, "row", [(i, (i + d) % parts) for i in range(parts)])
        acc = accumulate(((z - d) % parts)[None], block, fh, fl, acc)
    cross = lax.all_gather(acc[:, width:], "row")
    return acc[:, :width], jnp.swapaxes(cross.reshape(width, -1), 0, 1)


def by_blocks(z, core, parent, weight, cost_rows, parent_state, dense_parts, control_cost, messages):
    fh, fl, u = dense_parts
    edge = ((z == 0) | (z == 3)).astype(jnp.int32)
    left = z < 2
    second, third = jnp.where(left, 2, 1), jnp.where(left, 3, 0)
    pair, mid = messages
    lead = 2 * mid.shape[0] - pair.shape[0]

    def moved(x, *pairs):
        return lax.ppermute(x, "row", pairs)

    def across(x):
        return moved(x, (1, 2), (2, 1))

    def to_end(x):
        return moved(x, (1, 0), (2, 3))

    pair = moved(pair, (0, 1), (1, 0), (2, 3), (3, 2))
    mid = across(mid)
    n, *sums = begin(z[None], weight, cost_rows, u, fh, fl)
    (mid,) = passed([mid], n)
    end = to_end(mid)
    mid_last = across(front(pair, lead))
    where = jnp.stack([z * 0, z ^ 1, second, third])
    *sums, n = stage(where, weight, [pair], 3, u, n, fh, fl, sums)
    (mid_last,) = passed([mid_last], n)
    end_last = to_end(mid_last)
    where = jnp.stack([edge, second, third])
    *sums, n = stage(where, weight, [mid, end], 2, u, n, fh, fl, sums)
    halves = collect(edge[None], [pair, mid, end, mid_last, end_last], n)
    where = jnp.stack([edge, third])
    s, g, h = stage(where, weight, [mid_last, end_last], 1, u, n, fh, fl, sums, [halves])
    where = jnp.stack([core, z, z ^ 1, second, third, parent])
    x, y = drift(where, parent_state, halves, swapped(halves), fh, fl, h)
    other = swapped(h)
    return h, other, passed([s, g], other, y), x, y


def swapped(x):
    n = lax.axis_size("leaf")
    return lax.ppermute(x, "leaf", [(i, i ^ 1) for i in range(n)])


def shards(
    leaf_cost,
    a_blocks,
    a_cols,
    b_blocks,
    b_cols,
    branch_prob,
    state_cost,
    control_cost,
    parent_state,
):
    cost_rows = leaf_cost[0]
    rows, width = cost_rows.shape
    blk = a_blocks.shape[3]
    orders = control_cost.shape[0]
    parts = lax.axis_size("row")
    z = lax.axis_index("row")
    leaf = lax.axis_index("leaf")
    core = leaf % 2
    line = parts == 4 and rows == orders

    sent = []
    if line:
        left = z < 2
        near = jnp.where(left, 0, 3)
        lead = [z, leaf // 2, core]
        sent.append(pack(jnp.stack(lead + [jnp.where(left, 2, 1), 3 - near]), cost_rows, parent_state, blk, []))
        sent.append(pack(jnp.stack(lead + [near]), cost_rows, parent_state, blk, sent))
    fh, fl, u = parts_of = dense(z[None], rows, a_blocks[0], a_cols, b_blocks[0], b_cols, orders, sent)
    if line:
        h, other_h, own, x, y = by_blocks(
            z, core, leaf // 2, branch_prob, cost_rows, parent_state, parts_of, control_cost, sent
        )
    else:
        w = dot3(parted(cost_rows), (fh[:, width:], fl[:, width:]))
        b_rows = [lax.dynamic_slice(f, (0, z * rows), (orders, rows)) for f in u]
        h = lax.psum(dot3(b_rows, parted(w)) * branch_prob[0], "row")
        other_h = swapped(h)
        own = by_images(z, parts, branch_prob, cost_rows, fh, fl)
        own_state = lax.dynamic_index_in_dim(parent_state, leaf // 2, 0, keepdims=False)
        x = lax.all_gather(own_state, "row", tiled=True)
        y = dot3([lax.dynamic_slice(f, (z * rows, 0), (rows, width)) for f in (fh, fl)], parted(x))
    hinv = inverse(h, other_h, control_cost, blk)
    other = tuple(swapped(x) for x in own)
    gain, pcost, reached = final(z[None], hinv, own, other, state_cost, x, y, fh, fl)
    return pcost[None], gain[None], reached[None]


def solution(mesh):
    placed = (
        P("leaf", "row", None),
        P("leaf", None, None, None, None),
        P("leaf", None, None),
        P("leaf", None, None, None, None),
        P("leaf", None, None),
        P("leaf"),
        P("row"),
        P(),
        P(None, "row", None),
    )
    return jax.shard_map(
        shards,
        mesh=mesh,
        in_specs=placed,
        out_specs=(P("leaf", "row", None), P("leaf", None, "row"), P("leaf", "row", None)),
        check_vma=False,
    )
```

```python
import functools

import jax
import jax.numpy as jnp
from jax import lax
from jax.experimental import pallas as pl
from jax.experimental.pallas import tpu as pltpu
from jax.sharding import PartitionSpec as P

F32 = jnp.float32
BF16 = jnp.bfloat16
VMEM_LIMIT = 62 * 2**20
NN = (((1,), (0,)), ((), ()))
NT = (((1,), (1,)), ((), ()))


def split(x):
    hi = x.astype(BF16)
    return hi, (x - hi.astype(F32)).astype(BF16)


def parted(x):
    hi = lax.reduce_precision(x, 8, 7)
    return hi.astype(BF16), (x - hi).astype(BF16)


def dot3(a, b, dims=NN):
    one = functools.partial(lax.dot_general, dimension_numbers=dims, preferred_element_type=F32)
    rows = a[0].shape[0]
    both = jnp.concatenate(a, axis=0) if isinstance(a, (tuple, list)) else a.reshape(2 * rows, a.shape[2])
    part = one(both, b[0])
    return part[:rows] + (part[rows:] + one(a[0], b[1]))


BEGIN_TILE = (256, 512)
STAGE_TILE = (256, 256)


def multiply(out, a, b, dims, tile, add=None):
    right = dims[0][1][0]
    for m in range(0, out.shape[0], tile[0]):
        rows = slice(m, m + tile[0])
        for n in range(0, out.shape[1], tile[1]):
            cols = slice(n, n + tile[1])
            b_part = [x[:, cols] if right == 0 else x[cols] for x in b]
            value = dot3((a[0, rows], a[1, rows]), b_part, dims)
            out[rows, cols] = value if add is None else add[rows, cols] + value


def call(kernel, grid, prefetch, ins, outs, shapes, name, scratch=(), aliases=None, after=(), through=()):
    n_in, n_out = len(ins), len(outs)
    extra = len(after) + len(through)
    anywhere = pl.BlockSpec(memory_space=pl.ANY)

    def body(*refs):
        start = prefetch + n_in
        stop = start + extra + n_out
        kernel(*refs[:start], *refs[start + extra : stop], *refs[stop + len(through) :])

    aliases = dict(aliases or {})
    for t in range(len(through)):
        aliases[prefetch + n_in + len(after) + t] = n_out + t
    built = pl.pallas_call(
        body,
        grid_spec=pltpu.PrefetchScalarGridSpec(
            num_scalar_prefetch=prefetch,
            grid=grid,
            in_specs=list(ins) + [anywhere] * extra,
            out_specs=list(outs) + [anywhere] * len(through),
            scratch_shapes=scratch,
        ),
        out_shape=[jax.ShapeDtypeStruct(shape, kind) for shape, kind in shapes]
        + [jax.ShapeDtypeStruct(x.shape, x.dtype) for x in through],
        input_output_aliases=aliases,
        compiler_params=pltpu.CompilerParams(vmem_limit_bytes=VMEM_LIMIT),
        cost_estimate=pl.CostEstimate(flops=1, bytes_accessed=1, transcendentals=0),
        name=name,
    )
    return lambda *args: built(*args, *after, *through)


def whole(*shape):
    return pl.BlockSpec(shape, lambda *_: (0,) * len(shape))


def lower(n):
    return [(i, j) for i in range(n) for j in range(i + 1)]


def dense_kernel(blk, step, width, where, acol, bcol, a_ref, b_ref, fh, fl, u):
    i = pl.program_id(0)
    orders = fh.shape[1] - width
    rows = u.shape[1] - orders
    for ref in (fh, fl):
        ref[...] = jnp.zeros_like(ref)
    diag = lax.broadcasted_iota(jnp.int32, (blk, blk), 0) == lax.broadcasted_iota(jnp.int32, (blk, blk), 1)
    eye = jnp.where(diag, 0.75, 0.0).astype(F32)
    for t in range(step // blk):
        row = i * (step // blk) + t
        at = slice(t * blk, (t + 1) * blk)
        for s in range(a_ref.shape[1]):
            col = acol[0, row, s]
            block = a_ref[t, s] + eye if s == 0 else a_ref[t, s]
            to = pl.ds(pl.multiple_of(col * blk, blk), blk)
            fh[at, to], fl[at, to] = split(block)
        for s in range(b_ref.shape[1]):
            to = pl.ds(pl.multiple_of(width + bcol[0, row, s] * blk, blk), blk)
            fh[at, to], fl[at, to] = split(b_ref[t, s])

    own = pl.ds(pl.multiple_of(where[0] * rows, rows), rows)
    for p, f in enumerate((fh, fl)):
        for to, cols in ((slice(0, orders), slice(width, None)), (slice(orders, None), own)):
            part = f[:, cols]
            n = part.shape[1]
            diag = lax.broadcasted_iota(jnp.int32, (n, n), 0) == lax.broadcasted_iota(jnp.int32, (n, n), 1)
            one = jnp.where(diag, 1.0, 0.0).astype(BF16)
            u[p, to] = lax.dot_general(one, part, NT, preferred_element_type=F32).astype(BF16)


def dense(where, rows, a_blocks, a_cols, b_blocks, b_cols, orders, after):
    count, nnza, blk, _ = a_blocks.shape
    nnzb = b_blocks.shape[1]
    width = count * blk
    step = 2 * blk
    total = width + orders
    factor = pl.BlockSpec((step, total), lambda i, *_: (i, 0))
    turned = pl.BlockSpec((2, rows + orders, step), lambda i, *_: (0, 0, i))
    return call(
        functools.partial(dense_kernel, blk, step, width),
        (width // step,),
        3,
        [
            pl.BlockSpec((2, nnza, blk, blk), lambda i, *_: (i, 0, 0, 0)),
            pl.BlockSpec((2, nnzb, blk, blk), lambda i, *_: (i, 0, 0, 0)),
        ],
        [factor, factor, turned],
        [((width, total), BF16)] * 2 + [((2, rows + orders, width), BF16)],
        "dense",
        after=after,
    )(where, a_cols, b_cols, a_blocks, b_blocks)


def inverse_block(m):
    n = m.shape[0]
    sub = lax.broadcasted_iota(jnp.int32, (8, n), 0)
    lane = lax.broadcasted_iota(jnp.int32, (8, n), 1)
    strips = [m[i : i + 8] for i in range(0, n, 8)]

    def along(v, j):
        return jnp.broadcast_to(v[:, j : j + 1], (8, n))

    def down(v, t):
        return jnp.broadcast_to(v[t : t + 1], (8, n))

    for q in range(n // 8):
        panel = strips[q]
        cols = [along(panel, 8 * q + b) for b in range(8)]
        for t in range(8):
            here = sub == t
            inv = 1.0 / down(cols[t], t)

            def reduced(v):
                r = down(v, t) * inv
                return jnp.where(here, r, v - cols[t] * r)

            panel = reduced(jnp.where(lane == 8 * q + t, jnp.where(here, 1.0, 0.0), panel))
            cols[t + 1 :] = [reduced(v) for v in cols[t + 1 :]]
        inside = (lane >= 8 * q) & (lane < 8 * q + 8)
        rows = [down(panel, b) for b in range(8)]
        for i in range(q + 1, q + n // 8):
            old = strips[i % (n // 8)]
            terms = [along(old, 8 * q + b) * rows[b] for b in range(8)]
            while len(terms) > 1:
                terms = [x + y for x, y in zip(terms[::2], terms[1::2])]
            strips[i % (n // 8)] = jnp.where(inside, 0.0, old) - terms[0]
        strips[q] = panel
    return jnp.concatenate(strips, axis=0)


def inverse_kernel(blk, mine, other, d_ref, out):
    n = out.shape[0]
    def dot(a, b):
        return dot3(split(a), split(b))

    diag = lax.broadcasted_iota(jnp.int32, (n, n), 0) == lax.broadcasted_iota(jnp.int32, (n, n), 1)
    out[...] = mine[...] + other[...] + jnp.where(diag, d_ref[...], 0.0)

    place = lax.broadcasted_iota(jnp.int32, (n, blk), 0) // blk

    @pl.loop(0, n // blk)
    def _(b):
        here = pl.ds(pl.multiple_of(b * blk, blk), blk)
        inv = inverse_block(out[here, here])
        row = dot(inv, out[here, :])
        out[...] -= dot(out[:, here], row)
        col = row.T
        out[:, here] = jnp.where(place < b, col, -col)
        out[here, :] = row
        out[here, here] = inv


def inverse(mine, other, control_cost, blk):
    n = control_cost.shape[0]
    return call(
        functools.partial(inverse_kernel, blk),
        (1,),
        0,
        [whole(n, n)] * 2 + [whole(1, n)],
        [whole(n, n)],
        [((n, n), F32)],
        "inverse",
    )(mine, other, control_cost[None])[0]


def tiled(block, blk):
    n = block.shape[0] // blk
    return [block[i * blk : (i + 1) * blk, j * blk : (j + 1) * blk] for i in range(n) for j in range(n)]


def pack_kernel(blk, where, own, x_ref, *refs):
    *blocks, out = refs
    diag = [own[i * blk : (i + 1) * blk, j * blk : (j + 1) * blk] for i, j in lower(own.shape[0] // blk)]
    x = [x_ref[0, :blk], x_ref[0, blk:]]
    for t, tile in enumerate(diag + x + [tile for block in blocks for tile in tiled(block, blk)]):
        out[t] = tile


def pack(where, cost_rows, parent_state, blk, after):
    rows = cost_rows.shape[0]
    samples = parent_state.shape[2]
    picks = [0] + list(range(3, where.shape[0]))
    size = len(lower(rows // blk)) + 2 + (len(picks) - 1) * (rows // blk) ** 2
    specs = [pl.BlockSpec((rows, rows), functools.partial(lambda t, i, where: (0, where[t]), t)) for t in picks]
    specs.insert(1, pl.BlockSpec((1, rows // 2, samples), lambda i, where: (where[1], where[2], 0)))
    args = [cost_rows] * len(picks)
    args.insert(1, parent_state)
    return call(
        functools.partial(pack_kernel, blk),
        (1,),
        1,
        specs,
        [whole(size, blk, blk)],
        [((size, blk, blk), F32)],
        "pack",
        after=after,
    )(where, *args)[0]


def front(message, size):
    shape = (size,) + message.shape[1:]

    def kernel(x, out):
        out[...] = x[...]

    return call(kernel, (1,), 0, [whole(*shape)], [whole(*shape)], [(shape, F32)], "front")(message)[0]


def unpack(tiles, step, n, xh, xl):
    blk = tiles.shape[1]
    lead = len(lower(n))
    for t, (i, j) in enumerate(lower(n) if step == 0 else [(i, j) for i in range(n) for j in range(n)]):
        tile = tiles[t if step == 0 else lead + 2 + (step - 1) * n * n + t]
        places = [(i, j, tile)] + ([(j, i, tile.T)] if step == 0 and i != j else [])
        for r, c, value in places:
            at = slice(r * blk, (r + 1) * blk), slice(c * blk, (c + 1) * blk)
            xh[at], xl[at] = split(value)


def collect_kernel(where, pair, mid, end, mid_last, end_last, out):
    out[:2] = pair[...]

    @pl.when(where[0] == 1)
    def _():
        out[2:4] = end[...]
        out[4:6] = end_last[...]

    @pl.when(where[0] == 0)
    def _():
        out[2:4] = mid[...]
        out[4:6] = mid_last[...]


def collect(where, messages, after):
    blk = messages[0].shape[1]
    lead = messages[3].shape[0] // 2 - 1
    return call(
        collect_kernel,
        (1,),
        1,
        [pl.BlockSpec((2, blk, blk), lambda i, where: (lead, 0, 0))] * 5,
        [whole(6, blk, blk)],
        [((6, blk, blk), F32)],
        "collect",
        after=[after],
    )(where, *messages)[0]


def drift_kernel(where, own, mine, other, fh, fl, x_ref, out):
    g = pl.program_id(0)
    core = where[0]
    blk = mine.shape[1]
    rows = own.shape[1]

    @pl.when(g == 0)
    def _():
        x_ref[...] = own[0]

    for d in range(3):

        @pl.when(g == d + 1)
        def _():
            for t in range(2):
                x_ref[pl.ds(pl.multiple_of(core * (rows // 2) + t * blk, blk), blk)] = mine[2 * d + t]
                x_ref[pl.ds(pl.multiple_of((1 - core) * (rows // 2) + t * blk, blk), blk)] = other[2 * d + t]

    part = dot3((fh[...], fl[...]), split(x_ref[...]))

    @pl.when(g == 0)
    def _():
        out[...] = part

    @pl.when(g > 0)
    def _():
        out[...] += part


def drift(where, parent_state, mine, other, fh, fl, after):
    _, rows, samples = parent_state.shape
    count, blk, _ = mine.shape
    factor = pl.BlockSpec((rows, rows), lambda g, where: (where[1], where[1 + g]))
    return call(
        drift_kernel,
        (4,),
        1,
        [pl.BlockSpec((1, rows, samples), lambda g, where: (where[5], 0, 0))]
        + [whole(count, blk, blk)] * 2
        + [factor, factor],
        [pl.BlockSpec((rows, samples), lambda g, where: (where[1 + g], 0)), whole(rows, samples)],
        [((4 * rows, samples), F32), ((rows, samples), F32)],
        "drift",
        after=[after],
    )(where, parent_state, mine, other, fh, fl)


def passed(arrays, *after):
    return call(lambda *_: None, (1,), 0, [], [], [], "passed", after=after, through=arrays)()


def begin_kernel(steps, where, weight, p_ref, u, v, fh, fl, bh, bl, rest, s_out, g_out, h_out, mine, pair, ph, pl_):
    g = pl.program_id(0)

    @pl.when(g < steps)
    def _():
        ph[...], pl_[...] = split(p_ref[...])

        @pl.when(g == 0)
        def _():
            multiply(mine, u, (ph, pl_), NT, BEGIN_TILE)

        @pl.when(g > 0)
        def _():
            multiply(mine, u, (ph, pl_), NT, BEGIN_TILE, mine)

        @pl.when(g != where[0])
        def _():
            multiply(rest, v, (ph, pl_), NN, BEGIN_TILE)

    @pl.when(g == steps)
    def _():
        pair[0], pair[1] = split(mine[...] * weight[0])
        orders = h_out.shape[0]
        h_out[...] = dot3(pair[:, :orders], (bh[...], bl[...]))

    @pl.when(g >= steps)
    def _():
        orders = g_out.shape[0]
        multiply(g_out, pair.at[:, :orders], (fh, fl), NN, BEGIN_TILE)
        multiply(s_out, pair.at[:, orders:], (fh, fl), NN, BEGIN_TILE)


def begin(where, weight, cost_rows, u, fh, fl):
    rows, width = cost_rows.shape
    tall = u.shape[1]
    orders = tall - rows
    steps = width // rows
    tile = 512

    def early(g):
        return jnp.minimum(g, steps - 1)

    def late(g):
        return jnp.maximum(g - steps, 0)

    each = pl.BlockSpec((2, tall, rows), lambda g, *_: (0, 0, early(g)))
    own = pl.BlockSpec((2, tall, rows), lambda g, where, _: (0, 0, where[0]))
    factor = pl.BlockSpec((rows, tile), lambda g, where, _: (where[0], late(g)))
    control = pl.BlockSpec((rows, orders), lambda g, where, _: (where[0], width // orders))
    return call(
        functools.partial(begin_kernel, steps),
        (steps + width // tile,),
        2,
        [pl.BlockSpec((rows, rows), lambda g, *_: (0, early(g))), each, own, factor, factor, control, control],
        [
            pl.BlockSpec((tall, rows), lambda g, *_: (0, early(g))),
            pl.BlockSpec((rows, tile), lambda g, *_: (0, late(g))),
            pl.BlockSpec((orders, tile), lambda g, *_: (0, late(g))),
            whole(orders, orders),
        ],
        [((tall, width), F32), ((rows, width), F32), ((orders, width), F32), ((orders, orders), F32)],
        "begin",
        [pltpu.VMEM((tall, rows), F32), pltpu.VMEM((2, tall, rows), BF16)] + [pltpu.VMEM((rows, rows), BF16)] * 2,
    )(where, weight, cost_rows, u, u, fh, fl, fh, fl)


def stage_kernel(options, size, where, weight, *refs):
    arrived = refs[:options]
    v, n_in, fh, fl, bh, bl, s_in, g_in, h_in, *refs = refs[options:]
    if size > 1:
        u, s_out, g_out, h_out, n_out, done, pair, xh, xl = refs
    else:
        s_out, g_out, h_out, done, pair, xh, xl = refs
    g = pl.program_id(0)
    n = xh.shape[0] // arrived[0].shape[1]
    for c in range(options):
        for t in range(size):

            @pl.when((g == t) & (where[0] == c))
            def _():
                unpack(arrived[c], t, n, xh, xl)

    @pl.when(g == 0)
    def _():
        multiply(done, v, (xh, xl), NN, STAGE_TILE, n_in)

    if size > 1:

        @pl.when((g > 0) & (g < size))
        def _():
            multiply(done, u, (xh, xl), NT, STAGE_TILE, done)
            multiply(n_out, v, (xh, xl), NN, STAGE_TILE, n_in)

    @pl.when(g == size)
    def _():
        pair[0], pair[1] = split(done[...] * weight[0])
        orders = h_out.shape[0]
        h_out[...] = h_in[...] + dot3(pair[:, :orders], (bh[...], bl[...]))

    @pl.when(g >= size)
    def _():
        orders = g_out.shape[0]
        multiply(g_out, pair.at[:, :orders], (fh, fl), NN, STAGE_TILE, g_in)
        multiply(s_out, pair.at[:, orders:], (fh, fl), NN, STAGE_TILE, s_in)


def stage(where, weight, arrived, size, u, n, fh, fl, sums, after=(), through=()):
    tall, width = n.shape
    rows, orders = sums[0].shape[0], sums[1].shape[0]
    tile = 512

    def place(g, where):
        return where[1 + jnp.minimum(g, size - 1)]

    def later(g, where):
        return where[1 + jnp.clip(g, 1, size - 1)]

    def turn(g):
        return jnp.maximum(g - size, 0)

    block = pl.BlockSpec((tall, rows), lambda g, where, _: (0, place(g, where)))
    beyond = pl.BlockSpec((tall, rows), lambda g, where, _: (0, later(g, where)))
    u_beyond = pl.BlockSpec((2, tall, rows), lambda g, where, _: (0, 0, later(g, where)))
    u_focus = pl.BlockSpec((2, tall, rows), lambda g, where, _: (0, 0, where[1]))
    factor = pl.BlockSpec((rows, tile), lambda g, where, _: (where[1], turn(g)))
    s_spec = pl.BlockSpec((rows, tile), lambda g, *_: (0, turn(g)))
    g_spec = pl.BlockSpec((orders, tile), lambda g, *_: (0, turn(g)))
    control = pl.BlockSpec((rows, orders), lambda g, where, _: (where[1], width // orders))
    first = 2 + len(arrived)
    more = size > 1
    return call(
        functools.partial(stage_kernel, len(arrived), size),
        (size + width // tile,),
        2,
        [whole(*x.shape) for x in arrived]
        + [u_focus, block, factor, factor, control, control, s_spec, g_spec, whole(orders, orders)]
        + [u_beyond] * more,
        [s_spec, g_spec, whole(orders, orders)] + [beyond] * more,
        [((rows, width), F32), ((orders, width), F32), ((orders, orders), F32)] + [((tall, width), F32)] * more,
        "stage",
        [pltpu.VMEM((tall, rows), F32), pltpu.VMEM((2, tall, rows), BF16)] + [pltpu.VMEM((rows, rows), BF16)] * 2,
        {first + 6: 0, first + 7: 1, first + 8: 2, **({first + 1: 3} if more else {})},
        after,
        through,
    )(where, weight, *arrived, u, n, fh, fl, fh, fl, *sums, *([u] if more else []))


def final_kernel(where, h_ref, g1, g2, s1, s2, q1, q2, d_ref, x_ref, y_ref, bh, bl, gain, out, reached, pair, q):
    n = pl.program_id(0)
    rows = out.shape[0]

    @pl.when(n == 0)
    def _():
        value = -dot3(split(h_ref[...]), split(g1[...] + g2[...]))
        gain[...] = value
        pair[0], pair[1] = split(value.T)
        q[...] = jnp.zeros_like(q)

    cross = split(q1[...] + q2[...])
    part = s1[...] + s2[...] + dot3(pair[...], cross)
    diag = lax.broadcasted_iota(jnp.int32, (rows, rows), 0) == lax.broadcasted_iota(jnp.int32, (rows, rows), 1)
    out[...] = part + jnp.where(diag & (n == where[0]), d_ref[...], 0.0)
    q[...] += dot3(cross, split(x_ref[...]))

    @pl.when(n == pl.num_programs(0) - 1)
    def _():
        u = -dot3(split(h_ref[...]), split(q[...]))
        reached[...] = y_ref[...] + dot3((bh[...], bl[...]), split(u))


def final(where, hinv, own, other, state_cost, x, y, fh, fl):
    rows, width = own[0].shape
    orders = own[1].shape[0]
    samples = x.shape[1]
    s_spec = pl.BlockSpec((rows, rows), lambda n, where: (0, n))
    g_spec = pl.BlockSpec((orders, rows), lambda n, where: (0, n))
    mine = pl.BlockSpec((orders, rows), lambda n, where: (0, where[0]))
    factor = pl.BlockSpec((rows, orders), lambda n, where: (where[0], width // orders))
    return call(
        final_kernel,
        (width // rows,),
        1,
        [whole(orders, orders), mine, mine, s_spec, s_spec, g_spec, g_spec, whole(1, rows)]
        + [pl.BlockSpec((rows, samples), lambda n, where: (n, 0)), whole(rows, samples), factor, factor],
        [whole(orders, rows), s_spec, whole(rows, samples)],
        [((orders, rows), F32), ((rows, width), F32), ((rows, samples), F32)],
        "final",
        [pltpu.VMEM((2, rows, orders), BF16), pltpu.VMEM((orders, samples), F32)],
    )(where, hinv, own[1], other[1], own[0], other[0], own[1], other[1], state_cost[None], x, y, fh, fl)


def image_kernel(where, weight, fh, fl, p_ref, out, acc):
    k = pl.program_id(0)
    part = dot3(split(p_ref[...]), (fh[...], fl[...]))

    @pl.when(k == 0)
    def _():
        acc[...] = part

    @pl.when(k > 0)
    def _():
        acc[...] += part

    @pl.when(k == pl.num_programs(0) - 1)
    def _():
        out[...] = acc[...].T * weight[0]


def image(where, weight, fh, fl, cost_rows):
    rows, width = cost_rows.shape
    chunk = 512
    factor = pl.BlockSpec((chunk, rows), lambda k, where, _: (k, where[0]))
    return call(
        image_kernel,
        (width // chunk,),
        2,
        [factor, factor, pl.BlockSpec((rows, chunk), lambda k, *_: (0, k))],
        [whole(rows, rows)],
        [((rows, rows), F32)],
        "image",
        [pltpu.VMEM((rows, rows), F32)],
    )(where, weight, fh, fl, cost_rows)[0]


def accumulate_kernel(first, where, y_ref, fh, fl, *refs):
    out = refs[-1]
    part = dot3(split(y_ref[...]), (fh[...], fl[...]))
    out[...] = part if first else refs[0][...] + part


def accumulate(where, y, fh, fl, acc):
    rows = y.shape[0]
    total = fh.shape[1]
    tile = 512
    first = acc is None
    spec = pl.BlockSpec((rows, tile), lambda n, where: (0, n))
    factor = pl.BlockSpec((rows, tile), lambda n, where: (where[0], n))
    return call(
        functools.partial(accumulate_kernel, first),
        (total // tile,),
        1,
        [whole(rows, rows), factor, factor] + [spec] * (not first),
        [spec],
        [((rows, total), F32)],
        "accumulate",
        aliases=None if first else {4: 0},
    )(where, y, fh, fl, *(() if first else (acc,)))[0]


def by_images(z, parts, weight, cost_rows, fh, fl):
    rows, width = cost_rows.shape
    acc = None
    for d in range(parts):
        block = image(((z + d) % parts)[None], weight, fh, fl, cost_rows)
        if d:
            block = lax.ppermute(block, "row", [(i, (i + d) % parts) for i in range(parts)])
        acc = accumulate(((z - d) % parts)[None], block, fh, fl, acc)
    cross = lax.all_gather(acc[:, width:], "row")
    return acc[:, :width], jnp.swapaxes(cross.reshape(width, -1), 0, 1)


def by_blocks(z, core, parent, weight, cost_rows, parent_state, dense_parts, control_cost, messages):
    fh, fl, u = dense_parts
    edge = ((z == 0) | (z == 3)).astype(jnp.int32)
    left = z < 2
    second, third = jnp.where(left, 2, 1), jnp.where(left, 3, 0)
    pair, mid = messages
    lead = 2 * mid.shape[0] - pair.shape[0]

    def moved(x, *pairs):
        return lax.ppermute(x, "row", pairs)

    def across(x):
        return moved(x, (1, 2), (2, 1))

    def to_end(x):
        return moved(x, (1, 0), (2, 3))

    pair = moved(pair, (0, 1), (1, 0), (2, 3), (3, 2))
    mid = across(mid)
    n, *sums = begin(z[None], weight, cost_rows, u, fh, fl)
    (mid,) = passed([mid], n)
    end = to_end(mid)
    mid_last = across(front(pair, lead))
    where = jnp.stack([z * 0, z ^ 1, second, third])
    *sums, n = stage(where, weight, [pair], 3, u, n, fh, fl, sums)
    (mid_last,) = passed([mid_last], n)
    end_last = to_end(mid_last)
    where = jnp.stack([edge, second, third])
    *sums, n = stage(where, weight, [mid, end], 2, u, n, fh, fl, sums)
    halves = collect(edge[None], [pair, mid, end, mid_last, end_last], n)
    where = jnp.stack([edge, third])
    s, g, h = stage(where, weight, [mid_last, end_last], 1, u, n, fh, fl, sums, [halves])
    where = jnp.stack([core, z, z ^ 1, second, third, parent])
    x, y = drift(where, parent_state, halves, swapped(halves), fh, fl, h)
    other = swapped(h)
    return h, other, passed([s, g], other, y), x, y


def swapped(x):
    n = lax.axis_size("leaf")
    return lax.ppermute(x, "leaf", [(i, i ^ 1) for i in range(n)])


def shards(
    leaf_cost,
    a_blocks,
    a_cols,
    b_blocks,
    b_cols,
    branch_prob,
    state_cost,
    control_cost,
    parent_state,
):
    cost_rows = leaf_cost[0]
    rows, width = cost_rows.shape
    blk = a_blocks.shape[3]
    orders = control_cost.shape[0]
    parts = lax.axis_size("row")
    z = lax.axis_index("row")
    leaf = lax.axis_index("leaf")
    core = leaf % 2
    line = parts == 4 and rows == orders

    sent = []
    if line:
        left = z < 2
        near = jnp.where(left, 0, 3)
        lead = [z, leaf // 2, core]
        sent.append(pack(jnp.stack(lead + [jnp.where(left, 2, 1), 3 - near]), cost_rows, parent_state, blk, []))
        sent.append(pack(jnp.stack(lead + [near]), cost_rows, parent_state, blk, sent))
    fh, fl, u = parts_of = dense(z[None], rows, a_blocks[0], a_cols, b_blocks[0], b_cols, orders, sent)
    if line:
        h, other_h, own, x, y = by_blocks(
            z, core, leaf // 2, branch_prob, cost_rows, parent_state, parts_of, control_cost, sent
        )
    else:
        w = dot3(parted(cost_rows), (fh[:, width:], fl[:, width:]))
        b_rows = [lax.dynamic_slice(f, (0, z * rows), (orders, rows)) for f in u]
        h = lax.psum(dot3(b_rows, parted(w)) * branch_prob[0], "row")
        other_h = swapped(h)
        own = by_images(z, parts, branch_prob, cost_rows, fh, fl)
        own_state = lax.dynamic_index_in_dim(parent_state, leaf // 2, 0, keepdims=False)
        x = lax.all_gather(own_state, "row", tiled=True)
        y = dot3([lax.dynamic_slice(f, (z * rows, 0), (rows, width)) for f in (fh, fl)], parted(x))
    hinv = inverse(h, other_h, control_cost, blk)
    other = tuple(swapped(x) for x in own)
    gain, pcost, reached = final(z[None], hinv, own, other, state_cost, x, y, fh, fl)
    return pcost[None], gain[None], reached[None]


def solution(mesh):
    placed = (
        P("leaf", "row", None),
        P("leaf", None, None, None, None),
        P("leaf", None, None),
        P("leaf", None, None, None, None),
        P("leaf", None, None),
        P("leaf"),
        P("row"),
        P(),
        P(None, "row", None),
    )
    return jax.shard_map(
        shards,
        mesh=mesh,
        in_specs=placed,
        out_specs=(P("leaf", "row", None), P("leaf", None, "row"), P("leaf", "row", None)),
        check_vma=False,
    )
```

```python
import functools

import jax
import jax.numpy as jnp
from jax import lax
from jax.experimental import pallas as pl
from jax.experimental.pallas import tpu as pltpu
from jax.sharding import PartitionSpec as P

F32 = jnp.float32
BF16 = jnp.bfloat16
VMEM_LIMIT = 24 * 2**20
NN = (((1,), (0,)), ((), ()))
NT = (((1,), (1,)), ((), ()))


def split(x):
    hi = x.astype(BF16)
    return hi, (x - hi.astype(F32)).astype(BF16)


def parted(x):
    hi = lax.reduce_precision(x, 8, 7)
    return hi.astype(BF16), (x - hi).astype(BF16)


def dot3(a, b, dims=NN):
    one = functools.partial(lax.dot_general, dimension_numbers=dims, preferred_element_type=F32)
    rows = a[0].shape[0]
    both = jnp.concatenate(a, axis=0) if isinstance(a, (tuple, list)) else a.reshape(2 * rows, a.shape[2])
    part = one(both, b[0])
    return part[:rows] + (part[rows:] + one(a[0], b[1]))


TILE = (256, 512)
VMEM = pltpu.VMEM
STAYS = pl.BlockSpec(memory_space=VMEM)


def resident(x):
    return pltpu.with_memory_space_constraint(x, VMEM)


def outside(x):
    return pltpu.with_memory_space_constraint(x, pltpu.HBM)


def column(ref, i, size):
    return ref.at[..., pl.ds(pl.multiple_of(i * size, size), size)]


def multiply(out, a, b, dims, add=None):
    right = dims[0][1][0]
    for m in range(0, out.shape[0], TILE[0]):
        rows = slice(m, m + TILE[0])
        for n in range(0, out.shape[1], TILE[1]):
            cols = slice(n, n + TILE[1])
            b_part = [x[:, cols] if right == 0 else x[cols] for x in b]
            value = dot3((a[0, rows], a[1, rows]), b_part, dims)
            out[rows, cols] = value if add is None else add[rows, cols] + value


def call(kernel, grid, prefetch, ins, outs, shapes, name, scratch=(), aliases=None, after=(), through=(), keep=False):
    n_in, n_out = len(ins), len(outs)
    extra = len(after) + len(through)
    anywhere = pl.BlockSpec(memory_space=pl.ANY)

    def body(*refs):
        start = prefetch + n_in
        stop = start + extra + n_out
        kernel(*refs[:start], *refs[start + extra : stop], *refs[stop + len(through) :])

    aliases = dict(aliases or {})
    for t in range(len(through)):
        aliases[prefetch + n_in + len(after) + t] = n_out + t
    built = pl.pallas_call(
        body,
        grid_spec=pltpu.PrefetchScalarGridSpec(
            num_scalar_prefetch=prefetch,
            grid=grid,
            in_specs=list(ins) + [anywhere] * extra,
            out_specs=list(outs) + [anywhere] * len(through),
            scratch_shapes=scratch,
        ),
        out_shape=[x if isinstance(x, pl.MemoryRef) else jax.ShapeDtypeStruct(*x) for x in shapes]
        + [(VMEM if keep else jax.ShapeDtypeStruct)(x.shape, x.dtype) for x in through],
        input_output_aliases=aliases,
        compiler_params=pltpu.CompilerParams(vmem_limit_bytes=VMEM_LIMIT),
        cost_estimate=pl.CostEstimate(flops=1, bytes_accessed=1, transcendentals=0),
        name=name,
    )

    def run(*args):
        placed = [resident(x) if spec is STAYS else x for spec, x in zip(ins, args[prefetch:])]
        return built(*args[:prefetch], *placed, *after, *[resident(x) if keep else x for x in through])

    return run


def whole(*shape):
    return pl.BlockSpec(shape, lambda *_: (0,) * len(shape))


def lower(n):
    return [(i, j) for i in range(n) for j in range(i + 1)]


def dense_kernel(blk, step, width, where, acol, bcol, a_ref, b_ref, fh, fl, u):
    i = pl.program_id(0)
    orders = fh.shape[1] - width
    rows = u.shape[1] - orders
    for ref in (fh, fl):
        ref[...] = jnp.zeros_like(ref)
    diag = lax.broadcasted_iota(jnp.int32, (blk, blk), 0) == lax.broadcasted_iota(jnp.int32, (blk, blk), 1)
    eye = jnp.where(diag, 0.75, 0.0).astype(F32)
    for t in range(step // blk):
        row = i * (step // blk) + t
        at = slice(t * blk, (t + 1) * blk)
        for s in range(a_ref.shape[1]):
            col = acol[0, row, s]
            block = a_ref[t, s] + eye if s == 0 else a_ref[t, s]
            to = pl.ds(pl.multiple_of(col * blk, blk), blk)
            fh[at, to], fl[at, to] = split(block)
        for s in range(b_ref.shape[1]):
            to = pl.ds(pl.multiple_of(width + bcol[0, row, s] * blk, blk), blk)
            fh[at, to], fl[at, to] = split(b_ref[t, s])

    own = pl.ds(pl.multiple_of(where[0] * rows, rows), rows)
    for p, f in enumerate((fh, fl)):
        for to, cols in ((slice(0, orders), slice(width, None)), (slice(orders, None), own)):
            part = f[:, cols]
            n = part.shape[1]
            diag = lax.broadcasted_iota(jnp.int32, (n, n), 0) == lax.broadcasted_iota(jnp.int32, (n, n), 1)
            one = jnp.where(diag, 1.0, 0.0).astype(BF16)
            u[p, to, pl.ds(pl.multiple_of(i * step, step), step)] = lax.dot_general(one, part, NT, preferred_element_type=F32).astype(BF16)


def dense(where, rows, a_blocks, a_cols, b_blocks, b_cols, orders, after):
    count, nnza, blk, _ = a_blocks.shape
    nnzb = b_blocks.shape[1]
    width = count * blk
    step = 2 * blk
    total = width + orders
    factor = pl.BlockSpec((step, total), lambda i, *_: (i, 0))
    return call(
        functools.partial(dense_kernel, blk, step, width),
        (width // step,),
        3,
        [
            pl.BlockSpec((2, nnza, blk, blk), lambda i, *_: (i, 0, 0, 0)),
            pl.BlockSpec((2, nnzb, blk, blk), lambda i, *_: (i, 0, 0, 0)),
        ],
        [factor, factor, STAYS],
        [pltpu.HBM((width, total), BF16)] * 2 + [VMEM((2, rows + orders, width), BF16)],
        "dense",
        after=after,
    )(where, a_cols, b_cols, outside(a_blocks), outside(b_blocks))


def inverse_block(m):
    n = m.shape[0]
    sub = lax.broadcasted_iota(jnp.int32, (8, n), 0)
    lane = lax.broadcasted_iota(jnp.int32, (8, n), 1)
    strips = [m[i : i + 8] for i in range(0, n, 8)]

    def along(v, j):
        return jnp.broadcast_to(v[:, j : j + 1], (8, n))

    def down(v, t):
        return jnp.broadcast_to(v[t : t + 1], (8, n))

    for q in range(n // 8):
        panel = strips[q]
        cols = [along(panel, 8 * q + b) for b in range(8)]
        for t in range(8):
            here = sub == t
            inv = 1.0 / down(cols[t], t)

            def reduced(v):
                r = down(v, t) * inv
                return jnp.where(here, r, v - cols[t] * r)

            panel = reduced(jnp.where(lane == 8 * q + t, jnp.where(here, 1.0, 0.0), panel))
            cols[t + 1 :] = [reduced(v) for v in cols[t + 1 :]]
        inside = (lane >= 8 * q) & (lane < 8 * q + 8)
        rows = [down(panel, b) for b in range(8)]
        for i in range(q + 1, q + n // 8):
            old = strips[i % (n // 8)]
            terms = [along(old, 8 * q + b) * rows[b] for b in range(8)]
            while len(terms) > 1:
                terms = [x + y for x, y in zip(terms[::2], terms[1::2])]
            strips[i % (n // 8)] = jnp.where(inside, 0.0, old) - terms[0]
        strips[q] = panel
    return jnp.concatenate(strips, axis=0)


def inverse_kernel(blk, mine, other, d_ref, out):
    n = out.shape[0]
    def dot(a, b):
        return dot3(split(a), split(b))

    diag = lax.broadcasted_iota(jnp.int32, (n, n), 0) == lax.broadcasted_iota(jnp.int32, (n, n), 1)
    out[...] = mine[...] + other[...] + jnp.where(diag, d_ref[...], 0.0)

    place = lax.broadcasted_iota(jnp.int32, (n, blk), 0) // blk

    @pl.loop(0, n // blk)
    def _(b):
        here = pl.ds(pl.multiple_of(b * blk, blk), blk)
        inv = inverse_block(out[here, here])
        row = dot(inv, out[here, :])
        out[...] -= dot(out[:, here], row)
        col = row.T
        out[:, here] = jnp.where(place < b, col, -col)
        out[here, :] = row
        out[here, here] = inv


def inverse(mine, other, control_cost, blk):
    n = control_cost.shape[0]
    return call(
        functools.partial(inverse_kernel, blk),
        (1,),
        0,
        [whole(n, n)] * 2 + [whole(1, n)],
        [whole(n, n)],
        [((n, n), F32)],
        "inverse",
    )(mine, other, control_cost[None])[0]


def tiled(block, blk):
    n = block.shape[0] // blk
    return [block[i * blk : (i + 1) * blk, j * blk : (j + 1) * blk] for i in range(n) for j in range(n)]


def pack_kernel(blk, where, own, x_ref, *refs):
    *blocks, out = refs
    diag = [own[i * blk : (i + 1) * blk, j * blk : (j + 1) * blk] for i, j in lower(own.shape[0] // blk)]
    x = [x_ref[0, :blk], x_ref[0, blk:]]
    for t, tile in enumerate(diag + x + [tile for block in blocks for tile in tiled(block, blk)]):
        out[t] = tile


def pack(where, cost_rows, parent_state, blk, after):
    rows = cost_rows.shape[0]
    samples = parent_state.shape[2]
    picks = [0] + list(range(3, where.shape[0]))
    size = len(lower(rows // blk)) + 2 + (len(picks) - 1) * (rows // blk) ** 2
    specs = [pl.BlockSpec((rows, rows), functools.partial(lambda t, i, where: (0, where[t]), t)) for t in picks]
    specs.insert(1, pl.BlockSpec((1, rows // 2, samples), lambda i, where: (where[1], where[2], 0)))
    args = [outside(cost_rows)] * len(picks)
    args.insert(1, outside(parent_state))
    return call(
        functools.partial(pack_kernel, blk),
        (1,),
        1,
        specs,
        [whole(size, blk, blk)],
        [((size, blk, blk), F32)],
        "pack",
        after=after,
    )(where, *args)[0]


def front(message, size):
    shape = (size,) + message.shape[1:]

    def kernel(x, out):
        out[...] = x[...]

    return call(kernel, (1,), 0, [whole(*shape)], [whole(*shape)], [(shape, F32)], "front")(message)[0]


def unpack(tiles, step, n, xh, xl):
    blk = tiles.shape[1]
    lead = len(lower(n))
    for t, (i, j) in enumerate(lower(n) if step == 0 else [(i, j) for i in range(n) for j in range(n)]):
        tile = tiles[t if step == 0 else lead + 2 + (step - 1) * n * n + t]
        places = [(i, j, tile)] + ([(j, i, tile.T)] if step == 0 and i != j else [])
        for r, c, value in places:
            at = slice(r * blk, (r + 1) * blk), slice(c * blk, (c + 1) * blk)
            xh[at], xl[at] = split(value)


def collect_kernel(where, pair, mid, end, mid_last, end_last, out):
    out[:2] = pair[...]

    @pl.when(where[0] == 1)
    def _():
        out[2:4] = end[...]
        out[4:6] = end_last[...]

    @pl.when(where[0] == 0)
    def _():
        out[2:4] = mid[...]
        out[4:6] = mid_last[...]


def collect(where, messages, after):
    blk = messages[0].shape[1]
    lead = messages[3].shape[0] // 2 - 1
    return call(
        collect_kernel,
        (1,),
        1,
        [pl.BlockSpec((2, blk, blk), lambda i, where: (lead, 0, 0))] * 5,
        [whole(6, blk, blk)],
        [((6, blk, blk), F32)],
        "collect",
        after=[after],
    )(where, *messages)[0]


def drift_kernel(where, own, mine, other, fh, fl, x_ref, out):
    g = pl.program_id(0)
    core = where[0]
    blk = mine.shape[1]
    rows = own.shape[1]

    @pl.when(g == 0)
    def _():
        x_ref[...] = own[0]

    for d in range(3):

        @pl.when(g == d + 1)
        def _():
            for t in range(2):
                x_ref[pl.ds(pl.multiple_of(core * (rows // 2) + t * blk, blk), blk)] = mine[2 * d + t]
                x_ref[pl.ds(pl.multiple_of((1 - core) * (rows // 2) + t * blk, blk), blk)] = other[2 * d + t]

    part = dot3((fh[...], fl[...]), split(x_ref[...]))

    @pl.when(g == 0)
    def _():
        out[...] = part

    @pl.when(g > 0)
    def _():
        out[...] += part


def drift(where, parent_state, mine, other, fh, fl, after):
    _, rows, samples = parent_state.shape
    count, blk, _ = mine.shape
    factor = pl.BlockSpec((rows, rows), lambda g, where: (where[1], where[1 + g]))
    return call(
        drift_kernel,
        (4,),
        1,
        [pl.BlockSpec((1, rows, samples), lambda g, where: (where[5], 0, 0))]
        + [whole(count, blk, blk)] * 2
        + [factor, factor],
        [pl.BlockSpec((rows, samples), lambda g, where: (where[1 + g], 0)), whole(rows, samples)],
        [((4 * rows, samples), F32), ((rows, samples), F32)],
        "drift",
        after=[after],
    )(where, outside(parent_state), mine, other, outside(fh), outside(fl))


def passed(arrays, *after, keep=False):
    return call(lambda *_: None, (1,), 0, [], [], [], "passed", after=after, through=arrays, keep=keep)()


def begin_kernel(steps, where, weight, p_ref, u, fh, fl, bh, bl, n_out, s_out, g_out, h_out, token, mine, pair, ph, pl_):
    g = pl.program_id(0)
    token[...] = jnp.zeros_like(token)
    rows = ph.shape[0]
    orders = g_out.shape[0]
    tile = fh.shape[1]

    @pl.when(g < steps)
    def _():
        ph[...], pl_[...] = split(p_ref[...])

        @pl.when(g == 0)
        def _():
            mine[...] = jnp.zeros_like(mine)

        multiply(mine, column(u, g, rows), (ph, pl_), NT, mine)

        @pl.when(g != where[0])
        def _():
            multiply(column(n_out, g, rows), column(u, where[0], rows), (ph, pl_), NN)

    @pl.when(g == steps)
    def _():
        pair[0], pair[1] = split(mine[...] * weight[0])
        h_out[...] = dot3(pair[:, :orders], (bh[...], bl[...]))

    @pl.when(g >= steps)
    def _():
        multiply(column(g_out, g - steps, tile), pair.at[:, :orders], (fh, fl), NN)
        multiply(column(s_out, g - steps, tile), pair.at[:, orders:], (fh, fl), NN)


def begin(where, weight, cost_rows, u, fh, fl):
    rows, width = cost_rows.shape
    tall = u.shape[1]
    orders = tall - rows
    steps = width // rows
    tile = 512
    factor = pl.BlockSpec((rows, tile), lambda g, where, _: (where[0], jnp.maximum(g - steps, 0)))
    control = pl.BlockSpec((rows, orders), lambda g, where, _: (where[0], width // orders))
    return call(
        functools.partial(begin_kernel, steps),
        (steps + width // tile,),
        2,
        [
            pl.BlockSpec((rows, rows), lambda g, *_: (0, jnp.minimum(g, steps - 1))),
            STAYS,
            factor,
            factor,
            control,
            control,
        ],
        [STAYS] * 4 + [whole(8, 128)],
        [VMEM((tall, width), F32), VMEM((rows, width), F32), VMEM((orders, width), F32), VMEM((orders, orders), F32)]
        + [((8, 128), F32)],
        "begin",
        [VMEM((tall, rows), F32), VMEM((2, tall, rows), BF16)] + [VMEM((rows, rows), BF16)] * 2,
    )(where, weight, outside(cost_rows), u, *[outside(f) for f in (fh, fl, fh, fl)])


def stage_kernel(options, size, where, weight, *refs):
    arrived = refs[:options]
    u, n_in, fh, fl, bh, bl, s_in, g_in, h_in, *refs = refs[options:]
    if size > 1:
        s_out, g_out, h_out, n_out, token, done, pair, xh, xl = refs
    else:
        s_out, g_out, h_out, token, done, pair, xh, xl = refs
    g = pl.program_id(0)
    token[...] = jnp.zeros_like(token)
    rows = xh.shape[0]
    orders = g_out.shape[0]
    tile = fh.shape[1]
    f = where[1]
    v = column(u, f, rows)
    for c in range(options):
        for t in range(size):

            @pl.when((g == t) & (where[0] == c))
            def _():
                unpack(arrived[c], t, rows // arrived[c].shape[1], xh, xl)

    @pl.when(g == 0)
    def _():
        multiply(done, v, (xh, xl), NN, column(n_in, f, rows))

    if size > 1:

        @pl.when((g > 0) & (g < size))
        def _():
            c = where[1 + g]
            multiply(done, column(u, c, rows), (xh, xl), NT, done)
            multiply(column(n_out, c, rows), v, (xh, xl), NN, column(n_in, c, rows))

    @pl.when(g == size)
    def _():
        pair[0], pair[1] = split(done[...] * weight[0])
        h_out[...] = h_in[...] + dot3(pair[:, :orders], (bh[...], bl[...]))

    @pl.when(g >= size)
    def _():
        at = g - size
        multiply(column(g_out, at, tile), pair.at[:, :orders], (fh, fl), NN, column(g_in, at, tile))
        multiply(column(s_out, at, tile), pair.at[:, orders:], (fh, fl), NN, column(s_in, at, tile))


def stage(where, weight, arrived, size, u, n, fh, fl, sums, after=(), through=()):
    tall, width = n.shape
    rows, orders = sums[0].shape[0], sums[1].shape[0]
    tile = 512
    factor = pl.BlockSpec((rows, tile), lambda g, where, _: (where[1], jnp.maximum(g - size, 0)))
    control = pl.BlockSpec((rows, orders), lambda g, where, _: (where[1], width // orders))
    first = 2 + len(arrived)
    more = size > 1
    shapes = [VMEM((rows, width), F32), VMEM((orders, width), F32), VMEM((orders, orders), F32)]
    return call(
        functools.partial(stage_kernel, len(arrived), size),
        (size + width // tile,),
        2,
        [whole(*x.shape) for x in arrived] + [STAYS, STAYS, factor, factor, control, control] + [STAYS] * 3,
        [STAYS] * (3 + more) + [whole(8, 128)],
        shapes + [VMEM((tall, width), F32)] * more + [((8, 128), F32)],
        "stage",
        [VMEM((tall, rows), F32), VMEM((2, tall, rows), BF16)] + [VMEM((rows, rows), BF16)] * 2,
        {first + 6: 0, first + 7: 1, first + 8: 2, **({first + 1: 3} if more else {})},
        after,
        through,
    )(where, weight, *arrived, u, n, *[outside(f) for f in (fh, fl, fh, fl)], *sums)


def final_kernel(where, h_ref, s_own, g_own, g2, s2, q2, d_ref, x_ref, y_ref, bh, bl, gain, out, reached, pair, q):
    n = pl.program_id(0)
    rows = out.shape[0]

    @pl.when(n == 0)
    def _():
        value = -dot3(split(h_ref[...]), split(column(g_own, where[0], rows)[...] + g2[...]))
        gain[...] = value
        pair[0], pair[1] = split(value.T)
        q[...] = jnp.zeros_like(q)

    cross = split(column(g_own, n, rows)[...] + q2[...])
    part = column(s_own, n, rows)[...] + s2[...] + dot3(pair[...], cross)
    diag = lax.broadcasted_iota(jnp.int32, (rows, rows), 0) == lax.broadcasted_iota(jnp.int32, (rows, rows), 1)
    out[...] = part + jnp.where(diag & (n == where[0]), d_ref[...], 0.0)
    q[...] += dot3(cross, split(x_ref[...]))

    @pl.when(n == pl.num_programs(0) - 1)
    def _():
        u = -dot3(split(h_ref[...]), split(q[...]))
        reached[...] = y_ref[...] + dot3((bh[...], bl[...]), split(u))


def final(where, hinv, own, other, state_cost, x, y, fh, fl):
    rows, width = own[0].shape
    orders = own[1].shape[0]
    samples = x.shape[1]
    s_spec = pl.BlockSpec((rows, rows), lambda n, where: (0, n))
    g_spec = pl.BlockSpec((orders, rows), lambda n, where: (0, n))
    mine = pl.BlockSpec((orders, rows), lambda n, where: (0, where[0]))
    factor = pl.BlockSpec((rows, orders), lambda n, where: (where[0], width // orders))
    return call(
        final_kernel,
        (width // rows,),
        1,
        [whole(orders, orders), STAYS, STAYS, mine, s_spec, g_spec, whole(1, rows)]
        + [pl.BlockSpec((rows, samples), lambda n, where: (n, 0)), whole(rows, samples), factor, factor],
        [whole(orders, rows), s_spec, whole(rows, samples)],
        [((orders, rows), F32), ((rows, width), F32), ((rows, samples), F32)],
        "final",
        [pltpu.VMEM((2, rows, orders), BF16), pltpu.VMEM((orders, samples), F32)],
    )(where, hinv, *own, other[1], *other, state_cost[None], x, y, outside(fh), outside(fl))


def image_kernel(where, weight, fh, fl, p_ref, out, acc):
    k = pl.program_id(0)
    part = dot3(split(p_ref[...]), (fh[...], fl[...]))

    @pl.when(k == 0)
    def _():
        acc[...] = part

    @pl.when(k > 0)
    def _():
        acc[...] += part

    @pl.when(k == pl.num_programs(0) - 1)
    def _():
        out[...] = acc[...].T * weight[0]


def image(where, weight, fh, fl, cost_rows):
    rows, width = cost_rows.shape
    chunk = 512
    factor = pl.BlockSpec((chunk, rows), lambda k, where, _: (k, where[0]))
    return call(
        image_kernel,
        (width // chunk,),
        2,
        [factor, factor, pl.BlockSpec((rows, chunk), lambda k, *_: (0, k))],
        [whole(rows, rows)],
        [((rows, rows), F32)],
        "image",
        [pltpu.VMEM((rows, rows), F32)],
    )(where, weight, fh, fl, cost_rows)[0]


def accumulate_kernel(first, where, y_ref, fh, fl, *refs):
    out = refs[-1]
    part = dot3(split(y_ref[...]), (fh[...], fl[...]))
    out[...] = part if first else refs[0][...] + part


def accumulate(where, y, fh, fl, acc):
    rows = y.shape[0]
    total = fh.shape[1]
    tile = 512
    first = acc is None
    spec = pl.BlockSpec((rows, tile), lambda n, where: (0, n))
    factor = pl.BlockSpec((rows, tile), lambda n, where: (where[0], n))
    return call(
        functools.partial(accumulate_kernel, first),
        (total // tile,),
        1,
        [whole(rows, rows), factor, factor] + [spec] * (not first),
        [spec],
        [((rows, total), F32)],
        "accumulate",
        aliases=None if first else {4: 0},
    )(where, y, fh, fl, *(() if first else (acc,)))[0]


def by_images(z, parts, weight, cost_rows, fh, fl):
    rows, width = cost_rows.shape
    acc = None
    for d in range(parts):
        block = image(((z + d) % parts)[None], weight, fh, fl, cost_rows)
        if d:
            block = lax.ppermute(block, "row", [(i, (i + d) % parts) for i in range(parts)])
        acc = accumulate(((z - d) % parts)[None], block, fh, fl, acc)
    cross = lax.all_gather(acc[:, width:], "row")
    return acc[:, :width], jnp.swapaxes(cross.reshape(width, -1), 0, 1)


def by_blocks(z, core, parent, weight, cost_rows, parent_state, dense_parts, control_cost, messages):
    fh, fl, u = dense_parts
    edge = ((z == 0) | (z == 3)).astype(jnp.int32)
    left = z < 2
    second, third = jnp.where(left, 2, 1), jnp.where(left, 3, 0)
    pair, mid = messages
    lead = 2 * mid.shape[0] - pair.shape[0]

    def moved(x, *pairs):
        return lax.ppermute(x, "row", pairs)

    def across(x):
        return moved(x, (1, 2), (2, 1))

    def to_end(x):
        return moved(x, (1, 0), (2, 3))

    pair = moved(pair, (0, 1), (1, 0), (2, 3), (3, 2))
    mid = across(mid)
    n, *sums, token = begin(z[None], weight, cost_rows, u, fh, fl)
    (mid,) = passed([mid], token)
    end = to_end(mid)
    mid_last = across(front(pair, lead))
    where = jnp.stack([z * 0, z ^ 1, second, third])
    *sums, n, token = stage(where, weight, [pair], 3, u, n, fh, fl, sums)
    (mid_last,) = passed([mid_last], token)
    end_last = to_end(mid_last)
    where = jnp.stack([edge, second, third])
    *sums, n, token = stage(where, weight, [mid, end], 2, u, n, fh, fl, sums)
    halves = collect(edge[None], [pair, mid, end, mid_last, end_last], token)
    where = jnp.stack([edge, third])
    s, g, h, token = stage(where, weight, [mid_last, end_last], 1, u, n, fh, fl, sums, [halves])
    where = jnp.stack([core, z, z ^ 1, second, third, parent])
    x, y = drift(where, parent_state, halves, swapped(halves), fh, fl, token)
    other = swapped(h)
    return h, other, passed([s, g], other, y, keep=True), x, y


def swapped(x):
    n = lax.axis_size("leaf")
    return lax.ppermute(x, "leaf", [(i, i ^ 1) for i in range(n)])


def shards(
    leaf_cost,
    a_blocks,
    a_cols,
    b_blocks,
    b_cols,
    branch_prob,
    state_cost,
    control_cost,
    parent_state,
):
    cost_rows = leaf_cost[0]
    rows, width = cost_rows.shape
    blk = a_blocks.shape[3]
    orders = control_cost.shape[0]
    parts = lax.axis_size("row")
    z = lax.axis_index("row")
    leaf = lax.axis_index("leaf")
    core = leaf % 2
    line = parts == 4 and rows == orders

    sent = []
    if line:
        left = z < 2
        near = jnp.where(left, 0, 3)
        lead = [z, leaf // 2, core]
        sent.append(pack(jnp.stack(lead + [jnp.where(left, 2, 1), 3 - near]), cost_rows, parent_state, blk, []))
        sent.append(pack(jnp.stack(lead + [near]), cost_rows, parent_state, blk, sent))
    fh, fl, u = parts_of = dense(z[None], rows, a_blocks[0], a_cols, b_blocks[0], b_cols, orders, sent)
    if line:
        h, other_h, own, x, y = by_blocks(
            z, core, leaf // 2, branch_prob, cost_rows, parent_state, parts_of, control_cost, sent
        )
    else:
        w = dot3(parted(cost_rows), (fh[:, width:], fl[:, width:]))
        b_rows = [lax.dynamic_slice(f, (0, z * rows), (orders, rows)) for f in u]
        h = lax.psum(dot3(b_rows, parted(w)) * branch_prob[0], "row")
        other_h = swapped(h)
        own = by_images(z, parts, branch_prob, cost_rows, fh, fl)
        own_state = lax.dynamic_index_in_dim(parent_state, leaf // 2, 0, keepdims=False)
        x = lax.all_gather(own_state, "row", tiled=True)
        y = dot3([lax.dynamic_slice(f, (z * rows, 0), (rows, width)) for f in (fh, fl)], parted(x))
    hinv = inverse(h, other_h, control_cost, blk)
    other = tuple(swapped(x) for x in own)
    gain, pcost, reached = final(z[None], hinv, own, other, state_cost, x, y, fh, fl)
    return pcost[None], gain[None], reached[None]


def solution(mesh):
    placed = (
        P("leaf", "row", None),
        P("leaf", None, None, None, None),
        P("leaf", None, None),
        P("leaf", None, None, None, None),
        P("leaf", None, None),
        P("leaf"),
        P("row"),
        P(),
        P(None, "row", None),
    )
    return jax.shard_map(
        shards,
        mesh=mesh,
        in_specs=placed,
        out_specs=(P("leaf", "row", None), P("leaf", None, "row"), P("leaf", "row", None)),
        check_vma=False,
    )
```

```python
import functools

import jax
import jax.numpy as jnp
from jax import lax
from jax.experimental import pallas as pl
from jax.experimental.pallas import tpu as pltpu
from jax.sharding import PartitionSpec as P

F32 = jnp.float32
BF16 = jnp.bfloat16
NN = (((1,), (0,)), ((), ()))
NT = (((1,), (1,)), ((), ()))


def split(x):
    hi = x.astype(BF16)
    return hi, (x - hi.astype(F32)).astype(BF16)


def parted(x):
    hi = lax.reduce_precision(x, 8, 7)
    return hi.astype(BF16), (x - hi).astype(BF16)


def dot3(a, b, dims=NN):
    one = functools.partial(lax.dot_general, dimension_numbers=dims, preferred_element_type=F32)
    rows = a[0].shape[0]
    both = jnp.concatenate(a, axis=0) if isinstance(a, (tuple, list)) else a.reshape(2 * rows, a.shape[2])
    part = one(both, b[0])
    return part[:rows] + (part[rows:] + one(a[0], b[1]))


TILE = (256, 512)
OWN, PARTNER, SECOND, THIRD, PARENT, CORE, NEAR, EDGE = range(8)
VMEM = pltpu.VMEM
STAYS = pl.BlockSpec(memory_space=VMEM)


def resident(x):
    return pltpu.with_memory_space_constraint(x, VMEM)


def outside(x):
    return pltpu.with_memory_space_constraint(x, pltpu.HBM)


def column(ref, i, size):
    return ref.at[..., pl.ds(pl.multiple_of(i * size, size), size)]


def multiply(out, a, b, dims, add=None):
    right = dims[0][1][0]
    for m in range(0, out.shape[0], TILE[0]):
        rows = slice(m, m + TILE[0])
        for n in range(0, out.shape[1], TILE[1]):
            cols = slice(n, n + TILE[1])
            b_part = [x[:, cols] if right == 0 else x[cols] for x in b]
            value = dot3((a[0, rows], a[1, rows]), b_part, dims)
            out[rows, cols] = value if add is None else add[rows, cols] + value


def call(kernel, grid, prefetch, ins, outs, shapes, name, scratch=(), aliases=None, after=(), through=(), keep=False, limit=24):
    n_in, n_out = len(ins), len(outs)
    extra = len(after) + len(through)
    anywhere = pl.BlockSpec(memory_space=pl.ANY)

    def body(*refs):
        start = prefetch + n_in
        stop = start + extra + n_out
        kernel(*refs[:start], *refs[start + extra : stop], *refs[stop + len(through) :])

    aliases = dict(aliases or {})
    for t in range(len(through)):
        aliases[prefetch + n_in + len(after) + t] = n_out + t
    built = pl.pallas_call(
        body,
        grid_spec=pltpu.PrefetchScalarGridSpec(
            num_scalar_prefetch=prefetch,
            grid=grid,
            in_specs=list(ins) + [anywhere] * extra,
            out_specs=list(outs) + [anywhere] * len(through),
            scratch_shapes=scratch,
        ),
        out_shape=[x if isinstance(x, pl.MemoryRef) else jax.ShapeDtypeStruct(*x) for x in shapes]
        + [(VMEM if keep else jax.ShapeDtypeStruct)(x.shape, x.dtype) for x in through],
        input_output_aliases=aliases,
        compiler_params=pltpu.CompilerParams(vmem_limit_bytes=limit * 2**20),
        cost_estimate=pl.CostEstimate(flops=1, bytes_accessed=1, transcendentals=0),
        name=name,
    )

    def run(*args):
        placed = [resident(x) if spec is STAYS else x for spec, x in zip(ins, args[prefetch:])]
        return built(*args[:prefetch], *placed, *after, *[resident(x) if keep else x for x in through])

    return run


def whole(*shape):
    return pl.BlockSpec(shape, lambda *_: (0,) * len(shape))


def lower(n):
    return [(i, j) for i in range(n) for j in range(i + 1)]


def dense_kernel(blk, step, width, where, acol, bcol, a_ref, b_ref, fh, fl, u):
    i = pl.program_id(0)
    orders = fh.shape[1] - width
    rows = u.shape[1] - orders
    for ref in (fh, fl):
        ref[...] = jnp.zeros_like(ref)
    diag = lax.broadcasted_iota(jnp.int32, (blk, blk), 0) == lax.broadcasted_iota(jnp.int32, (blk, blk), 1)
    eye = jnp.where(diag, 0.75, 0.0).astype(F32)
    for t in range(step // blk):
        row = i * (step // blk) + t
        at = slice(t * blk, (t + 1) * blk)
        for s in range(a_ref.shape[1]):
            col = acol[0, row, s]
            block = a_ref[t, s] + eye if s == 0 else a_ref[t, s]
            to = pl.ds(pl.multiple_of(col * blk, blk), blk)
            fh[at, to], fl[at, to] = split(block)
        for s in range(b_ref.shape[1]):
            to = pl.ds(pl.multiple_of(width + bcol[0, row, s] * blk, blk), blk)
            fh[at, to], fl[at, to] = split(b_ref[t, s])

    own = pl.ds(pl.multiple_of(where[0] * rows, rows), rows)
    for p, f in enumerate((fh, fl)):
        for to, cols in ((slice(0, orders), slice(width, None)), (slice(orders, None), own)):
            part = f[:, cols]
            n = part.shape[1]
            diag = lax.broadcasted_iota(jnp.int32, (n, n), 0) == lax.broadcasted_iota(jnp.int32, (n, n), 1)
            one = jnp.where(diag, 1.0, 0.0).astype(BF16)
            u[p, to, pl.ds(pl.multiple_of(i * step, step), step)] = lax.dot_general(one, part, NT, preferred_element_type=F32).astype(BF16)


def dense(where, rows, a_blocks, a_cols, b_blocks, b_cols, orders, after):
    count, nnza, blk, _ = a_blocks.shape
    nnzb = b_blocks.shape[1]
    width = count * blk
    step = 2 * blk
    total = width + orders
    factor = pl.BlockSpec((step, total), lambda i, *_: (i, 0))
    return call(
        functools.partial(dense_kernel, blk, step, width),
        (width // step,),
        3,
        [
            pl.BlockSpec((2, nnza, blk, blk), lambda i, *_: (i, 0, 0, 0)),
            pl.BlockSpec((2, nnzb, blk, blk), lambda i, *_: (i, 0, 0, 0)),
        ],
        [factor, factor, STAYS],
        [pltpu.HBM((width, total), BF16)] * 2 + [VMEM((2, rows + orders, width), BF16)],
        "dense",
        after=after,
    )(where, a_cols, b_cols, outside(a_blocks), outside(b_blocks))


def inverse_block(m):
    n = m.shape[0]
    sub = lax.broadcasted_iota(jnp.int32, (8, n), 0)
    lane = lax.broadcasted_iota(jnp.int32, (8, n), 1)
    strips = [m[i : i + 8] for i in range(0, n, 8)]

    def along(v, j):
        return jnp.broadcast_to(v[:, j : j + 1], (8, n))

    def down(v, t):
        return jnp.broadcast_to(v[t : t + 1], (8, n))

    for q in range(n // 8):
        panel = strips[q]
        cols = [along(panel, 8 * q + b) for b in range(8)]
        for t in range(8):
            here = sub == t
            inv = 1.0 / down(cols[t], t)

            def reduced(v):
                r = down(v, t) * inv
                return jnp.where(here, r, v - cols[t] * r)

            panel = reduced(jnp.where(lane == 8 * q + t, jnp.where(here, 1.0, 0.0), panel))
            cols[t + 1 :] = [reduced(v) for v in cols[t + 1 :]]
        inside = (lane >= 8 * q) & (lane < 8 * q + 8)
        rows = [down(panel, b) for b in range(8)]
        for i in range(q + 1, q + n // 8):
            old = strips[i % (n // 8)]
            terms = [along(old, 8 * q + b) * rows[b] for b in range(8)]
            while len(terms) > 1:
                terms = [x + y for x, y in zip(terms[::2], terms[1::2])]
            strips[i % (n // 8)] = jnp.where(inside, 0.0, old) - terms[0]
        strips[q] = panel
    return jnp.concatenate(strips, axis=0)


def inverse_kernel(blk, mine, other, d_ref, out):
    n = out.shape[0]
    def dot(a, b):
        return dot3(split(a), split(b))

    diag = lax.broadcasted_iota(jnp.int32, (n, n), 0) == lax.broadcasted_iota(jnp.int32, (n, n), 1)
    out[...] = mine[...] + other[...] + jnp.where(diag, d_ref[...], 0.0)

    place = lax.broadcasted_iota(jnp.int32, (n, blk), 0) // blk

    @pl.loop(0, n // blk)
    def _(b):
        here = pl.ds(pl.multiple_of(b * blk, blk), blk)
        inv = inverse_block(out[here, here])
        row = dot(inv, out[here, :])
        out[...] -= dot(out[:, here], row)
        col = row.T
        out[:, here] = jnp.where(place < b, col, -col)
        out[here, :] = row
        out[here, here] = inv


def inverse(mine, other, control_cost, blk):
    n = control_cost.shape[0]
    return call(
        functools.partial(inverse_kernel, blk),
        (1,),
        0,
        [whole(n, n)] * 2 + [whole(1, n)],
        [whole(n, n)],
        [((n, n), F32)],
        "inverse",
        limit=10,
    )(mine, other, control_cost[None])[0]


def tiled(block, blk):
    n = block.shape[0] // blk
    return [block[i * blk : (i + 1) * blk, j * blk : (j + 1) * blk] for i in range(n) for j in range(n)]


def pack_kernel(blk, where, own, x_ref, *refs):
    *blocks, out = refs
    diag = [own[i * blk : (i + 1) * blk, j * blk : (j + 1) * blk] for i, j in lower(own.shape[0] // blk)]
    x = [x_ref[0, :blk], x_ref[0, blk:]]
    for t, tile in enumerate(diag + x + [tile for block in blocks for tile in tiled(block, blk)]):
        out[t] = tile


def pack(where, blocks, cost_rows, parent_state, blk, after):
    rows = cost_rows.shape[0]
    samples = parent_state.shape[2]
    picks = [OWN, *blocks]
    size = len(lower(rows // blk)) + 2 + (len(picks) - 1) * (rows // blk) ** 2
    specs = [pl.BlockSpec((rows, rows), functools.partial(lambda t, i, where: (0, where[t]), t)) for t in picks]
    specs.insert(1, pl.BlockSpec((1, rows // 2, samples), lambda i, where: (where[PARENT], where[CORE], 0)))
    args = [outside(cost_rows)] * len(picks)
    args.insert(1, outside(parent_state))
    return call(
        functools.partial(pack_kernel, blk),
        (1,),
        1,
        specs,
        [whole(size, blk, blk)],
        [((size, blk, blk), F32)],
        "pack",
        after=after,
        limit=16,
    )(where, *args)[0]


def front(message, size):
    shape = (size,) + message.shape[1:]

    def kernel(x, out):
        out[...] = x[...]

    return call(kernel, (1,), 0, [whole(*shape)], [whole(*shape)], [(shape, F32)], "front", limit=4)(message)[0]


def unpack(tiles, step, n, xh, xl):
    blk = tiles.shape[1]
    lead = len(lower(n))
    for t, (i, j) in enumerate(lower(n) if step == 0 else [(i, j) for i in range(n) for j in range(n)]):
        tile = tiles[t if step == 0 else lead + 2 + (step - 1) * n * n + t]
        places = [(i, j, tile)] + ([(j, i, tile.T)] if step == 0 and i != j else [])
        for r, c, value in places:
            at = slice(r * blk, (r + 1) * blk), slice(c * blk, (c + 1) * blk)
            xh[at], xl[at] = split(value)


def collect_kernel(where, pair, mid, end, mid_last, end_last, out):
    out[:2] = pair[...]

    @pl.when(where[EDGE] == 1)
    def _():
        out[2:4] = end[...]
        out[4:6] = end_last[...]

    @pl.when(where[EDGE] == 0)
    def _():
        out[2:4] = mid[...]
        out[4:6] = mid_last[...]


def collect(where, messages, after):
    blk = messages[0].shape[1]
    lead = messages[3].shape[0] // 2 - 1
    return call(
        collect_kernel,
        (1,),
        1,
        [pl.BlockSpec((2, blk, blk), lambda i, where: (lead, 0, 0))] * 5,
        [whole(6, blk, blk)],
        [((6, blk, blk), F32)],
        "collect",
        after=[after],
        limit=4,
    )(where, *messages)[0]


def drift_kernel(where, own, mine, other, fh, fl, x_ref, out):
    g = pl.program_id(0)
    core = where[CORE]
    blk = mine.shape[1]
    rows = own.shape[1]

    @pl.when(g == 0)
    def _():
        x_ref[...] = own[0]

    for d in range(3):

        @pl.when(g == d + 1)
        def _():
            for t in range(2):
                x_ref[pl.ds(pl.multiple_of(core * (rows // 2) + t * blk, blk), blk)] = mine[2 * d + t]
                x_ref[pl.ds(pl.multiple_of((1 - core) * (rows // 2) + t * blk, blk), blk)] = other[2 * d + t]

    part = dot3((fh[...], fl[...]), split(x_ref[...]))

    @pl.when(g == 0)
    def _():
        out[...] = part

    @pl.when(g > 0)
    def _():
        out[...] += part


def drift(where, parent_state, mine, other, fh, fl, after):
    _, rows, samples = parent_state.shape
    count, blk, _ = mine.shape
    factor = pl.BlockSpec((rows, rows), lambda g, where: (where[OWN], where[OWN + g]))
    return call(
        drift_kernel,
        (4,),
        1,
        [pl.BlockSpec((1, rows, samples), lambda g, where: (where[PARENT], 0, 0))]
        + [whole(count, blk, blk)] * 2
        + [factor, factor],
        [pl.BlockSpec((rows, samples), lambda g, where: (where[OWN + g], 0)), whole(rows, samples)],
        [((4 * rows, samples), F32), ((rows, samples), F32)],
        "drift",
        after=[after],
        limit=12,
    )(where, outside(parent_state), mine, other, outside(fh), outside(fl))


def passed(arrays, *after, keep=False):
    return call(lambda *_: None, (1,), 0, [], [], [], "passed", after=after, through=arrays, keep=keep, limit=1)()


def begin_kernel(steps, where, weight, p_ref, u, fh, fl, bh, bl, n_out, s_out, g_out, h_out, token, mine, pair, ph, pl_):
    g = pl.program_id(0)
    token[...] = jnp.zeros_like(token)
    rows = ph.shape[0]
    orders = g_out.shape[0]
    tile = fh.shape[1]

    @pl.when(g < steps)
    def _():
        ph[...], pl_[...] = split(p_ref[...])

        @pl.when(g == 0)
        def _():
            mine[...] = jnp.zeros_like(mine)

        multiply(mine, column(u, g, rows), (ph, pl_), NT, mine)

        @pl.when(g != where[0])
        def _():
            multiply(column(n_out, g, rows), column(u, where[0], rows), (ph, pl_), NN)

    @pl.when(g == steps)
    def _():
        pair[0], pair[1] = split(mine[...] * weight[0])
        h_out[...] = dot3(pair[:, :orders], (bh[...], bl[...]))

    @pl.when(g >= steps)
    def _():
        multiply(column(g_out, g - steps, tile), pair.at[:, :orders], (fh, fl), NN)
        multiply(column(s_out, g - steps, tile), pair.at[:, orders:], (fh, fl), NN)


def begin(where, weight, cost_rows, u, fh, fl):
    rows, width = cost_rows.shape
    tall = u.shape[1]
    orders = tall - rows
    steps = width // rows
    tile = 512
    factor = pl.BlockSpec((rows, tile), lambda g, where, _: (where[0], jnp.maximum(g - steps, 0)))
    control = pl.BlockSpec((rows, orders), lambda g, where, _: (where[0], width // orders))
    return call(
        functools.partial(begin_kernel, steps),
        (steps + width // tile,),
        2,
        [
            pl.BlockSpec((rows, rows), lambda g, *_: (0, jnp.minimum(g, steps - 1))),
            STAYS,
            factor,
            factor,
            control,
            control,
        ],
        [STAYS] * 4 + [whole(8, 128)],
        [VMEM((tall, width), F32), VMEM((rows, width), F32), VMEM((orders, width), F32), VMEM((orders, orders), F32)]
        + [((8, 128), F32)],
        "begin",
        [VMEM((tall, rows), F32), VMEM((2, tall, rows), BF16)] + [VMEM((rows, rows), BF16)] * 2,
        limit=18,
    )(where, weight, outside(cost_rows), u, *[outside(f) for f in (fh, fl, fh, fl)])


def stage_kernel(options, size, focus, where, weight, *refs):
    arrived = refs[:options]
    u, n_in, fh, fl, bh, bl, s_in, g_in, h_in, *refs = refs[options:]
    if size > 1:
        s_out, g_out, h_out, n_out, token, done, pair, xh, xl = refs
    else:
        s_out, g_out, h_out, token, done, pair, xh, xl = refs
    g = pl.program_id(0)
    token[...] = jnp.zeros_like(token)
    rows = xh.shape[0]
    orders = g_out.shape[0]
    tile = fh.shape[1]
    f = where[focus]
    v = column(u, f, rows)
    for c in range(options):
        for t in range(size):

            @pl.when((g == t) & ((where[EDGE] == c) | (options == 1)))
            def _():
                unpack(arrived[c], t, rows // arrived[c].shape[1], xh, xl)

    @pl.when(g == 0)
    def _():
        multiply(done, v, (xh, xl), NN, column(n_in, f, rows))

    if size > 1:

        @pl.when((g > 0) & (g < size))
        def _():
            c = where[focus + g]
            multiply(done, column(u, c, rows), (xh, xl), NT, done)
            multiply(column(n_out, c, rows), v, (xh, xl), NN, column(n_in, c, rows))

    @pl.when(g == size)
    def _():
        pair[0], pair[1] = split(done[...] * weight[0])
        h_out[...] = h_in[...] + dot3(pair[:, :orders], (bh[...], bl[...]))

    @pl.when(g >= size)
    def _():
        at = g - size
        multiply(column(g_out, at, tile), pair.at[:, :orders], (fh, fl), NN, column(g_in, at, tile))
        multiply(column(s_out, at, tile), pair.at[:, orders:], (fh, fl), NN, column(s_in, at, tile))


def stage(where, weight, arrived, focus, size, u, n, fh, fl, sums, after=()):
    tall, width = n.shape
    rows, orders = sums[0].shape[0], sums[1].shape[0]
    tile = 512
    factor = pl.BlockSpec((rows, tile), lambda g, where, _: (where[focus], jnp.maximum(g - size, 0)))
    control = pl.BlockSpec((rows, orders), lambda g, where, _: (where[focus], width // orders))
    first = 2 + len(arrived)
    more = size > 1
    shapes = [VMEM((rows, width), F32), VMEM((orders, width), F32), VMEM((orders, orders), F32)]
    return call(
        functools.partial(stage_kernel, len(arrived), size, focus),
        (size + width // tile,),
        2,
        [whole(*x.shape) for x in arrived] + [STAYS, STAYS, factor, factor, control, control] + [STAYS] * 3,
        [STAYS] * (3 + more) + [whole(8, 128)],
        shapes + [VMEM((tall, width), F32)] * more + [((8, 128), F32)],
        "stage",
        [VMEM((tall, rows), F32), VMEM((2, tall, rows), BF16)] + [VMEM((rows, rows), BF16)] * 2,
        {first + 6: 0, first + 7: 1, first + 8: 2, **({first + 1: 3} if more else {})},
        after,
        limit=20,
    )(where, weight, *arrived, u, n, *[outside(f) for f in (fh, fl, fh, fl)], *sums)


def final_kernel(where, h_ref, s_own, g_own, g2, s2, q2, d_ref, x_ref, y_ref, bh, bl, gain, out, reached, pair, q):
    n = pl.program_id(0)
    rows = out.shape[0]

    @pl.when(n == 0)
    def _():
        value = -dot3(split(h_ref[...]), split(column(g_own, where[0], rows)[...] + g2[...]))
        gain[...] = value
        pair[0], pair[1] = split(value.T)
        q[...] = jnp.zeros_like(q)

    cross = split(column(g_own, n, rows)[...] + q2[...])
    part = column(s_own, n, rows)[...] + s2[...] + dot3(pair[...], cross)
    diag = lax.broadcasted_iota(jnp.int32, (rows, rows), 0) == lax.broadcasted_iota(jnp.int32, (rows, rows), 1)
    out[...] = part + jnp.where(diag & (n == where[0]), d_ref[...], 0.0)
    q[...] += dot3(cross, split(x_ref[...]))

    @pl.when(n == pl.num_programs(0) - 1)
    def _():
        u = -dot3(split(h_ref[...]), split(q[...]))
        reached[...] = y_ref[...] + dot3((bh[...], bl[...]), split(u))


def final(where, hinv, own, other, state_cost, x, y, fh, fl):
    rows, width = own[0].shape
    orders = own[1].shape[0]
    samples = x.shape[1]
    s_spec = pl.BlockSpec((rows, rows), lambda n, where: (0, n))
    g_spec = pl.BlockSpec((orders, rows), lambda n, where: (0, n))
    mine = pl.BlockSpec((orders, rows), lambda n, where: (0, where[0]))
    factor = pl.BlockSpec((rows, orders), lambda n, where: (where[0], width // orders))
    return call(
        final_kernel,
        (width // rows,),
        1,
        [whole(orders, orders), STAYS, STAYS, mine, s_spec, g_spec, whole(1, rows)]
        + [pl.BlockSpec((rows, samples), lambda n, where: (n, 0)), whole(rows, samples), factor, factor],
        [whole(orders, rows), s_spec, whole(rows, samples)],
        [((orders, rows), F32), ((rows, width), F32), ((rows, samples), F32)],
        "final",
        [pltpu.VMEM((2, rows, orders), BF16), pltpu.VMEM((orders, samples), F32)],
    )(where, hinv, *own, other[1], *other, state_cost[None], x, y, outside(fh), outside(fl))


def image_kernel(where, weight, fh, fl, p_ref, out, acc):
    k = pl.program_id(0)
    part = dot3(split(p_ref[...]), (fh[...], fl[...]))

    @pl.when(k == 0)
    def _():
        acc[...] = part

    @pl.when(k > 0)
    def _():
        acc[...] += part

    @pl.when(k == pl.num_programs(0) - 1)
    def _():
        out[...] = acc[...].T * weight[0]


def image(where, weight, fh, fl, cost_rows):
    rows, width = cost_rows.shape
    chunk = 512
    factor = pl.BlockSpec((chunk, rows), lambda k, where, _: (k, where[0]))
    return call(
        image_kernel,
        (width // chunk,),
        2,
        [factor, factor, pl.BlockSpec((rows, chunk), lambda k, *_: (0, k))],
        [whole(rows, rows)],
        [((rows, rows), F32)],
        "image",
        [pltpu.VMEM((rows, rows), F32)],
    )(where, weight, fh, fl, cost_rows)[0]


def accumulate_kernel(first, where, y_ref, fh, fl, *refs):
    out = refs[-1]
    part = dot3(split(y_ref[...]), (fh[...], fl[...]))
    out[...] = part if first else refs[0][...] + part


def accumulate(where, y, fh, fl, acc):
    rows = y.shape[0]
    total = fh.shape[1]
    tile = 512
    first = acc is None
    spec = pl.BlockSpec((rows, tile), lambda n, where: (0, n))
    factor = pl.BlockSpec((rows, tile), lambda n, where: (where[0], n))
    return call(
        functools.partial(accumulate_kernel, first),
        (total // tile,),
        1,
        [whole(rows, rows), factor, factor] + [spec] * (not first),
        [spec],
        [((rows, total), F32)],
        "accumulate",
        aliases=None if first else {4: 0},
    )(where, y, fh, fl, *(() if first else (acc,)))[0]


def by_images(z, parts, weight, cost_rows, fh, fl):
    rows, width = cost_rows.shape
    acc = None
    for d in range(parts):
        block = image(((z + d) % parts)[None], weight, fh, fl, cost_rows)
        if d:
            block = lax.ppermute(block, "row", [(i, (i + d) % parts) for i in range(parts)])
        acc = accumulate(((z - d) % parts)[None], block, fh, fl, acc)
    cross = lax.all_gather(acc[:, width:], "row")
    return acc[:, :width], jnp.swapaxes(cross.reshape(width, -1), 0, 1)


def by_blocks(where, weight, cost_rows, parent_state, dense_parts, messages):
    fh, fl, u = dense_parts
    pair, mid = messages
    lead = 2 * mid.shape[0] - pair.shape[0]

    def moved(x, *pairs):
        return lax.ppermute(x, "row", pairs)

    def across(x):
        return moved(x, (1, 2), (2, 1))

    def to_end(x):
        return moved(x, (1, 0), (2, 3))

    pair = moved(pair, (0, 1), (1, 0), (2, 3), (3, 2))
    mid = across(mid)
    n, *sums, token = begin(where, weight, cost_rows, u, fh, fl)
    (mid,) = passed([mid], token)
    end = to_end(mid)
    mid_last = across(front(pair, lead))
    *sums, n, token = stage(where, weight, [pair], PARTNER, 3, u, n, fh, fl, sums)
    (mid_last,) = passed([mid_last], token)
    end_last = to_end(mid_last)
    *sums, n, token = stage(where, weight, [mid, end], SECOND, 2, u, n, fh, fl, sums)
    halves = collect(where, [pair, mid, end, mid_last, end_last], token)
    s, g, h, token = stage(where, weight, [mid_last, end_last], THIRD, 1, u, n, fh, fl, sums, [halves])
    x, y = drift(where, parent_state, halves, swapped(halves), fh, fl, token)
    other = swapped(h)
    return h, other, passed([s, g], other, y, keep=True), x, y


def swapped(x):
    n = lax.axis_size("leaf")
    return lax.ppermute(x, "leaf", [(i, i ^ 1) for i in range(n)])


def shards(
    leaf_cost,
    a_blocks,
    a_cols,
    b_blocks,
    b_cols,
    branch_prob,
    state_cost,
    control_cost,
    parent_state,
):
    cost_rows = leaf_cost[0]
    rows, width = cost_rows.shape
    blk = a_blocks.shape[3]
    orders = control_cost.shape[0]
    parts = lax.axis_size("row")
    z = lax.axis_index("row")
    leaf = lax.axis_index("leaf")
    line = parts == 4 and rows == orders

    left = z < 2
    near = jnp.where(left, 0, 3)
    edge = ((z == 0) | (z == 3)).astype(jnp.int32)
    where = jnp.stack([z, z ^ 1, jnp.where(left, 2, 1), 3 - near, leaf // 2, leaf % 2, near, edge])
    sent = []
    if line:
        sent.append(pack(where, [SECOND, THIRD], cost_rows, parent_state, blk, []))
        sent.append(pack(where, [NEAR], cost_rows, parent_state, blk, sent))
    fh, fl, u = parts_of = dense(where, rows, a_blocks[0], a_cols, b_blocks[0], b_cols, orders, sent)
    if line:
        h, other_h, own, x, y = by_blocks(where, branch_prob, cost_rows, parent_state, parts_of, sent)
    else:
        w = dot3(parted(cost_rows), (fh[:, width:], fl[:, width:]))
        b_rows = [lax.dynamic_slice(f, (0, z * rows), (orders, rows)) for f in u]
        h = lax.psum(dot3(b_rows, parted(w)) * branch_prob[0], "row")
        other_h = swapped(h)
        own = by_images(z, parts, branch_prob, cost_rows, fh, fl)
        own_state = lax.dynamic_index_in_dim(parent_state, leaf // 2, 0, keepdims=False)
        x = lax.all_gather(own_state, "row", tiled=True)
        y = dot3([lax.dynamic_slice(f, (z * rows, 0), (rows, width)) for f in (fh, fl)], parted(x))
    hinv = inverse(h, other_h, control_cost, blk)
    other = tuple(swapped(x) for x in own)
    gain, pcost, reached = final(where, hinv, own, other, state_cost, x, y, fh, fl)
    return pcost[None], gain[None], reached[None]


def solution(mesh):
    placed = (
        P("leaf", "row", None),
        P("leaf", None, None, None, None),
        P("leaf", None, None),
        P("leaf", None, None, None, None),
        P("leaf", None, None),
        P("leaf"),
        P("row"),
        P(),
        P(None, "row", None),
    )
    return jax.shard_map(
        shards,
        mesh=mesh,
        in_specs=placed,
        out_specs=(P("leaf", "row", None), P("leaf", None, "row"), P("leaf", "row", None)),
        check_vma=False,
    )
```

```python
import functools

import jax
import jax.numpy as jnp
from jax import lax
from jax.experimental import pallas as pl
from jax.experimental.pallas import tpu as pltpu
from jax.sharding import PartitionSpec as P

F32 = jnp.float32
BF16 = jnp.bfloat16
NN = (((1,), (0,)), ((), ()))
NT = (((1,), (1,)), ((), ()))


def split(x):
    hi = x.astype(BF16)
    return hi, (x - hi.astype(F32)).astype(BF16)


def parted(x):
    hi = lax.reduce_precision(x, 8, 7)
    return hi.astype(BF16), (x - hi).astype(BF16)


def dot3(a, b, dims=NN):
    one = functools.partial(lax.dot_general, dimension_numbers=dims, preferred_element_type=F32)
    rows = a[0].shape[0]
    both = jnp.concatenate(a, axis=0) if isinstance(a, (tuple, list)) else a.reshape(2 * rows, a.shape[2])
    part = one(both, b[0])
    return part[:rows] + (part[rows:] + one(a[0], b[1]))


TILE = (256, 512)
OWN, PARTNER, SECOND, THIRD, PARENT, CORE, NEAR, EDGE = 0, 4, 5, 6, 7, 8, 9, 10
VMEM = pltpu.VMEM
STAYS = pl.BlockSpec(memory_space=VMEM)


def resident(x):
    return pltpu.with_memory_space_constraint(x, VMEM)


def outside(x):
    return pltpu.with_memory_space_constraint(x, pltpu.HBM)


def column(ref, i, size):
    return ref.at[..., pl.ds(pl.multiple_of(i * size, size), size)]


def multiply(out, a, b, dims, add=None):
    right = dims[0][1][0]
    for m in range(0, out.shape[0], TILE[0]):
        rows = slice(m, m + TILE[0])
        for n in range(0, out.shape[1], TILE[1]):
            cols = slice(n, n + TILE[1])
            b_part = [x[:, cols] if right == 0 else x[cols] for x in b]
            value = dot3((a[0, rows], a[1, rows]), b_part, dims)
            out[rows, cols] = value if add is None else add[rows, cols] + value


def call(kernel, grid, prefetch, ins, outs, shapes, name, scratch=(), aliases=None, after=(), through=(), keep=False, limit=24):
    n_in, n_out = len(ins), len(outs)
    extra = len(after) + len(through)
    anywhere = pl.BlockSpec(memory_space=pl.ANY)

    def body(*refs):
        start = prefetch + n_in
        stop = start + extra + n_out
        kernel(*refs[:start], *refs[start + extra : stop], *refs[stop + len(through) :])

    aliases = dict(aliases or {})
    for t in range(len(through)):
        aliases[prefetch + n_in + len(after) + t] = n_out + t
    built = pl.pallas_call(
        body,
        grid_spec=pltpu.PrefetchScalarGridSpec(
            num_scalar_prefetch=prefetch,
            grid=grid,
            in_specs=list(ins) + [anywhere] * extra,
            out_specs=list(outs) + [anywhere] * len(through),
            scratch_shapes=scratch,
        ),
        out_shape=[x if isinstance(x, pl.MemoryRef) else jax.ShapeDtypeStruct(*x) for x in shapes]
        + [(VMEM if keep else jax.ShapeDtypeStruct)(x.shape, x.dtype) for x in through],
        input_output_aliases=aliases,
        compiler_params=pltpu.CompilerParams(vmem_limit_bytes=limit * 2**20),
        cost_estimate=pl.CostEstimate(flops=1, bytes_accessed=1, transcendentals=0),
        name=name,
    )

    def run(*args):
        placed = [resident(x) if spec is STAYS else x for spec, x in zip(ins, args[prefetch:])]
        return built(*args[:prefetch], *placed, *after, *[resident(x) if keep else x for x in through])

    return run


def whole(*shape):
    return pl.BlockSpec(shape, lambda *_: (0,) * len(shape))


def lower(n):
    return [(i, j) for i in range(n) for j in range(i + 1)]


def dense_kernel(blk, step, width, where, acol, bcol, a_ref, b_ref, fh, fl, u):
    i = pl.program_id(0)
    orders = fh.shape[1] - width
    rows = u.shape[1] - orders
    for ref in (fh, fl):
        ref[...] = jnp.zeros_like(ref)
    diag = lax.broadcasted_iota(jnp.int32, (blk, blk), 0) == lax.broadcasted_iota(jnp.int32, (blk, blk), 1)
    eye = jnp.where(diag, 0.75, 0.0).astype(F32)
    for t in range(step // blk):
        row = i * (step // blk) + t
        at = slice(t * blk, (t + 1) * blk)
        for s in range(a_ref.shape[1]):
            col = acol[0, row, s]
            block = a_ref[t, s] + eye if s == 0 else a_ref[t, s]
            to = pl.ds(pl.multiple_of(col * blk, blk), blk)
            fh[at, to], fl[at, to] = split(block)
        for s in range(b_ref.shape[1]):
            to = pl.ds(pl.multiple_of(width + bcol[0, row, s] * blk, blk), blk)
            fh[at, to], fl[at, to] = split(b_ref[t, s])

    own = pl.ds(pl.multiple_of(where[0] * rows, rows), rows)
    for p, f in enumerate((fh, fl)):
        for to, cols in ((slice(0, orders), slice(width, None)), (slice(orders, None), own)):
            part = f[:, cols]
            n = part.shape[1]
            diag = lax.broadcasted_iota(jnp.int32, (n, n), 0) == lax.broadcasted_iota(jnp.int32, (n, n), 1)
            one = jnp.where(diag, 1.0, 0.0).astype(BF16)
            u[p, to, pl.ds(pl.multiple_of(i * step, step), step)] = lax.dot_general(one, part, NT, preferred_element_type=F32).astype(BF16)


def dense(where, rows, a_blocks, a_cols, b_blocks, b_cols, orders, after):
    count, nnza, blk, _ = a_blocks.shape
    nnzb = b_blocks.shape[1]
    width = count * blk
    step = 2 * blk
    total = width + orders
    factor = pl.BlockSpec((step, total), lambda i, *_: (i, 0))
    return call(
        functools.partial(dense_kernel, blk, step, width),
        (width // step,),
        3,
        [
            pl.BlockSpec((2, nnza, blk, blk), lambda i, *_: (i, 0, 0, 0)),
            pl.BlockSpec((2, nnzb, blk, blk), lambda i, *_: (i, 0, 0, 0)),
        ],
        [factor, factor, STAYS],
        [pltpu.HBM((width, total), BF16)] * 2 + [VMEM((2, rows + orders, width), BF16)],
        "dense",
        after=after,
    )(where, a_cols, b_cols, outside(a_blocks), outside(b_blocks))


def inverse_block(m):
    n = m.shape[0]
    sub = lax.broadcasted_iota(jnp.int32, (8, n), 0)
    lane = lax.broadcasted_iota(jnp.int32, (8, n), 1)
    strips = [m[i : i + 8] for i in range(0, n, 8)]

    def along(v, j):
        return jnp.broadcast_to(v[:, j : j + 1], (8, n))

    def down(v, t):
        return jnp.broadcast_to(v[t : t + 1], (8, n))

    for q in range(n // 8):
        panel = strips[q]
        cols = [along(panel, 8 * q + b) for b in range(8)]
        for t in range(8):
            here = sub == t
            inv = 1.0 / down(cols[t], t)

            def reduced(v):
                r = down(v, t) * inv
                return jnp.where(here, r, v - cols[t] * r)

            panel = reduced(jnp.where(lane == 8 * q + t, jnp.where(here, 1.0, 0.0), panel))
            cols[t + 1 :] = [reduced(v) for v in cols[t + 1 :]]
        inside = (lane >= 8 * q) & (lane < 8 * q + 8)
        rows = [down(panel, b) for b in range(8)]
        for i in range(q + 1, q + n // 8):
            old = strips[i % (n // 8)]
            terms = [along(old, 8 * q + b) * rows[b] for b in range(8)]
            while len(terms) > 1:
                terms = [x + y for x, y in zip(terms[::2], terms[1::2])]
            strips[i % (n // 8)] = jnp.where(inside, 0.0, old) - terms[0]
        strips[q] = panel
    return jnp.concatenate(strips, axis=0)


def inverse_kernel(blk, mine, other, d_ref, out):
    n = out.shape[0]
    def dot(a, b):
        return dot3(split(a), split(b))

    diag = lax.broadcasted_iota(jnp.int32, (n, n), 0) == lax.broadcasted_iota(jnp.int32, (n, n), 1)
    out[...] = mine[...] + other[...] + jnp.where(diag, d_ref[...], 0.0)

    place = lax.broadcasted_iota(jnp.int32, (n, blk), 0) // blk

    @pl.loop(0, n // blk)
    def _(b):
        here = pl.ds(pl.multiple_of(b * blk, blk), blk)
        inv = inverse_block(out[here, here])
        row = dot(inv, out[here, :])
        out[...] -= dot(out[:, here], row)
        col = row.T
        out[:, here] = jnp.where(place < b, col, -col)
        out[here, :] = row
        out[here, here] = inv


def inverse(mine, other, control_cost, blk):
    n = control_cost.shape[0]
    return call(
        functools.partial(inverse_kernel, blk),
        (1,),
        0,
        [whole(n, n)] * 2 + [whole(1, n)],
        [whole(n, n)],
        [((n, n), F32)],
        "inverse",
        limit=10,
    )(mine, other, control_cost[None])[0]


def tiled(block, blk):
    n = block.shape[0] // blk
    return [block[i * blk : (i + 1) * blk, j * blk : (j + 1) * blk] for i in range(n) for j in range(n)]


def pack_kernel(blk, where, own, *refs):
    *blocks, out = refs
    diag = [own[i * blk : (i + 1) * blk, j * blk : (j + 1) * blk] for i, j in lower(own.shape[0] // blk)]
    for t, tile in enumerate(diag + [tile for block in blocks for tile in tiled(block, blk)]):
        out[t] = tile


def pack(where, blocks, cost_rows, blk, after):
    rows = cost_rows.shape[0]
    size = len(lower(rows // blk)) + len(blocks) * (rows // blk) ** 2
    specs = [
        pl.BlockSpec((rows, rows), functools.partial(lambda t, i, where: (0, where[t]), t)) for t in (OWN, *blocks)
    ]
    return call(
        functools.partial(pack_kernel, blk),
        (1,),
        1,
        specs,
        [whole(size, blk, blk)],
        [((size, blk, blk), F32)],
        "pack",
        after=after,
        limit=16,
    )(where, *[outside(cost_rows)] * len(specs))[0]


def half_state(where, parent_state, after):
    _, rows, samples = parent_state.shape

    def kernel(where, x, out):
        out[...] = x[0]

    return call(
        kernel,
        (1,),
        1,
        [pl.BlockSpec((1, rows // 2, samples), lambda i, where: (where[PARENT], where[CORE], 0))],
        [whole(rows // 2, samples)],
        [((rows // 2, samples), F32)],
        "half_state",
        after=after,
        limit=4,
    )(where, outside(parent_state))[0]


def front(message, size):
    shape = (size,) + message.shape[1:]

    def kernel(x, out):
        out[...] = x[...]

    return call(kernel, (1,), 0, [whole(*shape)], [whole(*shape)], [(shape, F32)], "front", limit=4)(message)[0]


def unpack(tiles, step, n, xh, xl):
    blk = tiles.shape[1]
    lead = len(lower(n))
    for t, (i, j) in enumerate(lower(n) if step == 0 else [(i, j) for i in range(n) for j in range(n)]):
        tile = tiles[t if step == 0 else lead + (step - 1) * n * n + t]
        places = [(i, j, tile)] + ([(j, i, tile.T)] if step == 0 and i != j else [])
        for r, c, value in places:
            at = slice(r * blk, (r + 1) * blk), slice(c * blk, (c + 1) * blk)
            xh[at], xl[at] = split(value)


def collect(halves, after):
    count = len(halves)
    rows, samples = halves[0].shape

    def kernel(*refs):
        for t in range(count):
            refs[count][t] = refs[t][...]

    return call(
        kernel,
        (1,),
        0,
        [whole(rows, samples)] * count,
        [whole(count, rows, samples)],
        [((count, rows, samples), F32)],
        "collect",
        after=[after],
        limit=4,
    )(*halves)[0]


def drift_kernel(where, own, mine, other, fh, fl, x_ref, out):
    g = pl.program_id(0)
    core = where[CORE]
    half = mine.shape[1]

    @pl.when(g == 0)
    def _():
        x_ref[...] = own[0]

    for d in range(3):

        @pl.when(g == d + 1)
        def _():
            x_ref[pl.ds(pl.multiple_of(core * half, half), half)] = mine[d]
            x_ref[pl.ds(pl.multiple_of((1 - core) * half, half), half)] = other[d]

    part = dot3((fh[...], fl[...]), split(x_ref[...]))

    @pl.when(g == 0)
    def _():
        out[...] = part

    @pl.when(g > 0)
    def _():
        out[...] += part


def drift(where, parent_state, mine, other, fh, fl, after):
    _, rows, samples = parent_state.shape
    factor = pl.BlockSpec((rows, rows), lambda g, where: (where[OWN], where[OWN + g]))
    return call(
        drift_kernel,
        (4,),
        1,
        [pl.BlockSpec((1, rows, samples), lambda g, where: (where[PARENT], 0, 0))]
        + [whole(*mine.shape)] * 2
        + [factor, factor],
        [pl.BlockSpec((rows, samples), lambda g, where: (where[OWN + g], 0)), whole(rows, samples)],
        [((4 * rows, samples), F32), ((rows, samples), F32)],
        "drift",
        after=[after],
        limit=12,
    )(where, outside(parent_state), mine, other, outside(fh), outside(fl))


def passed(arrays, *after, keep=False):
    return call(lambda *_: None, (1,), 0, [], [], [], "passed", after=after, through=arrays, keep=keep, limit=1)()


def begin_kernel(steps, where, weight, p_ref, u, fh, fl, bh, bl, n_out, s_out, g_out, h_out, token, mine, pair, ph, pl_):
    g = pl.program_id(0)
    token[...] = jnp.zeros_like(token)
    rows = ph.shape[0]
    orders = g_out.shape[0]
    tile = fh.shape[1]

    @pl.when(g < steps)
    def _():
        ph[...], pl_[...] = split(p_ref[...])

        @pl.when(g == 0)
        def _():
            mine[...] = jnp.zeros_like(mine)

        multiply(mine, column(u, g, rows), (ph, pl_), NT, mine)

        @pl.when(g != where[0])
        def _():
            multiply(column(n_out, g, rows), column(u, where[0], rows), (ph, pl_), NN)

    @pl.when(g == steps)
    def _():
        pair[0], pair[1] = split(mine[...] * weight[0])
        h_out[...] = dot3(pair[:, :orders], (bh[...], bl[...]))

    @pl.when(g >= steps)
    def _():
        multiply(column(g_out, g - steps, tile), pair.at[:, :orders], (fh, fl), NN)
        multiply(column(s_out, g - steps, tile), pair.at[:, orders:], (fh, fl), NN)


def begin(where, weight, cost_rows, u, fh, fl):
    rows, width = cost_rows.shape
    tall = u.shape[1]
    orders = tall - rows
    steps = width // rows
    tile = 512
    factor = pl.BlockSpec((rows, tile), lambda g, where, _: (where[0], jnp.maximum(g - steps, 0)))
    control = pl.BlockSpec((rows, orders), lambda g, where, _: (where[0], width // orders))
    return call(
        functools.partial(begin_kernel, steps),
        (steps + width // tile,),
        2,
        [
            pl.BlockSpec((rows, rows), lambda g, *_: (0, jnp.minimum(g, steps - 1))),
            STAYS,
            factor,
            factor,
            control,
            control,
        ],
        [STAYS] * 4 + [whole(8, 128)],
        [VMEM((tall, width), F32), VMEM((rows, width), F32), VMEM((orders, width), F32), VMEM((orders, orders), F32)]
        + [((8, 128), F32)],
        "begin",
        [VMEM((tall, rows), F32), VMEM((2, tall, rows), BF16)] + [VMEM((rows, rows), BF16)] * 2,
        limit=18,
    )(where, weight, outside(cost_rows), u, *[outside(f) for f in (fh, fl, fh, fl)])


def stage_kernel(options, size, focus, where, weight, *refs):
    arrived = refs[:options]
    u, n_in, fh, fl, bh, bl, s_in, g_in, h_in, *refs = refs[options:]
    if size > 1:
        s_out, g_out, h_out, n_out, token, done, pair, xh, xl = refs
    else:
        s_out, g_out, h_out, token, done, pair, xh, xl = refs
    g = pl.program_id(0)
    token[...] = jnp.zeros_like(token)
    rows = xh.shape[0]
    orders = g_out.shape[0]
    tile = fh.shape[1]
    f = where[focus]
    v = column(u, f, rows)
    for c in range(options):
        for t in range(size):

            @pl.when((g == t) & ((where[EDGE] == c) | (options == 1)))
            def _():
                unpack(arrived[c], t, rows // arrived[c].shape[1], xh, xl)

    @pl.when(g == 0)
    def _():
        multiply(done, v, (xh, xl), NN, column(n_in, f, rows))

    if size > 1:

        @pl.when((g > 0) & (g < size))
        def _():
            c = where[focus + g]
            multiply(done, column(u, c, rows), (xh, xl), NT, done)
            multiply(column(n_out, c, rows), v, (xh, xl), NN, column(n_in, c, rows))

    @pl.when(g == size)
    def _():
        pair[0], pair[1] = split(done[...] * weight[0])
        h_out[...] = h_in[...] + dot3(pair[:, :orders], (bh[...], bl[...]))

    @pl.when(g >= size)
    def _():
        at = g - size
        multiply(column(g_out, at, tile), pair.at[:, :orders], (fh, fl), NN, column(g_in, at, tile))
        multiply(column(s_out, at, tile), pair.at[:, orders:], (fh, fl), NN, column(s_in, at, tile))


def stage(where, weight, arrived, focus, size, u, n, fh, fl, sums, after=()):
    tall, width = n.shape
    rows, orders = sums[0].shape[0], sums[1].shape[0]
    tile = 512
    factor = pl.BlockSpec((rows, tile), lambda g, where, _: (where[focus], jnp.maximum(g - size, 0)))
    control = pl.BlockSpec((rows, orders), lambda g, where, _: (where[focus], width // orders))
    first = 2 + len(arrived)
    more = size > 1
    shapes = [VMEM((rows, width), F32), VMEM((orders, width), F32), VMEM((orders, orders), F32)]
    return call(
        functools.partial(stage_kernel, len(arrived), size, focus),
        (size + width // tile,),
        2,
        [whole(*x.shape) for x in arrived] + [STAYS, STAYS, factor, factor, control, control] + [STAYS] * 3,
        [STAYS] * (3 + more) + [whole(8, 128)],
        shapes + [VMEM((tall, width), F32)] * more + [((8, 128), F32)],
        "stage",
        [VMEM((tall, rows), F32), VMEM((2, tall, rows), BF16)] + [VMEM((rows, rows), BF16)] * 2,
        {first + 6: 0, first + 7: 1, first + 8: 2, **({first + 1: 3} if more else {})},
        after,
        limit=20,
    )(where, weight, *arrived, u, n, *[outside(f) for f in (fh, fl, fh, fl)], *sums)


def final_kernel(where, h_ref, s_own, g_own, g2, s2, q2, d_ref, x_ref, y_ref, bh, bl, gain, out, reached, pair, q):
    n = pl.program_id(0)
    rows = out.shape[0]

    @pl.when(n == 0)
    def _():
        value = -dot3(split(h_ref[...]), split(column(g_own, where[0], rows)[...] + g2[...]))
        gain[...] = value
        pair[0], pair[1] = split(value.T)
        q[...] = jnp.zeros_like(q)

    cross = split(column(g_own, n, rows)[...] + q2[...])
    part = column(s_own, n, rows)[...] + s2[...] + dot3(pair[...], cross)
    diag = lax.broadcasted_iota(jnp.int32, (rows, rows), 0) == lax.broadcasted_iota(jnp.int32, (rows, rows), 1)
    out[...] = part + jnp.where(diag & (n == where[0]), d_ref[...], 0.0)
    q[...] += dot3(cross, split(x_ref[...]))

    @pl.when(n == pl.num_programs(0) - 1)
    def _():
        u = -dot3(split(h_ref[...]), split(q[...]))
        reached[...] = y_ref[...] + dot3((bh[...], bl[...]), split(u))


def final(where, hinv, own, other, state_cost, x, y, fh, fl):
    rows, width = own[0].shape
    orders = own[1].shape[0]
    samples = x.shape[1]
    s_spec = pl.BlockSpec((rows, rows), lambda n, where: (0, n))
    g_spec = pl.BlockSpec((orders, rows), lambda n, where: (0, n))
    mine = pl.BlockSpec((orders, rows), lambda n, where: (0, where[0]))
    factor = pl.BlockSpec((rows, orders), lambda n, where: (where[0], width // orders))
    return call(
        final_kernel,
        (width // rows,),
        1,
        [whole(orders, orders), STAYS, STAYS, mine, s_spec, g_spec, whole(1, rows)]
        + [pl.BlockSpec((rows, samples), lambda n, where: (n, 0)), whole(rows, samples), factor, factor],
        [whole(orders, rows), s_spec, whole(rows, samples)],
        [((orders, rows), F32), ((rows, width), F32), ((rows, samples), F32)],
        "final",
        [pltpu.VMEM((2, rows, orders), BF16), pltpu.VMEM((orders, samples), F32)],
    )(where, hinv, *own, other[1], *other, state_cost[None], x, y, outside(fh), outside(fl))


def image_kernel(where, weight, fh, fl, p_ref, out, acc):
    k = pl.program_id(0)
    part = dot3(split(p_ref[...]), (fh[...], fl[...]))

    @pl.when(k == 0)
    def _():
        acc[...] = part

    @pl.when(k > 0)
    def _():
        acc[...] += part

    @pl.when(k == pl.num_programs(0) - 1)
    def _():
        out[...] = acc[...].T * weight[0]


def image(where, weight, fh, fl, cost_rows):
    rows, width = cost_rows.shape
    chunk = 512
    factor = pl.BlockSpec((chunk, rows), lambda k, where, _: (k, where[0]))
    return call(
        image_kernel,
        (width // chunk,),
        2,
        [factor, factor, pl.BlockSpec((rows, chunk), lambda k, *_: (0, k))],
        [whole(rows, rows)],
        [((rows, rows), F32)],
        "image",
        [pltpu.VMEM((rows, rows), F32)],
    )(where, weight, fh, fl, cost_rows)[0]


def accumulate_kernel(first, where, y_ref, fh, fl, *refs):
    out = refs[-1]
    part = dot3(split(y_ref[...]), (fh[...], fl[...]))
    out[...] = part if first else refs[0][...] + part


def accumulate(where, y, fh, fl, acc):
    rows = y.shape[0]
    total = fh.shape[1]
    tile = 512
    first = acc is None
    spec = pl.BlockSpec((rows, tile), lambda n, where: (0, n))
    factor = pl.BlockSpec((rows, tile), lambda n, where: (where[0], n))
    return call(
        functools.partial(accumulate_kernel, first),
        (total // tile,),
        1,
        [whole(rows, rows), factor, factor] + [spec] * (not first),
        [spec],
        [((rows, total), F32)],
        "accumulate",
        aliases=None if first else {4: 0},
    )(where, y, fh, fl, *(() if first else (acc,)))[0]


def by_images(z, parts, weight, cost_rows, fh, fl):
    rows, width = cost_rows.shape
    acc = None
    for d in range(parts):
        block = image(((z + d) % parts)[None], weight, fh, fl, cost_rows)
        if d:
            block = lax.ppermute(block, "row", [(i, (i + d) % parts) for i in range(parts)])
        acc = accumulate(((z - d) % parts)[None], block, fh, fl, acc)
    cross = lax.all_gather(acc[:, width:], "row")
    return acc[:, :width], jnp.swapaxes(cross.reshape(width, -1), 0, 1)


def by_blocks(where, weight, cost_rows, parent_state, dense_parts, messages, half):
    fh, fl, u = dense_parts
    pair, mid = messages
    lead = 2 * mid.shape[0] - pair.shape[0]

    def moved(x, *pairs):
        return lax.ppermute(x, "row", pairs)

    def across(x):
        return moved(x, (1, 2), (2, 1))

    def to_end(x):
        return moved(x, (1, 0), (2, 3))

    pair = moved(pair, (0, 1), (1, 0), (2, 3), (3, 2))
    mid = across(mid)
    halves = [moved(half, *[(i, (i + d) % 4) for i in range(4)]) for d in range(1, 4)]
    n, *sums, token = begin(where, weight, cost_rows, u, fh, fl)
    (mid,) = passed([mid], token, *halves)
    end = to_end(mid)
    mid_last = across(front(pair, lead))
    *sums, n, token = stage(where, weight, [pair], PARTNER, 3, u, n, fh, fl, sums)
    (mid_last,) = passed([mid_last], token)
    end_last = to_end(mid_last)
    halves = collect(halves, token)
    x, y = drift(where, parent_state, halves, swapped(halves), fh, fl, token)
    *sums, n, token = stage(where, weight, [mid, end], SECOND, 2, u, n, fh, fl, sums, [y])
    s, g, h, token = stage(where, weight, [mid_last, end_last], THIRD, 1, u, n, fh, fl, sums)
    other = swapped(h)
    return h, other, passed([s, g], other, keep=True), x, y


def swapped(x):
    n = lax.axis_size("leaf")
    return lax.ppermute(x, "leaf", [(i, i ^ 1) for i in range(n)])


def shards(
    leaf_cost,
    a_blocks,
    a_cols,
    b_blocks,
    b_cols,
    branch_prob,
    state_cost,
    control_cost,
    parent_state,
):
    cost_rows = leaf_cost[0]
    rows, width = cost_rows.shape
    blk = a_blocks.shape[3]
    orders = control_cost.shape[0]
    parts = lax.axis_size("row")
    z = lax.axis_index("row")
    leaf = lax.axis_index("leaf")
    line = parts == 4 and rows == orders

    left = z < 2
    near = jnp.where(left, 0, 3)
    edge = ((z == 0) | (z == 3)).astype(jnp.int32)
    before = [(z - d) % 4 for d in range(4)]
    where = jnp.stack([*before, z ^ 1, jnp.where(left, 2, 1), 3 - near, leaf // 2, leaf % 2, near, edge])
    sent = []
    if line:
        sent.append(pack(where, [SECOND, THIRD], cost_rows, blk, []))
        sent.append(pack(where, [NEAR], cost_rows, blk, sent))
        sent.append(half_state(where, parent_state, sent[1:]))
    fh, fl, u = parts_of = dense(where, rows, a_blocks[0], a_cols, b_blocks[0], b_cols, orders, sent)
    if line:
        h, other_h, own, x, y = by_blocks(where, branch_prob, cost_rows, parent_state, parts_of, sent[:2], sent[2])
    else:
        w = dot3(parted(cost_rows), (fh[:, width:], fl[:, width:]))
        b_rows = [lax.dynamic_slice(f, (0, z * rows), (orders, rows)) for f in u]
        h = lax.psum(dot3(b_rows, parted(w)) * branch_prob[0], "row")
        other_h = swapped(h)
        own = by_images(z, parts, branch_prob, cost_rows, fh, fl)
        own_state = lax.dynamic_index_in_dim(parent_state, leaf // 2, 0, keepdims=False)
        x = lax.all_gather(own_state, "row", tiled=True)
        y = dot3([lax.dynamic_slice(f, (z * rows, 0), (rows, width)) for f in (fh, fl)], parted(x))
    hinv = inverse(h, other_h, control_cost, blk)
    other = tuple(swapped(x) for x in own)
    gain, pcost, reached = final(where, hinv, own, other, state_cost, x, y, fh, fl)
    return pcost[None], gain[None], reached[None]


def solution(mesh):
    placed = (
        P("leaf", "row", None),
        P("leaf", None, None, None, None),
        P("leaf", None, None),
        P("leaf", None, None, None, None),
        P("leaf", None, None),
        P("leaf"),
        P("row"),
        P(),
        P(None, "row", None),
    )
    return jax.shard_map(
        shards,
        mesh=mesh,
        in_specs=placed,
        out_specs=(P("leaf", "row", None), P("leaf", None, "row"), P("leaf", "row", None)),
        check_vma=False,
    )
```

```python
import functools

import jax
import jax.numpy as jnp
from jax import lax
from jax.experimental import pallas as pl
from jax.experimental.pallas import tpu as pltpu
from jax.sharding import PartitionSpec as P

F32 = jnp.float32
BF16 = jnp.bfloat16
NN = (((1,), (0,)), ((), ()))
NT = (((1,), (1,)), ((), ()))


def split(x):
    hi = x.astype(BF16)
    return hi, (x - hi.astype(F32)).astype(BF16)


def parted(x):
    hi = lax.reduce_precision(x, 8, 7)
    return hi.astype(BF16), (x - hi).astype(BF16)


def dot3(a, b, dims=NN):
    one = functools.partial(lax.dot_general, dimension_numbers=dims, preferred_element_type=F32)
    rows = a[0].shape[0]
    both = jnp.concatenate(a, axis=0) if isinstance(a, (tuple, list)) else a.reshape(2 * rows, a.shape[2])
    part = one(both, b[0])
    return part[:rows] + (part[rows:] + one(a[0], b[1]))


TILE = (256, 512)
OWN, PARTNER, SECOND, THIRD, PARENT, CORE, NEAR, EDGE = range(8)
VMEM = pltpu.VMEM
STAYS = pl.BlockSpec(memory_space=VMEM)


def resident(x):
    return pltpu.with_memory_space_constraint(x, VMEM)


def outside(x):
    return pltpu.with_memory_space_constraint(x, pltpu.HBM)


def column(ref, i, size):
    return ref.at[..., pl.ds(pl.multiple_of(i * size, size), size)]


def multiply(out, a, b, dims, add=None):
    right = dims[0][1][0]
    for m in range(0, out.shape[0], TILE[0]):
        rows = slice(m, m + TILE[0])
        for n in range(0, out.shape[1], TILE[1]):
            cols = slice(n, n + TILE[1])
            b_part = [x[:, cols] if right == 0 else x[cols] for x in b]
            value = dot3((a[0, rows], a[1, rows]), b_part, dims)
            out[rows, cols] = value if add is None else add[rows, cols] + value


def call(kernel, grid, prefetch, ins, outs, shapes, name, scratch=(), aliases=None, after=(), through=(), keep=False, limit=24):
    n_in, n_out = len(ins), len(outs)
    extra = len(after) + len(through)
    anywhere = pl.BlockSpec(memory_space=pl.ANY)

    def body(*refs):
        start = prefetch + n_in
        stop = start + extra + n_out
        kernel(*refs[:start], *refs[start + extra : stop], *refs[stop + len(through) :])

    aliases = dict(aliases or {})
    for t in range(len(through)):
        aliases[prefetch + n_in + len(after) + t] = n_out + t
    built = pl.pallas_call(
        body,
        grid_spec=pltpu.PrefetchScalarGridSpec(
            num_scalar_prefetch=prefetch,
            grid=grid,
            in_specs=list(ins) + [anywhere] * extra,
            out_specs=list(outs) + [anywhere] * len(through),
            scratch_shapes=scratch,
        ),
        out_shape=[x if isinstance(x, pl.MemoryRef) else jax.ShapeDtypeStruct(*x) for x in shapes]
        + [(VMEM if keep else jax.ShapeDtypeStruct)(x.shape, x.dtype) for x in through],
        input_output_aliases=aliases,
        compiler_params=pltpu.CompilerParams(vmem_limit_bytes=limit * 2**20),
        cost_estimate=pl.CostEstimate(flops=1, bytes_accessed=1, transcendentals=0),
        name=name,
    )

    def run(*args):
        placed = [resident(x) if spec is STAYS else x for spec, x in zip(ins, args[prefetch:])]
        return built(*args[:prefetch], *placed, *after, *[resident(x) if keep else x for x in through])

    return run


def whole(*shape):
    return pl.BlockSpec(shape, lambda *_: (0,) * len(shape))


def lower(n):
    return [(i, j) for i in range(n) for j in range(i + 1)]


def dense_kernel(blk, step, width, where, acol, bcol, a_ref, b_ref, fh, fl, u):
    i = pl.program_id(0)
    orders = fh.shape[1] - width
    rows = u.shape[1] - orders
    for ref in (fh, fl):
        ref[...] = jnp.zeros_like(ref)
    diag = lax.broadcasted_iota(jnp.int32, (blk, blk), 0) == lax.broadcasted_iota(jnp.int32, (blk, blk), 1)
    eye = jnp.where(diag, 0.75, 0.0).astype(F32)
    for t in range(step // blk):
        row = i * (step // blk) + t
        at = slice(t * blk, (t + 1) * blk)
        for s in range(a_ref.shape[1]):
            col = acol[0, row, s]
            block = a_ref[t, s] + eye if s == 0 else a_ref[t, s]
            to = pl.ds(pl.multiple_of(col * blk, blk), blk)
            fh[at, to], fl[at, to] = split(block)
        for s in range(b_ref.shape[1]):
            to = pl.ds(pl.multiple_of(width + bcol[0, row, s] * blk, blk), blk)
            fh[at, to], fl[at, to] = split(b_ref[t, s])

    own = pl.ds(pl.multiple_of(where[0] * rows, rows), rows)
    for p, f in enumerate((fh, fl)):
        for to, cols in ((slice(0, orders), slice(width, None)), (slice(orders, None), own)):
            part = f[:, cols]
            n = part.shape[1]
            diag = lax.broadcasted_iota(jnp.int32, (n, n), 0) == lax.broadcasted_iota(jnp.int32, (n, n), 1)
            one = jnp.where(diag, 1.0, 0.0).astype(BF16)
            u[p, to, pl.ds(pl.multiple_of(i * step, step), step)] = lax.dot_general(one, part, NT, preferred_element_type=F32).astype(BF16)


def dense(where, rows, a_blocks, a_cols, b_blocks, b_cols, orders, after):
    count, nnza, blk, _ = a_blocks.shape
    nnzb = b_blocks.shape[1]
    width = count * blk
    step = 2 * blk
    total = width + orders
    factor = pl.BlockSpec((step, total), lambda i, *_: (i, 0))
    return call(
        functools.partial(dense_kernel, blk, step, width),
        (width // step,),
        3,
        [
            pl.BlockSpec((2, nnza, blk, blk), lambda i, *_: (i, 0, 0, 0)),
            pl.BlockSpec((2, nnzb, blk, blk), lambda i, *_: (i, 0, 0, 0)),
        ],
        [factor, factor, STAYS],
        [pltpu.HBM((width, total), BF16)] * 2 + [VMEM((2, rows + orders, width), BF16)],
        "dense",
        after=after,
    )(where, a_cols, b_cols, outside(a_blocks), outside(b_blocks))


def inverse_block(m):
    n = m.shape[0]
    sub = lax.broadcasted_iota(jnp.int32, (8, n), 0)
    lane = lax.broadcasted_iota(jnp.int32, (8, n), 1)
    strips = [m[i : i + 8] for i in range(0, n, 8)]

    def along(v, j):
        return jnp.broadcast_to(v[:, j : j + 1], (8, n))

    def down(v, t):
        return jnp.broadcast_to(v[t : t + 1], (8, n))

    for q in range(n // 8):
        panel = strips[q]
        cols = [along(panel, 8 * q + b) for b in range(8)]
        for t in range(8):
            here = sub == t
            inv = 1.0 / down(cols[t], t)

            def reduced(v):
                r = down(v, t) * inv
                return jnp.where(here, r, v - cols[t] * r)

            panel = reduced(jnp.where(lane == 8 * q + t, jnp.where(here, 1.0, 0.0), panel))
            cols[t + 1 :] = [reduced(v) for v in cols[t + 1 :]]
        inside = (lane >= 8 * q) & (lane < 8 * q + 8)
        rows = [down(panel, b) for b in range(8)]
        for i in range(q + 1, q + n // 8):
            old = strips[i % (n // 8)]
            terms = [along(old, 8 * q + b) * rows[b] for b in range(8)]
            while len(terms) > 1:
                terms = [x + y for x, y in zip(terms[::2], terms[1::2])]
            strips[i % (n // 8)] = jnp.where(inside, 0.0, old) - terms[0]
        strips[q] = panel
    return jnp.concatenate(strips, axis=0)


def inverse_kernel(blk, mine, other, d_ref, out):
    n = out.shape[0]
    def dot(a, b):
        return dot3(split(a), split(b))

    diag = lax.broadcasted_iota(jnp.int32, (n, n), 0) == lax.broadcasted_iota(jnp.int32, (n, n), 1)
    out[...] = mine[...] + other[...] + jnp.where(diag, d_ref[...], 0.0)

    place = lax.broadcasted_iota(jnp.int32, (n, blk), 0) // blk

    @pl.loop(0, n // blk)
    def _(b):
        here = pl.ds(pl.multiple_of(b * blk, blk), blk)
        inv = inverse_block(out[here, here])
        row = dot(inv, out[here, :])
        out[...] -= dot(out[:, here], row)
        col = row.T
        out[:, here] = jnp.where(place < b, col, -col)
        out[here, :] = row
        out[here, here] = inv


def inverse(mine, other, control_cost, blk):
    n = control_cost.shape[0]
    return call(
        functools.partial(inverse_kernel, blk),
        (1,),
        0,
        [whole(n, n)] * 2 + [whole(1, n)],
        [whole(n, n)],
        [((n, n), F32)],
        "inverse",
        limit=6,
    )(mine, other, control_cost[None])[0]


def folded(block, blk):
    n = block.shape[0] // blk
    half = blk // 2
    tiles = {(i, j): block[i * blk : (i + 1) * blk, j * blk : (j + 1) * blk] for i, j in lower(n)}
    last = tiles.pop((n - 1, n - 1))
    for d, (r, c) in enumerate(((0, 0), (half, 0), (half, half))):
        tile, part = tiles[d, d], last[r : r + half, c : c + half]
        top = jnp.concatenate((tile[:half, :half], part), axis=1)
        tiles[d, d] = jnp.concatenate((top, tile[half:]), axis=0)
    return list(tiles.values())


def unfolded(tiles, n):
    half = tiles.shape[1] // 2
    out = {place: tiles[t] for t, place in enumerate(lower(n)[:-1])}
    parts = [out[d, d][:half, half:] for d in range(3)]
    for d in range(3):
        tile = out[d, d]
        top = jnp.concatenate((tile[:half, :half], tile[half:, :half].T), axis=1)
        out[d, d] = jnp.concatenate((top, tile[half:]), axis=0)
    top = jnp.concatenate((parts[0], parts[1].T), axis=1)
    out[n - 1, n - 1] = jnp.concatenate((top, jnp.concatenate(parts[1:], axis=1)), axis=0)
    return [out[place] for place in lower(n)]


def tiled(block, blk):
    n = block.shape[0] // blk
    return [block[i * blk : (i + 1) * blk, j * blk : (j + 1) * blk] for i in range(n) for j in range(n)]


def pack_kernel(blk, where, own, x_ref, *refs):
    *blocks, out = refs
    diag = folded(own[...], blk)
    x = [x_ref[0, :blk], x_ref[0, blk:]]
    for t, tile in enumerate(diag + x + [tile for block in blocks for tile in tiled(block, blk)]):
        out[t] = tile


def pack(where, blocks, cost_rows, parent_state, blk, after):
    rows = cost_rows.shape[0]
    samples = parent_state.shape[2]
    picks = [OWN, *blocks]
    size = len(lower(rows // blk)) + 1 + (len(picks) - 1) * (rows // blk) ** 2
    specs = [pl.BlockSpec((rows, rows), functools.partial(lambda t, i, where: (0, where[t]), t)) for t in picks]
    specs.insert(1, pl.BlockSpec((1, rows // 2, samples), lambda i, where: (where[PARENT], where[CORE], 0)))
    args = [outside(cost_rows)] * len(picks)
    args.insert(1, outside(parent_state))
    return call(
        functools.partial(pack_kernel, blk),
        (1,),
        1,
        specs,
        [whole(size, blk, blk)],
        [((size, blk, blk), F32)],
        "pack",
        after=after,
        limit=16,
    )(where, *args)[0]


def front(message, size):
    shape = (size,) + message.shape[1:]

    def kernel(x, out):
        out[...] = x[...]

    return call(kernel, (1,), 0, [whole(*shape)], [whole(*shape)], [(shape, F32)], "front", limit=4)(message)[0]


def unpack(tiles, step, n, xh, xl):
    blk = tiles.shape[1]
    lead = len(lower(n)) - 1
    diag = unfolded(tiles, n) if step == 0 else None
    for t, (i, j) in enumerate(lower(n) if step == 0 else [(i, j) for i in range(n) for j in range(n)]):
        tile = diag[t] if step == 0 else tiles[lead + 2 + (step - 1) * n * n + t]
        places = [(i, j, tile)] + ([(j, i, tile.T)] if step == 0 and i != j else [])
        for r, c, value in places:
            at = slice(r * blk, (r + 1) * blk), slice(c * blk, (c + 1) * blk)
            xh[at], xl[at] = split(value)


def collect_kernel(where, pair, mid, end, mid_last, end_last, out):
    lead = mid_last.shape[0] - 2
    out[:2] = pair[lead : lead + 2]

    @pl.when(where[EDGE] == 1)
    def _():
        out[2:4] = end[lead : lead + 2]
        out[4:6] = end_last[lead : lead + 2]

    @pl.when(where[EDGE] == 0)
    def _():
        out[2:4] = mid[lead : lead + 2]
        out[4:6] = mid_last[lead : lead + 2]


def collect(where, messages, after):
    blk = messages[0].shape[1]
    lead = messages[3].shape[0] - 2
    return call(
        collect_kernel,
        (1,),
        1,
        [pl.BlockSpec((lead + 2, blk, blk), lambda i, where: (0, 0, 0))] * 5,
        [whole(6, blk, blk)],
        [((6, blk, blk), F32)],
        "collect",
        after=[after],
        limit=10,
    )(where, *messages)[0]


def drift_kernel(where, own, mine, other, fh, fl, x_ref, out):
    g = pl.program_id(0)
    core = where[CORE]
    blk = mine.shape[1]
    rows = own.shape[1]

    @pl.when(g == 0)
    def _():
        x_ref[...] = own[0]

    for d in range(3):

        @pl.when(g == d + 1)
        def _():
            for t in range(2):
                x_ref[pl.ds(pl.multiple_of(core * (rows // 2) + t * blk, blk), blk)] = mine[2 * d + t]
                x_ref[pl.ds(pl.multiple_of((1 - core) * (rows // 2) + t * blk, blk), blk)] = other[2 * d + t]

    part = dot3((fh[...], fl[...]), split(x_ref[...]))

    @pl.when(g == 0)
    def _():
        out[...] = part

    @pl.when(g > 0)
    def _():
        out[...] += part


def drift(where, parent_state, mine, other, fh, fl, after):
    _, rows, samples = parent_state.shape
    count, blk, _ = mine.shape
    factor = pl.BlockSpec((rows, rows), lambda g, where: (where[OWN], where[OWN + g]))
    return call(
        drift_kernel,
        (4,),
        1,
        [pl.BlockSpec((1, rows, samples), lambda g, where: (where[PARENT], 0, 0))]
        + [whole(count, blk, blk)] * 2
        + [factor, factor],
        [pl.BlockSpec((rows, samples), lambda g, where: (where[OWN + g], 0)), whole(rows, samples)],
        [((4 * rows, samples), F32), ((rows, samples), F32)],
        "drift",
        after=[after],
        limit=12,
    )(where, outside(parent_state), mine, other, outside(fh), outside(fl))


def passed(arrays, *after, keep=False):
    return call(lambda *_: None, (1,), 0, [], [], [], "passed", after=after, through=arrays, keep=keep, limit=1)()


def begin_kernel(steps, where, weight, p_ref, u, fh, fl, bh, bl, n_out, s_out, g_out, h_out, token, mine, pair, ph, pl_):
    g = pl.program_id(0)
    token[...] = jnp.zeros_like(token)
    rows = ph.shape[0]
    orders = g_out.shape[0]
    tile = fh.shape[1]

    @pl.when(g < steps)
    def _():
        ph[...], pl_[...] = split(p_ref[...])

        @pl.when(g == 0)
        def _():
            mine[...] = jnp.zeros_like(mine)

        multiply(mine, column(u, g, rows), (ph, pl_), NT, mine)

        @pl.when(g != where[0])
        def _():
            multiply(column(n_out, g, rows), column(u, where[0], rows), (ph, pl_), NN)

    @pl.when(g == steps)
    def _():
        pair[0], pair[1] = split(mine[...] * weight[0])
        h_out[...] = dot3(pair[:, :orders], (bh[...], bl[...]))

    @pl.when(g >= steps)
    def _():
        multiply(column(g_out, g - steps, tile), pair.at[:, :orders], (fh, fl), NN)
        multiply(column(s_out, g - steps, tile), pair.at[:, orders:], (fh, fl), NN)


def begin(where, weight, cost_rows, u, fh, fl):
    rows, width = cost_rows.shape
    tall = u.shape[1]
    orders = tall - rows
    steps = width // rows
    tile = 512
    factor = pl.BlockSpec((rows, tile), lambda g, where, _: (where[0], jnp.maximum(g - steps, 0)))
    control = pl.BlockSpec((rows, orders), lambda g, where, _: (where[0], width // orders))
    return call(
        functools.partial(begin_kernel, steps),
        (steps + width // tile,),
        2,
        [
            pl.BlockSpec((rows, rows), lambda g, *_: (0, jnp.minimum(g, steps - 1))),
            STAYS,
            factor,
            factor,
            control,
            control,
        ],
        [STAYS] * 4 + [whole(8, 128)],
        [VMEM((tall, width), F32), VMEM((rows, width), F32), VMEM((orders, width), F32), VMEM((orders, orders), F32)]
        + [((8, 128), F32)],
        "begin",
        [VMEM((tall, rows), F32), VMEM((2, tall, rows), BF16)] + [VMEM((rows, rows), BF16)] * 2,
        limit=18,
    )(where, weight, outside(cost_rows), u, *[outside(f) for f in (fh, fl, fh, fl)])


def stage_kernel(options, size, focus, where, weight, *refs):
    arrived = refs[:options]
    u, n_in, fh, fl, bh, bl, s_in, g_in, h_in, *refs = refs[options:]
    if size > 1:
        s_out, g_out, h_out, n_out, token, done, pair, xh, xl = refs
    else:
        s_out, g_out, h_out, token, done, pair, xh, xl = refs
    g = pl.program_id(0)
    token[...] = jnp.zeros_like(token)
    rows = xh.shape[0]
    orders = g_out.shape[0]
    tile = fh.shape[1]
    f = where[focus]
    v = column(u, f, rows)
    for c in range(options):
        for t in range(size):

            @pl.when((g == t) & ((where[EDGE] == c) | (options == 1)))
            def _():
                unpack(arrived[c], t, rows // arrived[c].shape[1], xh, xl)

    @pl.when(g == 0)
    def _():
        multiply(done, v, (xh, xl), NN, column(n_in, f, rows))

    if size > 1:

        @pl.when((g > 0) & (g < size))
        def _():
            c = where[focus + g]
            multiply(done, column(u, c, rows), (xh, xl), NT, done)
            multiply(column(n_out, c, rows), v, (xh, xl), NN, column(n_in, c, rows))

    @pl.when(g == size)
    def _():
        pair[0], pair[1] = split(done[...] * weight[0])
        h_out[...] = h_in[...] + dot3(pair[:, :orders], (bh[...], bl[...]))

    @pl.when(g >= size)
    def _():
        at = g - size
        multiply(column(g_out, at, tile), pair.at[:, :orders], (fh, fl), NN, column(g_in, at, tile))
        multiply(column(s_out, at, tile), pair.at[:, orders:], (fh, fl), NN, column(s_in, at, tile))


def stage(where, weight, arrived, focus, size, u, n, fh, fl, sums, after=()):
    tall, width = n.shape
    rows, orders = sums[0].shape[0], sums[1].shape[0]
    tile = 512
    factor = pl.BlockSpec((rows, tile), lambda g, where, _: (where[focus], jnp.maximum(g - size, 0)))
    control = pl.BlockSpec((rows, orders), lambda g, where, _: (where[focus], width // orders))
    first = 2 + len(arrived)
    more = size > 1
    shapes = [VMEM((rows, width), F32), VMEM((orders, width), F32), VMEM((orders, orders), F32)]
    return call(
        functools.partial(stage_kernel, len(arrived), size, focus),
        (size + width // tile,),
        2,
        [whole(*x.shape) for x in arrived] + [STAYS, STAYS, factor, factor, control, control] + [STAYS] * 3,
        [STAYS] * (3 + more) + [whole(8, 128)],
        shapes + [VMEM((tall, width), F32)] * more + [((8, 128), F32)],
        "stage",
        [VMEM((tall, rows), F32), VMEM((2, tall, rows), BF16)] + [VMEM((rows, rows), BF16)] * 2,
        {first + 6: 0, first + 7: 1, first + 8: 2, **({first + 1: 3} if more else {})},
        after,
        limit=20,
    )(where, weight, *arrived, u, n, *[outside(f) for f in (fh, fl, fh, fl)], *sums)


def final_kernel(where, h_ref, s_own, g_own, g2, s2, q2, d_ref, x_ref, y_ref, bh, bl, gain, out, reached, pair, q):
    n = pl.program_id(0)
    rows = out.shape[0]

    @pl.when(n == 0)
    def _():
        value = -dot3(split(h_ref[...]), split(column(g_own, where[0], rows)[...] + g2[...]))
        gain[...] = value
        pair[0], pair[1] = split(value.T)
        q[...] = jnp.zeros_like(q)

    cross = split(column(g_own, n, rows)[...] + q2[...])
    part = column(s_own, n, rows)[...] + s2[...] + dot3(pair[...], cross)
    diag = lax.broadcasted_iota(jnp.int32, (rows, rows), 0) == lax.broadcasted_iota(jnp.int32, (rows, rows), 1)
    out[...] = part + jnp.where(diag & (n == where[0]), d_ref[...], 0.0)
    q[...] += dot3(cross, split(x_ref[...]))

    @pl.when(n == pl.num_programs(0) - 1)
    def _():
        u = -dot3(split(h_ref[...]), split(q[...]))
        reached[...] = y_ref[...] + dot3((bh[...], bl[...]), split(u))


def final(where, hinv, own, other, state_cost, x, y, fh, fl):
    rows, width = own[0].shape
    orders = own[1].shape[0]
    samples = x.shape[1]
    s_spec = pl.BlockSpec((rows, rows), lambda n, where: (0, n))
    g_spec = pl.BlockSpec((orders, rows), lambda n, where: (0, n))
    mine = pl.BlockSpec((orders, rows), lambda n, where: (0, where[0]))
    factor = pl.BlockSpec((rows, orders), lambda n, where: (where[0], width // orders))
    return call(
        final_kernel,
        (width // rows,),
        1,
        [whole(orders, orders), STAYS, STAYS, mine, s_spec, g_spec, whole(1, rows)]
        + [pl.BlockSpec((rows, samples), lambda n, where: (n, 0)), whole(rows, samples), factor, factor],
        [whole(orders, rows), s_spec, whole(rows, samples)],
        [((orders, rows), F32), ((rows, width), F32), ((rows, samples), F32)],
        "final",
        limit=16,
        scratch=[pltpu.VMEM((2, rows, orders), BF16), pltpu.VMEM((orders, samples), F32)],
    )(where, hinv, *own, other[1], *other, state_cost[None], x, y, outside(fh), outside(fl))


def image_kernel(where, weight, fh, fl, p_ref, out, acc):
    k = pl.program_id(0)
    part = dot3(split(p_ref[...]), (fh[...], fl[...]))

    @pl.when(k == 0)
    def _():
        acc[...] = part

    @pl.when(k > 0)
    def _():
        acc[...] += part

    @pl.when(k == pl.num_programs(0) - 1)
    def _():
        out[...] = acc[...].T * weight[0]


def image(where, weight, fh, fl, cost_rows):
    rows, width = cost_rows.shape
    chunk = 512
    factor = pl.BlockSpec((chunk, rows), lambda k, where, _: (k, where[0]))
    return call(
        image_kernel,
        (width // chunk,),
        2,
        [factor, factor, pl.BlockSpec((rows, chunk), lambda k, *_: (0, k))],
        [whole(rows, rows)],
        [((rows, rows), F32)],
        "image",
        [pltpu.VMEM((rows, rows), F32)],
    )(where, weight, fh, fl, cost_rows)[0]


def accumulate_kernel(first, where, y_ref, fh, fl, *refs):
    out = refs[-1]
    part = dot3(split(y_ref[...]), (fh[...], fl[...]))
    out[...] = part if first else refs[0][...] + part


def accumulate(where, y, fh, fl, acc):
    rows = y.shape[0]
    total = fh.shape[1]
    tile = 512
    first = acc is None
    spec = pl.BlockSpec((rows, tile), lambda n, where: (0, n))
    factor = pl.BlockSpec((rows, tile), lambda n, where: (where[0], n))
    return call(
        functools.partial(accumulate_kernel, first),
        (total // tile,),
        1,
        [whole(rows, rows), factor, factor] + [spec] * (not first),
        [spec],
        [((rows, total), F32)],
        "accumulate",
        aliases=None if first else {4: 0},
    )(where, y, fh, fl, *(() if first else (acc,)))[0]


def by_images(z, parts, weight, cost_rows, fh, fl):
    rows, width = cost_rows.shape
    acc = None
    for d in range(parts):
        block = image(((z + d) % parts)[None], weight, fh, fl, cost_rows)
        if d:
            block = lax.ppermute(block, "row", [(i, (i + d) % parts) for i in range(parts)])
        acc = accumulate(((z - d) % parts)[None], block, fh, fl, acc)
    cross = lax.all_gather(acc[:, width:], "row")
    return acc[:, :width], jnp.swapaxes(cross.reshape(width, -1), 0, 1)


def by_blocks(where, weight, cost_rows, parent_state, dense_parts, messages):
    fh, fl, u = dense_parts
    pair, mid = messages
    lead = 2 * mid.shape[0] - pair.shape[0]

    def moved(x, *pairs):
        return lax.ppermute(x, "row", pairs)

    def across(x):
        return moved(x, (1, 2), (2, 1))

    def to_end(x):
        return moved(x, (1, 0), (2, 3))

    pair = moved(pair, (0, 1), (1, 0), (2, 3), (3, 2))
    mid = across(mid)
    n, *sums, token = begin(where, weight, cost_rows, u, fh, fl)
    (mid,) = passed([mid], token)
    end = to_end(mid)
    mid_last = across(front(pair, lead))
    *sums, n, token = stage(where, weight, [pair], PARTNER, 3, u, n, fh, fl, sums)
    (mid_last,) = passed([mid_last], token)
    end_last = to_end(mid_last)
    *sums, n, token = stage(where, weight, [mid, end], SECOND, 2, u, n, fh, fl, sums)
    halves = collect(where, [pair, mid, end, mid_last, end_last], token)
    s, g, h, token = stage(where, weight, [mid_last, end_last], THIRD, 1, u, n, fh, fl, sums, [halves])
    x, y = drift(where, parent_state, halves, swapped(halves), fh, fl, token)
    other = swapped(h)
    return h, other, passed([s, g], other, y, keep=True), x, y


def swapped(x):
    n = lax.axis_size("leaf")
    return lax.ppermute(x, "leaf", [(i, i ^ 1) for i in range(n)])


def shards(
    leaf_cost,
    a_blocks,
    a_cols,
    b_blocks,
    b_cols,
    branch_prob,
    state_cost,
    control_cost,
    parent_state,
):
    cost_rows = leaf_cost[0]
    rows, width = cost_rows.shape
    blk = a_blocks.shape[3]
    orders = control_cost.shape[0]
    parts = lax.axis_size("row")
    z = lax.axis_index("row")
    leaf = lax.axis_index("leaf")
    line = parts == 4 and rows == orders

    left = z < 2
    near = jnp.where(left, 0, 3)
    edge = ((z == 0) | (z == 3)).astype(jnp.int32)
    where = jnp.stack([z, z ^ 1, jnp.where(left, 2, 1), 3 - near, leaf // 2, leaf % 2, near, edge])
    sent = []
    if line:
        sent.append(pack(where, [SECOND, THIRD], cost_rows, parent_state, blk, []))
        sent.append(pack(where, [NEAR], cost_rows, parent_state, blk, sent))
    fh, fl, u = parts_of = dense(where, rows, a_blocks[0], a_cols, b_blocks[0], b_cols, orders, sent)
    if line:
        h, other_h, own, x, y = by_blocks(where, branch_prob, cost_rows, parent_state, parts_of, sent)
    else:
        w = dot3(parted(cost_rows), (fh[:, width:], fl[:, width:]))
        b_rows = [lax.dynamic_slice(f, (0, z * rows), (orders, rows)) for f in u]
        h = lax.psum(dot3(b_rows, parted(w)) * branch_prob[0], "row")
        other_h = swapped(h)
        own = by_images(z, parts, branch_prob, cost_rows, fh, fl)
        own_state = lax.dynamic_index_in_dim(parent_state, leaf // 2, 0, keepdims=False)
        x = lax.all_gather(own_state, "row", tiled=True)
        y = dot3([lax.dynamic_slice(f, (z * rows, 0), (rows, width)) for f in (fh, fl)], parted(x))
    hinv = inverse(h, other_h, control_cost, blk)
    other = tuple(swapped(x) for x in own)
    gain, pcost, reached = final(where, hinv, own, other, state_cost, x, y, fh, fl)
    return pcost[None], gain[None], reached[None]


def solution(mesh):
    placed = (
        P("leaf", "row", None),
        P("leaf", None, None, None, None),
        P("leaf", None, None),
        P("leaf", None, None, None, None),
        P("leaf", None, None),
        P("leaf"),
        P("row"),
        P(),
        P(None, "row", None),
    )
    return jax.shard_map(
        shards,
        mesh=mesh,
        in_specs=placed,
        out_specs=(P("leaf", "row", None), P("leaf", None, "row"), P("leaf", "row", None)),
        check_vma=False,
    )
```

```python
import functools

import jax
import jax.numpy as jnp
from jax import lax
from jax.experimental import pallas as pl
from jax.experimental.pallas import tpu as pltpu
from jax.sharding import PartitionSpec as P

F32 = jnp.float32
BF16 = jnp.bfloat16
NN = (((1,), (0,)), ((), ()))
NT = (((1,), (1,)), ((), ()))


def split(x):
    hi = x.astype(BF16)
    return hi, (x - hi.astype(F32)).astype(BF16)


def parted(x):
    hi = lax.reduce_precision(x, 8, 7)
    return hi.astype(BF16), (x - hi).astype(BF16)


def dot3(a, b, dims=NN):
    one = functools.partial(lax.dot_general, dimension_numbers=dims, preferred_element_type=F32)
    rows = a[0].shape[0]
    both = jnp.concatenate(a, axis=0) if isinstance(a, (tuple, list)) else a.reshape(2 * rows, a.shape[2])
    part = one(both, b[0])
    return part[:rows] + (part[rows:] + one(a[0], b[1]))


TILE = (512, 512)
TALL = (1024, 512)
OWN, PARTNER, SECOND, THIRD, PARENT, CORE, NEAR, EDGE = range(8)
VMEM = pltpu.VMEM
STAYS = pl.BlockSpec(memory_space=VMEM)


def resident(x):
    return pltpu.with_memory_space_constraint(x, VMEM)


def outside(x):
    return pltpu.with_memory_space_constraint(x, pltpu.HBM)


def column(ref, i, size):
    return ref.at[..., pl.ds(pl.multiple_of(i * size, size), size)]


def multiply(out, a, b, dims, add=None, tile=TILE):
    right = dims[0][1][0]
    for m in range(0, out.shape[0], tile[0]):
        rows = slice(m, m + tile[0])
        for n in range(0, out.shape[1], tile[1]):
            cols = slice(n, n + tile[1])
            b_part = [x[:, cols] if right == 0 else x[cols] for x in b]
            value = dot3((a[0, rows], a[1, rows]), b_part, dims)
            out[rows, cols] = value if add is None else add[rows, cols] + value


def call(kernel, grid, prefetch, ins, outs, shapes, name, scratch=(), aliases=None, after=(), through=(), keep=False, limit=24):
    n_in, n_out = len(ins), len(outs)
    extra = len(after) + len(through)
    anywhere = pl.BlockSpec(memory_space=pl.ANY)

    def body(*refs):
        start = prefetch + n_in
        stop = start + extra + n_out
        kernel(*refs[:start], *refs[start + extra : stop], *refs[stop + len(through) :])

    aliases = dict(aliases or {})
    for t in range(len(through)):
        aliases[prefetch + n_in + len(after) + t] = n_out + t
    built = pl.pallas_call(
        body,
        grid_spec=pltpu.PrefetchScalarGridSpec(
            num_scalar_prefetch=prefetch,
            grid=grid,
            in_specs=list(ins) + [anywhere] * extra,
            out_specs=list(outs) + [anywhere] * len(through),
            scratch_shapes=scratch,
        ),
        out_shape=[x if isinstance(x, pl.MemoryRef) else jax.ShapeDtypeStruct(*x) for x in shapes]
        + [(VMEM if keep else jax.ShapeDtypeStruct)(x.shape, x.dtype) for x in through],
        input_output_aliases=aliases,
        compiler_params=pltpu.CompilerParams(vmem_limit_bytes=limit * 2**20),
        cost_estimate=pl.CostEstimate(flops=1, bytes_accessed=1, transcendentals=0),
        name=name,
    )

    def run(*args):
        placed = [resident(x) if spec is STAYS else x for spec, x in zip(ins, args[prefetch:])]
        return built(*args[:prefetch], *placed, *after, *[resident(x) if keep else x for x in through])

    return run


def whole(*shape):
    return pl.BlockSpec(shape, lambda *_: (0,) * len(shape))


def lower(n):
    return [(i, j) for i in range(n) for j in range(i + 1)]


def dense_kernel(blk, step, width, where, acol, bcol, a_ref, b_ref, fh, fl, u):
    i = pl.program_id(0)
    orders = fh.shape[1] - width
    rows = u.shape[1] - orders
    for ref in (fh, fl):
        ref[...] = jnp.zeros_like(ref)
    diag = lax.broadcasted_iota(jnp.int32, (blk, blk), 0) == lax.broadcasted_iota(jnp.int32, (blk, blk), 1)
    eye = jnp.where(diag, 0.75, 0.0).astype(F32)
    for t in range(step // blk):
        row = i * (step // blk) + t
        at = slice(t * blk, (t + 1) * blk)
        for s in range(a_ref.shape[1]):
            col = acol[0, row, s]
            block = a_ref[t, s] + eye if s == 0 else a_ref[t, s]
            to = pl.ds(pl.multiple_of(col * blk, blk), blk)
            fh[at, to], fl[at, to] = split(block)
        for s in range(b_ref.shape[1]):
            to = pl.ds(pl.multiple_of(width + bcol[0, row, s] * blk, blk), blk)
            fh[at, to], fl[at, to] = split(b_ref[t, s])

    own = pl.ds(pl.multiple_of(where[0] * rows, rows), rows)
    for p, f in enumerate((fh, fl)):
        for to, cols in ((slice(0, orders), slice(width, None)), (slice(orders, None), own)):
            part = f[:, cols]
            n = part.shape[1]
            diag = lax.broadcasted_iota(jnp.int32, (n, n), 0) == lax.broadcasted_iota(jnp.int32, (n, n), 1)
            one = jnp.where(diag, 1.0, 0.0).astype(BF16)
            u[p, to, pl.ds(pl.multiple_of(i * step, step), step)] = lax.dot_general(one, part, NT, preferred_element_type=F32).astype(BF16)


def dense(where, rows, a_blocks, a_cols, b_blocks, b_cols, orders, after):
    count, nnza, blk, _ = a_blocks.shape
    nnzb = b_blocks.shape[1]
    width = count * blk
    step = 2 * blk
    total = width + orders
    factor = pl.BlockSpec((step, total), lambda i, *_: (i, 0))
    return call(
        functools.partial(dense_kernel, blk, step, width),
        (width // step,),
        3,
        [
            pl.BlockSpec((2, nnza, blk, blk), lambda i, *_: (i, 0, 0, 0)),
            pl.BlockSpec((2, nnzb, blk, blk), lambda i, *_: (i, 0, 0, 0)),
        ],
        [factor, factor, STAYS],
        [pltpu.HBM((width, total), BF16)] * 2 + [VMEM((2, rows + orders, width), BF16)],
        "dense",
        after=after,
    )(where, a_cols, b_cols, outside(a_blocks), outside(b_blocks))


def inverse_block(m):
    n = m.shape[0]
    sub = lax.broadcasted_iota(jnp.int32, (8, n), 0)
    lane = lax.broadcasted_iota(jnp.int32, (8, n), 1)
    strips = [m[i : i + 8] for i in range(0, n, 8)]

    def along(v, j):
        return jnp.broadcast_to(v[:, j : j + 1], (8, n))

    def down(v, t):
        return jnp.broadcast_to(v[t : t + 1], (8, n))

    for q in range(n // 8):
        panel = strips[q]
        cols = [along(panel, 8 * q + b) for b in range(8)]
        for t in range(8):
            here = sub == t
            inv = 1.0 / down(cols[t], t)

            def reduced(v):
                r = down(v, t) * inv
                return jnp.where(here, r, v - cols[t] * r)

            panel = reduced(jnp.where(lane == 8 * q + t, jnp.where(here, 1.0, 0.0), panel))
            cols[t + 1 :] = [reduced(v) for v in cols[t + 1 :]]
        inside = (lane >= 8 * q) & (lane < 8 * q + 8)
        rows = [down(panel, b) for b in range(8)]
        for i in range(q + 1, q + n // 8):
            old = strips[i % (n // 8)]
            terms = [along(old, 8 * q + b) * rows[b] for b in range(8)]
            while len(terms) > 1:
                terms = [x + y for x, y in zip(terms[::2], terms[1::2])]
            strips[i % (n // 8)] = jnp.where(inside, 0.0, old) - terms[0]
        strips[q] = panel
    return jnp.concatenate(strips, axis=0)


def inverse_kernel(blk, mine, other, d_ref, out):
    n = out.shape[0]
    def dot(a, b):
        return dot3(split(a), split(b))

    diag = lax.broadcasted_iota(jnp.int32, (n, n), 0) == lax.broadcasted_iota(jnp.int32, (n, n), 1)
    out[...] = mine[...] + other[...] + jnp.where(diag, d_ref[...], 0.0)

    place = lax.broadcasted_iota(jnp.int32, (n, blk), 0) // blk

    for b in range(n // blk):
        here = slice(b * blk, (b + 1) * blk)
        inv = inverse_block(out[here, here])
        row = dot(inv, out[here, :])
        out[...] -= dot(out[:, here], row)
        col = row.T
        out[:, here] = jnp.where(place < b, col, -col)
        out[here, :] = row
        out[here, here] = inv


def inverse(mine, other, control_cost, blk):
    n = control_cost.shape[0]
    return call(
        functools.partial(inverse_kernel, blk),
        (1,),
        0,
        [whole(n, n)] * 2 + [whole(1, n)],
        [whole(n, n)],
        [((n, n), F32)],
        "inverse",
        limit=6,
    )(mine, other, control_cost[None])[0]


def folded(block, blk):
    n = block.shape[0] // blk
    half = blk // 2
    tiles = {(i, j): block[i * blk : (i + 1) * blk, j * blk : (j + 1) * blk] for i, j in lower(n)}
    last = tiles.pop((n - 1, n - 1))
    for d, (r, c) in enumerate(((0, 0), (half, 0), (half, half))):
        tile, part = tiles[d, d], last[r : r + half, c : c + half]
        top = jnp.concatenate((tile[:half, :half], part), axis=1)
        tiles[d, d] = jnp.concatenate((top, tile[half:]), axis=0)
    return list(tiles.values())


def unfolded(tiles, n):
    half = tiles.shape[1] // 2
    out = {place: tiles[t] for t, place in enumerate(lower(n)[:-1])}
    parts = [out[d, d][:half, half:] for d in range(3)]
    for d in range(3):
        tile = out[d, d]
        top = jnp.concatenate((tile[:half, :half], tile[half:, :half].T), axis=1)
        out[d, d] = jnp.concatenate((top, tile[half:]), axis=0)
    top = jnp.concatenate((parts[0], parts[1].T), axis=1)
    out[n - 1, n - 1] = jnp.concatenate((top, jnp.concatenate(parts[1:], axis=1)), axis=0)
    return [out[place] for place in lower(n)]


def tiled(block, blk):
    n = block.shape[0] // blk
    return [block[i * blk : (i + 1) * blk, j * blk : (j + 1) * blk] for i in range(n) for j in range(n)]


def pack_kernel(blk, where, own, x_ref, *refs):
    *blocks, out = refs
    diag = folded(own[...], blk)
    x = [x_ref[0, :blk], x_ref[0, blk:]]
    for t, tile in enumerate(diag + x + [tile for block in blocks for tile in tiled(block, blk)]):
        out[t] = tile


def pack(where, blocks, cost_rows, parent_state, blk, after):
    rows = cost_rows.shape[0]
    samples = parent_state.shape[2]
    picks = [OWN, *blocks]
    size = len(lower(rows // blk)) + 1 + (len(picks) - 1) * (rows // blk) ** 2
    specs = [pl.BlockSpec((rows, rows), functools.partial(lambda t, i, where: (0, where[t]), t)) for t in picks]
    specs.insert(1, pl.BlockSpec((1, rows // 2, samples), lambda i, where: (where[PARENT], where[CORE], 0)))
    args = [outside(cost_rows)] * len(picks)
    args.insert(1, outside(parent_state))
    return call(
        functools.partial(pack_kernel, blk),
        (1,),
        1,
        specs,
        [whole(size, blk, blk)],
        [((size, blk, blk), F32)],
        "pack",
        after=after,
        limit=16,
    )(where, *args)[0]


def front(message, size):
    shape = (size,) + message.shape[1:]

    def kernel(x, out):
        out[...] = x[...]

    return call(kernel, (1,), 0, [whole(*shape)], [whole(*shape)], [(shape, F32)], "front", limit=4)(message)[0]


def unpack(tiles, step, n, xh, xl):
    blk = tiles.shape[1]
    lead = len(lower(n)) - 1
    diag = unfolded(tiles, n) if step == 0 else None
    for t, (i, j) in enumerate(lower(n) if step == 0 else [(i, j) for i in range(n) for j in range(n)]):
        tile = diag[t] if step == 0 else tiles[lead + 2 + (step - 1) * n * n + t]
        places = [(i, j, tile)] + ([(j, i, tile.T)] if step == 0 and i != j else [])
        for r, c, value in places:
            at = slice(r * blk, (r + 1) * blk), slice(c * blk, (c + 1) * blk)
            xh[at], xl[at] = split(value)


def collect_kernel(where, pair, mid, end, mid_last, end_last, out):
    lead = mid_last.shape[0] - 2
    out[:2] = pair[lead : lead + 2]

    @pl.when(where[EDGE] == 1)
    def _():
        out[2:4] = end[lead : lead + 2]
        out[4:6] = end_last[lead : lead + 2]

    @pl.when(where[EDGE] == 0)
    def _():
        out[2:4] = mid[lead : lead + 2]
        out[4:6] = mid_last[lead : lead + 2]


def collect(where, messages, after):
    blk = messages[0].shape[1]
    lead = messages[3].shape[0] - 2
    return call(
        collect_kernel,
        (1,),
        1,
        [pl.BlockSpec((lead + 2, blk, blk), lambda i, where: (0, 0, 0))] * 5,
        [whole(6, blk, blk)],
        [((6, blk, blk), F32)],
        "collect",
        after=[after],
        limit=10,
    )(where, *messages)[0]


def drift_kernel(where, own, mine, other, fh, fl, x_ref, out):
    g = pl.program_id(0)
    core = where[CORE]
    blk = mine.shape[1]
    rows = own.shape[1]

    @pl.when(g == 0)
    def _():
        x_ref[...] = own[0]

    for d in range(3):

        @pl.when(g == d + 1)
        def _():
            for t in range(2):
                x_ref[pl.ds(pl.multiple_of(core * (rows // 2) + t * blk, blk), blk)] = mine[2 * d + t]
                x_ref[pl.ds(pl.multiple_of((1 - core) * (rows // 2) + t * blk, blk), blk)] = other[2 * d + t]

    part = dot3((fh[...], fl[...]), split(x_ref[...]))

    @pl.when(g == 0)
    def _():
        out[...] = part

    @pl.when(g > 0)
    def _():
        out[...] += part


def drift(where, parent_state, mine, other, fh, fl, after):
    _, rows, samples = parent_state.shape
    count, blk, _ = mine.shape
    factor = pl.BlockSpec((rows, rows), lambda g, where: (where[OWN], where[OWN + g]))
    return call(
        drift_kernel,
        (4,),
        1,
        [pl.BlockSpec((1, rows, samples), lambda g, where: (where[PARENT], 0, 0))]
        + [whole(count, blk, blk)] * 2
        + [factor, factor],
        [pl.BlockSpec((rows, samples), lambda g, where: (where[OWN + g], 0)), whole(rows, samples)],
        [((4 * rows, samples), F32), ((rows, samples), F32)],
        "drift",
        after=[after],
        limit=12,
    )(where, outside(parent_state), mine, other, outside(fh), outside(fl))


def passed(arrays, *after, keep=False):
    return call(lambda *_: None, (1,), 0, [], [], [], "passed", after=after, through=arrays, keep=keep, limit=1)()


def begin_kernel(steps, where, weight, p_ref, u, fh, fl, bh, bl, n_out, s_out, g_out, h_out, token, mine, pair, ph, pl_):
    g = pl.program_id(0)
    token[...] = jnp.zeros_like(token)
    rows = ph.shape[0]
    orders = g_out.shape[0]
    tile = fh.shape[1]

    @pl.when(g < steps)
    def _():
        ph[...], pl_[...] = split(p_ref[...])

        @pl.when(g == 0)
        def _():
            mine[...] = jnp.zeros_like(mine)

        multiply(mine, column(u, g, rows), (ph, pl_), NT, mine, TALL)

        @pl.when(g != where[0])
        def _():
            multiply(column(n_out, g, rows), column(u, where[0], rows), (ph, pl_), NN, None, TALL)

    @pl.when(g == steps)
    def _():
        pair[0], pair[1] = split(mine[...] * weight[0])
        h_out[...] = dot3(pair[:, :orders], (bh[...], bl[...]))

    @pl.when(g >= steps)
    def _():
        multiply(column(g_out, g - steps, tile), pair.at[:, :orders], (fh, fl), NN)
        multiply(column(s_out, g - steps, tile), pair.at[:, orders:], (fh, fl), NN)


def begin(where, weight, cost_rows, u, fh, fl):
    rows, width = cost_rows.shape
    tall = u.shape[1]
    orders = tall - rows
    steps = width // rows
    tile = 512
    factor = pl.BlockSpec((rows, tile), lambda g, where, _: (where[0], jnp.maximum(g - steps, 0)))
    control = pl.BlockSpec((rows, orders), lambda g, where, _: (where[0], width // orders))
    return call(
        functools.partial(begin_kernel, steps),
        (steps + width // tile,),
        2,
        [
            pl.BlockSpec((rows, rows), lambda g, *_: (0, jnp.minimum(g, steps - 1))),
            STAYS,
            factor,
            factor,
            control,
            control,
        ],
        [STAYS] * 4 + [whole(8, 128)],
        [VMEM((tall, width), F32), VMEM((rows, width), F32), VMEM((orders, width), F32), VMEM((orders, orders), F32)]
        + [((8, 128), F32)],
        "begin",
        [VMEM((tall, rows), F32), VMEM((2, tall, rows), BF16)] + [VMEM((rows, rows), BF16)] * 2,
        limit=18,
    )(where, weight, outside(cost_rows), u, *[outside(f) for f in (fh, fl, fh, fl)])


def stage_kernel(options, size, focus, where, weight, *refs):
    arrived = refs[:options]
    u, n_in, fh, fl, bh, bl, s_in, g_in, h_in, *refs = refs[options:]
    if size > 1:
        s_out, g_out, h_out, n_out, token, done, pair, xh, xl = refs
    else:
        s_out, g_out, h_out, token, done, pair, xh, xl = refs
    g = pl.program_id(0)
    token[...] = jnp.zeros_like(token)
    rows = xh.shape[0]
    orders = g_out.shape[0]
    tile = fh.shape[1]
    f = where[focus]
    v = column(u, f, rows)
    for c in range(options):
        for t in range(size):

            @pl.when((g == t) & ((where[EDGE] == c) | (options == 1)))
            def _():
                unpack(arrived[c], t, rows // arrived[c].shape[1], xh, xl)

    @pl.when(g == 0)
    def _():
        multiply(done, v, (xh, xl), NN, column(n_in, f, rows))

    if size > 1:

        @pl.when((g > 0) & (g < size))
        def _():
            c = where[focus + g]
            multiply(done, column(u, c, rows), (xh, xl), NT, done)
            multiply(column(n_out, c, rows), v, (xh, xl), NN, column(n_in, c, rows))

    @pl.when(g == size)
    def _():
        pair[0], pair[1] = split(done[...] * weight[0])
        h_out[...] = h_in[...] + dot3(pair[:, :orders], (bh[...], bl[...]))

    @pl.when(g >= size)
    def _():
        at = g - size
        multiply(column(g_out, at, tile), pair.at[:, :orders], (fh, fl), NN, column(g_in, at, tile))
        multiply(column(s_out, at, tile), pair.at[:, orders:], (fh, fl), NN, column(s_in, at, tile))


def stage(where, weight, arrived, focus, size, u, n, fh, fl, sums, after=()):
    tall, width = n.shape
    rows, orders = sums[0].shape[0], sums[1].shape[0]
    tile = 512
    factor = pl.BlockSpec((rows, tile), lambda g, where, _: (where[focus], jnp.maximum(g - size, 0)))
    control = pl.BlockSpec((rows, orders), lambda g, where, _: (where[focus], width // orders))
    first = 2 + len(arrived)
    more = size > 1
    shapes = [VMEM((rows, width), F32), VMEM((orders, width), F32), VMEM((orders, orders), F32)]
    return call(
        functools.partial(stage_kernel, len(arrived), size, focus),
        (size + width // tile,),
        2,
        [whole(*x.shape) for x in arrived] + [STAYS, STAYS, factor, factor, control, control] + [STAYS] * 3,
        [STAYS] * (3 + more) + [whole(8, 128)],
        shapes + [VMEM((tall, width), F32)] * more + [((8, 128), F32)],
        "stage",
        [VMEM((tall, rows), F32), VMEM((2, tall, rows), BF16)] + [VMEM((rows, rows), BF16)] * 2,
        {first + 6: 0, first + 7: 1, first + 8: 2, **({first + 1: 3} if more else {})},
        after,
        limit=20,
    )(where, weight, *arrived, u, n, *[outside(f) for f in (fh, fl, fh, fl)], *sums)


def final_kernel(where, h_ref, s_own, g_own, g2, s2, q2, d_ref, x_ref, y_ref, bh, bl, gain, out, reached, pair, q):
    n = pl.program_id(0)
    rows = out.shape[0]

    @pl.when(n == 0)
    def _():
        value = -dot3(split(h_ref[...]), split(column(g_own, where[0], rows)[...] + g2[...]))
        gain[...] = value
        pair[0], pair[1] = split(value.T)
        q[...] = jnp.zeros_like(q)

    cross = split(column(g_own, n, rows)[...] + q2[...])
    part = column(s_own, n, rows)[...] + s2[...] + dot3(pair[...], cross)
    diag = lax.broadcasted_iota(jnp.int32, (rows, rows), 0) == lax.broadcasted_iota(jnp.int32, (rows, rows), 1)
    out[...] = part + jnp.where(diag & (n == where[0]), d_ref[...], 0.0)
    q[...] += dot3(cross, split(x_ref[...]))

    @pl.when(n == pl.num_programs(0) - 1)
    def _():
        u = -dot3(split(h_ref[...]), split(q[...]))
        reached[...] = y_ref[...] + dot3((bh[...], bl[...]), split(u))


def final(where, hinv, own, other, state_cost, x, y, fh, fl):
    rows, width = own[0].shape
    orders = own[1].shape[0]
    samples = x.shape[1]
    s_spec = pl.BlockSpec((rows, rows), lambda n, where: (0, n))
    g_spec = pl.BlockSpec((orders, rows), lambda n, where: (0, n))
    mine = pl.BlockSpec((orders, rows), lambda n, where: (0, where[0]))
    factor = pl.BlockSpec((rows, orders), lambda n, where: (where[0], width // orders))
    return call(
        final_kernel,
        (width // rows,),
        1,
        [whole(orders, orders), STAYS, STAYS, mine, s_spec, g_spec, whole(1, rows)]
        + [pl.BlockSpec((rows, samples), lambda n, where: (n, 0)), whole(rows, samples), factor, factor],
        [whole(orders, rows), s_spec, whole(rows, samples)],
        [((orders, rows), F32), ((rows, width), F32), ((rows, samples), F32)],
        "final",
        limit=16,
        scratch=[pltpu.VMEM((2, rows, orders), BF16), pltpu.VMEM((orders, samples), F32)],
    )(where, hinv, *own, other[1], *other, state_cost[None], x, y, outside(fh), outside(fl))


def image_kernel(where, weight, fh, fl, p_ref, out, acc):
    k = pl.program_id(0)
    part = dot3(split(p_ref[...]), (fh[...], fl[...]))

    @pl.when(k == 0)
    def _():
        acc[...] = part

    @pl.when(k > 0)
    def _():
        acc[...] += part

    @pl.when(k == pl.num_programs(0) - 1)
    def _():
        out[...] = acc[...].T * weight[0]


def image(where, weight, fh, fl, cost_rows):
    rows, width = cost_rows.shape
    chunk = 512
    factor = pl.BlockSpec((chunk, rows), lambda k, where, _: (k, where[0]))
    return call(
        image_kernel,
        (width // chunk,),
        2,
        [factor, factor, pl.BlockSpec((rows, chunk), lambda k, *_: (0, k))],
        [whole(rows, rows)],
        [((rows, rows), F32)],
        "image",
        [pltpu.VMEM((rows, rows), F32)],
    )(where, weight, fh, fl, cost_rows)[0]


def accumulate_kernel(first, where, y_ref, fh, fl, *refs):
    out = refs[-1]
    part = dot3(split(y_ref[...]), (fh[...], fl[...]))
    out[...] = part if first else refs[0][...] + part


def accumulate(where, y, fh, fl, acc):
    rows = y.shape[0]
    total = fh.shape[1]
    tile = 512
    first = acc is None
    spec = pl.BlockSpec((rows, tile), lambda n, where: (0, n))
    factor = pl.BlockSpec((rows, tile), lambda n, where: (where[0], n))
    return call(
        functools.partial(accumulate_kernel, first),
        (total // tile,),
        1,
        [whole(rows, rows), factor, factor] + [spec] * (not first),
        [spec],
        [((rows, total), F32)],
        "accumulate",
        aliases=None if first else {4: 0},
    )(where, y, fh, fl, *(() if first else (acc,)))[0]


def by_images(z, parts, weight, cost_rows, fh, fl):
    rows, width = cost_rows.shape
    acc = None
    for d in range(parts):
        block = image(((z + d) % parts)[None], weight, fh, fl, cost_rows)
        if d:
            block = lax.ppermute(block, "row", [(i, (i + d) % parts) for i in range(parts)])
        acc = accumulate(((z - d) % parts)[None], block, fh, fl, acc)
    cross = lax.all_gather(acc[:, width:], "row")
    return acc[:, :width], jnp.swapaxes(cross.reshape(width, -1), 0, 1)


def by_blocks(where, weight, cost_rows, parent_state, dense_parts, messages):
    fh, fl, u = dense_parts
    pair, mid = messages
    lead = 2 * mid.shape[0] - pair.shape[0]

    def moved(x, *pairs):
        return lax.ppermute(x, "row", pairs)

    def across(x):
        return moved(x, (1, 2), (2, 1))

    def to_end(x):
        return moved(x, (1, 0), (2, 3))

    pair = moved(pair, (0, 1), (1, 0), (2, 3), (3, 2))
    mid = across(mid)
    n, *sums, token = begin(where, weight, cost_rows, u, fh, fl)
    (mid,) = passed([mid], token)
    end = to_end(mid)
    mid_last = across(front(pair, lead))
    *sums, n, token = stage(where, weight, [pair], PARTNER, 3, u, n, fh, fl, sums)
    (mid_last,) = passed([mid_last], token)
    end_last = to_end(mid_last)
    *sums, n, token = stage(where, weight, [mid, end], SECOND, 2, u, n, fh, fl, sums)
    halves = collect(where, [pair, mid, end, mid_last, end_last], token)
    s, g, h, token = stage(where, weight, [mid_last, end_last], THIRD, 1, u, n, fh, fl, sums, [halves])
    x, y = drift(where, parent_state, halves, swapped(halves), fh, fl, token)
    other = swapped(h)
    return h, other, passed([s, g], other, y, keep=True), x, y


def swapped(x):
    n = lax.axis_size("leaf")
    return lax.ppermute(x, "leaf", [(i, i ^ 1) for i in range(n)])


def shards(
    leaf_cost,
    a_blocks,
    a_cols,
    b_blocks,
    b_cols,
    branch_prob,
    state_cost,
    control_cost,
    parent_state,
):
    cost_rows = leaf_cost[0]
    rows, width = cost_rows.shape
    blk = a_blocks.shape[3]
    orders = control_cost.shape[0]
    parts = lax.axis_size("row")
    z = lax.axis_index("row")
    leaf = lax.axis_index("leaf")
    line = parts == 4 and rows == orders

    left = z < 2
    near = jnp.where(left, 0, 3)
    edge = ((z == 0) | (z == 3)).astype(jnp.int32)
    where = jnp.stack([z, z ^ 1, jnp.where(left, 2, 1), 3 - near, leaf // 2, leaf % 2, near, edge])
    sent = []
    if line:
        sent.append(pack(where, [SECOND, THIRD], cost_rows, parent_state, blk, []))
        sent.append(pack(where, [NEAR], cost_rows, parent_state, blk, sent))
    fh, fl, u = parts_of = dense(where, rows, a_blocks[0], a_cols, b_blocks[0], b_cols, orders, sent)
    if line:
        h, other_h, own, x, y = by_blocks(where, branch_prob, cost_rows, parent_state, parts_of, sent)
    else:
        w = dot3(parted(cost_rows), (fh[:, width:], fl[:, width:]))
        b_rows = [lax.dynamic_slice(f, (0, z * rows), (orders, rows)) for f in u]
        h = lax.psum(dot3(b_rows, parted(w)) * branch_prob[0], "row")
        other_h = swapped(h)
        own = by_images(z, parts, branch_prob, cost_rows, fh, fl)
        own_state = lax.dynamic_index_in_dim(parent_state, leaf // 2, 0, keepdims=False)
        x = lax.all_gather(own_state, "row", tiled=True)
        y = dot3([lax.dynamic_slice(f, (z * rows, 0), (rows, width)) for f in (fh, fl)], parted(x))
    hinv = inverse(h, other_h, control_cost, blk)
    other = tuple(swapped(x) for x in own)
    gain, pcost, reached = final(where, hinv, own, other, state_cost, x, y, fh, fl)
    return pcost[None], gain[None], reached[None]


def solution(mesh):
    placed = (
        P("leaf", "row", None),
        P("leaf", None, None, None, None),
        P("leaf", None, None),
        P("leaf", None, None, None, None),
        P("leaf", None, None),
        P("leaf"),
        P("row"),
        P(),
        P(None, "row", None),
    )
    return jax.shard_map(
        shards,
        mesh=mesh,
        in_specs=placed,
        out_specs=(P("leaf", "row", None), P("leaf", None, "row"), P("leaf", "row", None)),
        check_vma=False,
    )
```
